32 devices in a mesh: dp: 8 (over z, y), fsdp: 4 (over x, core).
Axes of the slice: x: 2, y: 2, z: 4, core: 2. Of those that a mesh axis runs over, the one named last changes fastest.
Arguments:
- tokens: bfloat16 [32768, 768], P(('dp', 'fsdp')), may hold values from -6 to 6
- lengths: int32 [32, 8], P(('dp', 'fsdp')), may hold values from 1 to 768, 1024 in all within a row
- w_qkv: bfloat16 [768, 2304], P('fsdp'), may hold values from -0.21875 to 0.21875
- w_out: bfloat16 [768, 768], P('fsdp'), may hold values from -0.625 to 0.625
- w_gate: bfloat16 [768, 3072], P('fsdp'), may hold values from -0.21875 to 0.21875
- w_up: bfloat16 [768, 3072], P('fsdp'), may hold values from -0.21875 to 0.21875
- w_down: bfloat16 [3072, 768], P('fsdp'), may hold values from -0.15625 to 0.15625
- gain_one: bfloat16 [768], P('fsdp'), may hold values from 0.5 to 1.5
- shift_one: bfloat16 [768], P('fsdp'), may hold values from -3 to 3
- gain_two: bfloat16 [768], P('fsdp'), may hold values from 0.5 to 1.5
- shift_two: bfloat16 [768], P('fsdp'), may hold values from -3 to 3
Outputs:
- info_loss: float32 [], replicated
- output: bfloat16 [32768, 768], P(('dp', 'fsdp'))
- grad_tokens: float32 [32768, 768], P(('dp', 'fsdp'))
- grad_qkv: float32 [768, 2304], P('fsdp')
- grad_out: float32 [768, 768], P('fsdp')
- grad_gate: float32 [768, 3072], P('fsdp')
- grad_up: float32 [768, 3072], P('fsdp')
- grad_down: float32 [3072, 768], P('fsdp')
- grad_gain_one: float32 [768], P('fsdp')
- grad_shift_one: float32 [768], P('fsdp')
- grad_gain_two: float32 [768], P('fsdp')
- grad_shift_two: float32 [768], P('fsdp')
The draws below stay inside these ranges and needn't reach their ends.
Inputs may be any that keep to these rules, and one draw needn't show every extreme that they name: Each row holds the lengths of one pack's 8 sequences, summing to 1024; the largest in every row is 768.
All inputs are finite; a program needn't handle non-finite values.
Results may differ from the reference program's by a relative error of at most 0.015.
Values may be sent and summed in bfloat16 or wider, within the bound.
No kernel may reach another device: no remote copies, remote signals or barrier semaphores. Data moves between devices by JAX's collectives and lax.ppermute only.
A program may use at most 192 MiB of HBM per device.

```python
import math
import jax
import jax.numpy as jnp
import numpy as np
from jax import lax

D = 768
HD = 64
FF = 3072
TOK_DEV = 1024
PAIRS = 4
SEQS = 8
MAXLEN = 768
TOKENS = 32768
DEVICES = 32


def levels(rng, shape, cuts, smallest, top_value):
    level = 1.0
    for dim, blocks in cuts:
        draws = jax.random.uniform(jax.random.fold_in(jax.random.fold_in(rng, 6), dim), (blocks,), jnp.float32, smallest / len(cuts), top_value / len(cuts))
        level = level * jnp.repeat(jnp.exp(draws), shape[dim] // blocks).reshape((-1,) + (1,) * (len(shape) - 1 - dim))
    return level


def profile(number_of, total, limit, lean):
    portions = [(1 << 20) // math.isqrt(rank ** lean) + 1 for rank in range(2, number_of + 1)]
    spare, holding = total - limit - (number_of - 1), [1] * (number_of - 1)
    while spare > 0:
        candidates = [i for i in range(number_of - 1) if holding[i] < limit]
        pool, budget = sum([portions[i] for i in candidates]), spare
        for i in candidates:
            addition = min(limit - holding[i], max(1, budget * portions[i] // pool), spare)
            holding[i] = holding[i] + addition
            spare = spare - addition
    return np.array([limit] + holding)


def ragged_sizes(stream_key, amount, total, bound, slope):
    if amount == 2:
        one = jax.random.randint(stream_key, (), max(1, total - bound), min(bound, total - 1) + 1)
        return jnp.stack([one, total - one])
    tallies = jnp.asarray(profile(amount, total, bound, slope), jnp.int32)
    pairs = (amount - 1) // 2
    giver, taker = tallies[1:1 + 2 * pairs:2], tallies[2:2 + 2 * pairs:2]
    margin = jnp.minimum(giver - 1, bound - taker)
    shifted = jax.random.randint(jax.random.fold_in(stream_key, 1), (pairs,), 0, 1 << 20) % (margin + 1)
    tallies = tallies.at[1:1 + 2 * pairs:2].set(giver - shifted).at[2:2 + 2 * pairs:2].set(taker + shifted)
    return tallies[jax.random.permutation(jax.random.fold_in(stream_key, 2), amount)]


def centred(key, shape, width, limit, cuts=(), kind=jnp.bfloat16):
    drawn = width * jax.random.normal(key, shape, jnp.float32)
    if cuts:
        drawn = drawn * levels(key, shape, cuts, -0.22, 0.18)
    return jnp.clip(drawn, -limit, limit).astype(kind)


def setup_inputs(seed: int = 0) -> dict:
    keys = jax.random.split(jax.random.key(seed), 12)
    return {
        "tokens": centred(keys[0], (TOKENS, D), 1.0, 6.0, ((0, 32),)),
        "lengths": jax.vmap(lambda own: ragged_sizes(own, SEQS, TOK_DEV, MAXLEN, 2))(jax.random.split(keys[1], DEVICES)).reshape((DEVICES, SEQS)).astype(jnp.int32),
        "w_qkv": centred(keys[2], (D, 3 * D), D ** -0.5, 0.21875, ((0, 4),)),
        "w_out": centred(keys[3], (D, D), (D // 8) ** -0.5, 0.625, ((0, 4),)),
        "w_gate": centred(keys[4], (D, FF), D ** -0.5, 0.21875, ((0, 4),)),
        "w_up": centred(keys[5], (D, FF), D ** -0.5, 0.21875, ((0, 4),)),
        "w_down": centred(keys[6], (FF, D), (FF // 2) ** -0.5, 0.15625, ((0, 4),)),
        "gain_one": jnp.clip(1.0 + 0.1 * jax.random.normal(keys[7], (D,), jnp.float32), 0.5, 1.5).astype(jnp.bfloat16),
        "shift_one": centred(keys[8], (D,), 0.3, 3.0, ((0, 4),)),
        "gain_two": jnp.clip(1.0 + 0.1 * jax.random.normal(keys[9], (D,), jnp.float32), 0.5, 1.5).astype(jnp.bfloat16),
        "shift_two": centred(keys[10], (D,), 0.3, 3.0, ((0, 4),)),
    }


@jax.custom_vjp
def low(v):
    return lax.optimization_barrier(v.astype(jnp.bfloat16)).astype(jnp.float32)

@jax.custom_vjp
def low_back(v):
    return v

def low_keep(v):
    return (low(v), None)

def low_pass(kept, grad):
    return (grad,)

def back_keep(v):
    return (v, None)

def back_low(kept, grad):
    return (low(grad),)
low.defvjp(low_keep, low_pass)
low_back.defvjp(back_keep, back_low)
exact_arithmetic = lax.Precision.HIGHEST
eps_norm = 1e-05
eps_embed = 1e-06
logit_divisor = 0.05
rope_base = 1000.0

def pack_layout(lengths_row, tok_count):
    seq_ends = jnp.cumsum(lengths_row).astype(jnp.int32)
    starts = (seq_ends - lengths_row).astype(jnp.int32)
    places = lax.iota(jnp.int32, tok_count)
    segment = lax.optimization_barrier(jnp.sum((places[:, None] >= seq_ends[None, :]).astype(jnp.int32), axis=1))
    member = segment[:, None] == lax.iota(jnp.int32, lengths_row.shape[0])[None, :]
    offset = lax.optimization_barrier(jnp.sum(jnp.where(member, starts[None, :], 0), axis=1)).astype(jnp.int32)
    return (segment, places - offset, member)

def rotary_tables(position, half_dim):
    frequency = rope_base ** (-2.0 * lax.iota(jnp.float32, half_dim) / (2 * half_dim))
    angles = position.astype(jnp.float32)[:, None] * frequency[None, :]
    return (jnp.cos(angles), jnp.sin(angles))

def rotate(heads_in, cosine, sine_table):
    half_dim = heads_in.shape[-1] // 2
    first_half = heads_in[..., :half_dim]
    second_half = heads_in[..., half_dim:]
    return jnp.concatenate([first_half * cosine - second_half * sine_table, second_half * cosine + first_half * sine_table], axis=-1)

def norm_parts(vector_in):
    centered = vector_in - lax.optimization_barrier(jnp.mean(vector_in, axis=1, keepdims=True))
    inv_root = lax.rsqrt(lax.optimization_barrier(jnp.mean(centered * centered, axis=1, keepdims=True)) + eps_norm)
    return centered * inv_root

def pack_forward(params, tokens_in, lengths_row):
    w_qkv, w_out, w_gate, w_up, w_down, gain_one, shift_one, gain_two, shift_two = params
    tok_count, model_width = tokens_in.shape
    head_count = model_width // HD
    segment, position, member = pack_layout(lengths_row, tok_count)
    cosine, sine_table = rotary_tables(position, HD // 2)
    joined_qkv = low_back(jnp.dot(tokens_in, w_qkv, precision=exact_arithmetic))
    head_parts = joined_qkv.reshape(tok_count, 3, head_count, HD).transpose(1, 2, 0, 3)
    request_vectors = low(low_back(rotate(head_parts[0], cosine, sine_table)))
    key_heads = low(low_back(rotate(head_parts[1], cosine, sine_table)))
    value_heads = low(low_back(head_parts[2]))
    same_segment = segment[:, None] == segment[None, :]
    scores = low_back(jnp.einsum('hqd,hkd->hqk', request_vectors, key_heads, precision=exact_arithmetic) * 0.125)
    scores = jnp.where(same_segment[None], scores, -1e+30)
    soft_probs = jax.nn.softmax(scores, axis=-1)
    attended = jnp.einsum('hqk,hkd->hqd', low(soft_probs), value_heads, precision=exact_arithmetic)
    attended = low(low_back(attended.transpose(1, 0, 2).reshape(tok_count, model_width)))
    branch = low_back(jnp.dot(attended, w_out, precision=exact_arithmetic))
    hidden = norm_parts(tokens_in + branch) * gain_one + shift_one
    hidden_low = low(hidden)
    gate_proj = low_back(jnp.dot(hidden_low, w_gate, precision=exact_arithmetic))
    up_proj = low_back(jnp.dot(hidden_low, w_up, precision=exact_arithmetic))
    inner = low(jax.nn.silu(gate_proj) * up_proj)
    feed_out = low_back(jnp.dot(inner, w_down, precision=exact_arithmetic))
    output = norm_parts(hidden + feed_out) * gain_two + shift_two
    sizes_float = lengths_row.astype(jnp.float32)[:, None]
    pooled = jnp.dot(member.astype(jnp.float32).T, output, precision=exact_arithmetic) / sizes_float
    embedding = pooled * lax.rsqrt(lax.optimization_barrier(jnp.sum(pooled * pooled, axis=1, keepdims=True)) + eps_embed)
    return (output, embedding)

def whole_layer(params, tokens_all, lengths):
    packs = tokens_all.reshape(lengths.shape[0], -1, tokens_all.shape[1])

    def pack_step(running, pack_item):
        result = jax.checkpoint(pack_forward)(params, pack_item[0], pack_item[1])
        return (running, result)
    unused, (outputs, embedding) = lax.scan(pack_step, jnp.zeros((), jnp.float32), (packs, lengths))
    request_vectors = embedding[:, :PAIRS].reshape(-1, embedding.shape[2])
    passage_vectors = embedding[:, PAIRS:].reshape(-1, embedding.shape[2])
    affinity_table = jnp.dot(request_vectors, passage_vectors.T, precision=exact_arithmetic) / logit_divisor
    info_loss = jnp.mean(jax.nn.logsumexp(affinity_table, axis=1) - jnp.diagonal(affinity_table))
    return (info_loss, outputs.reshape(-1, outputs.shape[2]))

def reference(tokens, lengths, w_qkv, w_out, w_gate, w_up, w_down, gain_one, shift_one, gain_two, shift_two):
    params = (w_qkv.astype(jnp.float32), w_out.astype(jnp.float32), w_gate.astype(jnp.float32), w_up.astype(jnp.float32), w_down.astype(jnp.float32), gain_one.astype(jnp.float32), shift_one.astype(jnp.float32), gain_two.astype(jnp.float32), shift_two.astype(jnp.float32))

    def objective(weights_in, tokens_in):
        return whole_layer(weights_in, tokens_in, lengths)
    info_loss, pullback, outputs = jax.vjp(objective, params, tokens.astype(jnp.float32), has_aux=True)
    grad_params, grad_tokens = pullback(jnp.ones_like(info_loss))
    return (info_loss, outputs.astype(jnp.bfloat16), grad_tokens, grad_params[0], grad_params[1], grad_params[2], grad_params[3], grad_params[4], grad_params[5], grad_params[6], grad_params[7], grad_params[8])
```

```python
import jax
import jax.numpy as jnp
from jax import lax
from jax.sharding import PartitionSpec as P

HD = 64
PAIRS = 4


exact_arithmetic = lax.Precision.HIGHEST
eps_norm = 1e-05
eps_embed = 1e-06
logit_divisor = 0.05
rope_base = 1000.0


def pack_layout(lengths_row, tok_count):
    seq_ends = jnp.cumsum(lengths_row)
    starts = seq_ends - lengths_row
    places = lax.iota(jnp.int32, tok_count)
    segment = jnp.sum((places[:, None] >= seq_ends[None, :]).astype(jnp.int32), axis=1)
    member = segment[:, None] == lax.iota(jnp.int32, lengths_row.shape[0])[None, :]
    offset = jnp.sum(jnp.where(member, starts[None, :], 0), axis=1)
    return (segment, places - offset, member)


def rotary_tables(position, half_dim):
    frequency = rope_base ** (-2.0 * lax.iota(jnp.float32, half_dim) / (2 * half_dim))
    angles = position.astype(jnp.float32)[:, None] * frequency[None, :]
    return (jnp.cos(angles), jnp.sin(angles))


def rotate(heads_in, cosine, sine_table):
    half_dim = heads_in.shape[-1] // 2
    first_half = heads_in[..., :half_dim]
    second_half = heads_in[..., half_dim:]
    return jnp.concatenate(
        [
            first_half * cosine - second_half * sine_table,
            second_half * cosine + first_half * sine_table,
        ],
        axis=-1,
    )


def unrotate(heads_in, cosine, sine_table):
    half_dim = heads_in.shape[-1] // 2
    first_half = heads_in[..., :half_dim]
    second_half = heads_in[..., half_dim:]
    return jnp.concatenate(
        [
            first_half * cosine + second_half * sine_table,
            second_half * cosine - first_half * sine_table,
        ],
        axis=-1,
    )


def norm_parts(vector_in):
    centered = vector_in - jnp.mean(vector_in, axis=1, keepdims=True)
    inv_root = lax.rsqrt(jnp.mean(centered * centered, axis=1, keepdims=True) + eps_norm)
    return (centered * inv_root, inv_root)


def norm_back(upstream, normed, inv_root, gain_vec):
    grad_normed = upstream * gain_vec
    return inv_root * (
        grad_normed
        - jnp.mean(grad_normed, axis=1, keepdims=True)
        - normed * jnp.mean(grad_normed * normed, axis=1, keepdims=True)
    )


def inner_pairing(left, right, left_dim, right_dim, matmul_precision=None):
    return lax.dot_general(
        left,
        right,
        (((left_dim,), (right_dim,)), ((), ())),
        precision=matmul_precision,
        preferred_element_type=jnp.float32,
    )


def swap(value, axis, bit):
    size = lax.axis_size(axis)
    return lax.ppermute(value, axis, [(i, i ^ bit) for i in range(size)])


def choose(value, index):
    return lax.dynamic_index_in_dim(value, index, 0, keepdims=False)


def gather_small(block):
    dp_size, fsdp_size = lax.axis_size("dp"), lax.axis_size("fsdp")
    held = block[None]
    bit = dp_size // 2
    while bit:
        other = swap(held, "dp", bit)
        low = (lax.axis_index("dp") & bit) == 0
        held = jnp.where(low, jnp.stack([held, other]), jnp.stack([other, held]))
        held = held.reshape((-1,) + block.shape)
        bit //= 2
    bits = dp_size.bit_length() - 1
    held = held.reshape((2,) * bits + block.shape)
    held = held.transpose(tuple(range(bits))[::-1] + tuple(range(bits, bits + block.ndim)))
    held = held.reshape((dp_size,) + block.shape)
    held = lax.all_gather(held, "fsdp", axis=1)
    return held.reshape((dp_size * fsdp_size,) + block.shape)


def low_add(*terms):
    total = terms[0].astype(jnp.float32)
    for term in terms[1:]:
        total = total + term.astype(jnp.float32)
    return total.astype(jnp.bfloat16)


def reduce_steps(grad):
    fsdp = lax.axis_index("fsdp")
    dp = lax.axis_index("dp")
    dp_size = lax.axis_size("dp")
    rows, columns = grad.shape
    quarter = rows // lax.axis_size("fsdp")
    parts = grad.astype(jnp.bfloat16).reshape(4, quarter, columns)
    theirs = jnp.stack([choose(parts, fsdp ^ 3), choose(parts, fsdp ^ 1)])
    from_core = swap(theirs, "fsdp", 1)
    yield None
    from_far = swap(low_add(choose(parts, fsdp ^ 2), from_core[0]), "fsdp", 2)
    yield None
    held = low_add(choose(parts, fsdp), from_core[1], from_far)
    bits = min(3, dp_size.bit_length() - 1)
    for step in range(bits):
        halves = held.reshape(2, held.shape[0] // 2, columns)
        side = (dp >> step) & 1
        other = swap(choose(halves, 1 - side), "dp", 1 << step)
        yield None
        held = low_add(choose(halves, side), other)
    step = bits
    while (1 << step) < dp_size:
        other = swap(held, "dp", 1 << step)
        yield None
        held = low_add(held, other)
        step += 1
    for step in reversed(range(bits)):
        other = swap(held, "dp", 1 << step)
        yield None
        side = (dp >> step) & 1
        held = jnp.where(side == 0, jnp.concatenate([held, other]), jnp.concatenate([other, held]))
    yield held.astype(jnp.float32)


def reduce_weights(grads):
    steps = [reduce_steps(grad) for grad in grads]
    done = [None] * len(steps)
    while any(item is None for item in done):
        for index, step in enumerate(steps):
            if done[index] is None:
                done[index] = next(step)
    return done


def gather_weights(w_qkv, w_out, w_gate, w_up, w_down, gain_one, shift_one, gain_two, shift_two):
    return (
        lax.all_gather(w_qkv, "fsdp", axis=0, tiled=True),
        lax.all_gather(w_out, "fsdp", axis=0, tiled=True),
        lax.all_gather(w_gate, "fsdp", axis=0, tiled=True),
        lax.all_gather(w_up, "fsdp", axis=0, tiled=True),
        lax.all_gather(w_down, "fsdp", axis=0, tiled=True),
        lax.all_gather(gain_one, "fsdp", axis=0, tiled=True),
        lax.all_gather(shift_one, "fsdp", axis=0, tiled=True),
        lax.all_gather(gain_two, "fsdp", axis=0, tiled=True),
        lax.all_gather(shift_two, "fsdp", axis=0, tiled=True),
    )


def per_device(
    tokens, lengths, w_qkv, w_out, w_gate, w_up, w_down, gain_one, shift_one, gain_two, shift_two
):
    tok_count, model_width = tokens.shape
    head_count = model_width // HD
    lengths_row = lengths[0]
    segment, position, member = pack_layout(lengths_row, tok_count)
    member_float = member.astype(jnp.float32)
    sizes_float = lengths_row.astype(jnp.float32)[:, None]
    cosine, sine_table = rotary_tables(position, HD // 2)
    same_segment = segment[:, None] == segment[None, :]

    def attend(head_item):
        query_head, key_head, value_head = head_item
        raw_scores = inner_pairing(query_head, key_head, 1, 1) * 0.125
        masked = jnp.where(same_segment, raw_scores, -1e30)
        row_top = jnp.max(masked, axis=1, keepdims=True)
        exp_terms = jnp.exp(masked - row_top)
        row_loss_sum = jnp.sum(exp_terms, axis=1, keepdims=True)
        soft_probs = (exp_terms / row_loss_sum).astype(jnp.bfloat16)
        return (
            jnp.dot(soft_probs, value_head, preferred_element_type=jnp.float32),
            (row_top + jnp.log(row_loss_sum))[:, 0],
        )

    def attend_back(head_item):
        query_head, key_head, value_head, grad_head, log_total = head_item
        raw_scores = inner_pairing(query_head, key_head, 1, 1) * 0.125
        masked = jnp.where(same_segment, raw_scores, -1e30)
        soft_probs = jnp.exp(masked - log_total[:, None])
        grad_probs = inner_pairing(grad_head, value_head, 1, 1)
        row_delta = jnp.sum(soft_probs * grad_probs, axis=1, keepdims=True)
        grad_scores = (soft_probs * (grad_probs - row_delta)).astype(jnp.bfloat16)
        grad_query = jnp.dot(grad_scores, key_head, preferred_element_type=jnp.float32) * 0.125
        grad_key = inner_pairing(grad_scores, query_head, 0, 0) * 0.125
        grad_value = inner_pairing(soft_probs.astype(jnp.bfloat16), grad_head, 0, 0)
        return (grad_query, grad_key, grad_value)

    full_qkv, full_out, full_gate, full_up, full_down, gain_a, shift_a, gain_b, shift_b = (
        gather_weights(w_qkv, w_out, w_gate, w_up, w_down, gain_one, shift_one, gain_two, shift_two)
    )
    gain_a = gain_a.astype(jnp.float32)
    shift_a = shift_a.astype(jnp.float32)
    gain_b = gain_b.astype(jnp.float32)
    shift_b = shift_b.astype(jnp.float32)
    joined_qkv = jnp.dot(tokens, full_qkv, preferred_element_type=jnp.float32)
    head_parts = joined_qkv.reshape(tok_count, 3, head_count, HD).transpose(1, 2, 0, 3)
    query_low = rotate(head_parts[0], cosine, sine_table).astype(jnp.bfloat16)
    key_low = rotate(head_parts[1], cosine, sine_table).astype(jnp.bfloat16)
    value_low = head_parts[2].astype(jnp.bfloat16)
    attended, log_totals = lax.map(attend, (query_low, key_low, value_low))
    attended = attended.transpose(1, 0, 2).reshape(tok_count, model_width).astype(jnp.bfloat16)
    branch = jnp.dot(attended, full_out, preferred_element_type=jnp.float32)
    normed_one, inv_one = norm_parts(tokens.astype(jnp.float32) + branch)
    hidden = normed_one * gain_a + shift_a
    hidden_low = hidden.astype(jnp.bfloat16)
    gate_proj = jnp.dot(hidden_low, full_gate, preferred_element_type=jnp.float32)
    up_proj = jnp.dot(hidden_low, full_up, preferred_element_type=jnp.float32)
    inner = (jax.nn.silu(gate_proj) * up_proj).astype(jnp.bfloat16)
    feed_out = jnp.dot(inner, full_down, preferred_element_type=jnp.float32)
    normed_two, inv_two = norm_parts(hidden + feed_out)
    output = normed_two * gain_b + shift_b
    pooled = inner_pairing(member_float, output, 0, 0, exact_arithmetic) / sizes_float
    inv_embed = lax.rsqrt(jnp.sum(pooled * pooled, axis=1, keepdims=True) + eps_embed)
    embedding = pooled * inv_embed
    everyone = gather_small(embedding)
    requests = everyone[:, :PAIRS].reshape(-1, model_width)
    passages = everyone[:, PAIRS:].reshape(-1, model_width)
    count = requests.shape[0]
    sims = inner_pairing(requests, passages, 1, 1, exact_arithmetic) / logit_divisor
    row_top = jnp.max(sims, axis=1, keepdims=True)
    exp_terms = jnp.exp(sims - row_top)
    row_sum = jnp.sum(exp_terms, axis=1, keepdims=True)
    log_norm = (row_top + jnp.log(row_sum))[:, 0]
    diagonal = jnp.sum(requests * passages, axis=1) / logit_divisor
    info_loss = jnp.sum(log_norm - diagonal) / count
    pulls = exp_terms / row_sum
    first = (lax.axis_index("dp") * lax.axis_size("fsdp") + lax.axis_index("fsdp")) * PAIRS
    my_rows = lax.dynamic_slice_in_dim(pulls, first, PAIRS, 0)
    my_columns = lax.dynamic_slice_in_dim(pulls, first, PAIRS, 1)
    scale = 1.0 / (logit_divisor * count)
    query_gradient = (
        jnp.dot(my_rows, passages, precision=exact_arithmetic) - embedding[PAIRS:]
    ) * scale
    passage_derivative = (
        inner_pairing(my_columns, requests, 0, 0, exact_arithmetic) - embedding[:PAIRS]
    ) * scale
    grad_embed = jnp.concatenate([query_gradient, passage_derivative], axis=0)
    grad_pooled = inv_embed * grad_embed - inv_embed**3 * pooled * jnp.sum(
        pooled * grad_embed, axis=1, keepdims=True
    )
    grad_output = jnp.dot(member_float, grad_pooled / sizes_float, precision=exact_arithmetic)
    full_qkv, full_out, full_gate, full_up, full_down, gain_a, shift_a, gain_b, shift_b = (
        gather_weights(w_qkv, w_out, w_gate, w_up, w_down, gain_one, shift_one, gain_two, shift_two)
    )
    gain_a = gain_a.astype(jnp.float32)
    gain_b = gain_b.astype(jnp.float32)
    grad_gain_two = jnp.sum(grad_output * normed_two, axis=0)
    grad_shift_two = jnp.sum(grad_output, axis=0)
    grad_second = norm_back(grad_output, normed_two, inv_two, gain_b)
    grad_feed = grad_second.astype(jnp.bfloat16)
    grad_down = inner_pairing(inner, grad_feed, 0, 0)
    grad_inner = inner_pairing(grad_feed, full_down, 1, 1)
    gate_proj = jnp.dot(hidden_low, full_gate, preferred_element_type=jnp.float32)
    up_proj = jnp.dot(hidden_low, full_up, preferred_element_type=jnp.float32)
    sigmoid_gate = jax.nn.sigmoid(gate_proj)
    grad_gate_low = (
        grad_inner * up_proj * sigmoid_gate * (1.0 + gate_proj * (1.0 - sigmoid_gate))
    ).astype(jnp.bfloat16)
    grad_up_low = (grad_inner * gate_proj * sigmoid_gate).astype(jnp.bfloat16)
    grad_gate = inner_pairing(hidden_low, grad_gate_low, 0, 0)
    grad_up = inner_pairing(hidden_low, grad_up_low, 0, 0)
    grad_hidden = (
        grad_second
        + inner_pairing(grad_gate_low, full_gate, 1, 1)
        + inner_pairing(grad_up_low, full_up, 1, 1)
    )
    grad_gain_one = jnp.sum(grad_hidden * normed_one, axis=0)
    grad_shift_one = jnp.sum(grad_hidden, axis=0)
    grad_first = norm_back(grad_hidden, normed_one, inv_one, gain_a)
    grad_branch = grad_first.astype(jnp.bfloat16)
    grad_out = inner_pairing(attended, grad_branch, 0, 0)
    grad_attended = inner_pairing(grad_branch, full_out, 1, 1).astype(jnp.bfloat16)
    grad_heads = grad_attended.reshape(tok_count, head_count, HD).transpose(1, 0, 2)
    grad_query, grad_key, grad_value = lax.map(
        attend_back, (query_low, key_low, value_low, grad_heads, log_totals)
    )
    grad_query = unrotate(grad_query.astype(jnp.bfloat16).astype(jnp.float32), cosine, sine_table)
    grad_key = unrotate(grad_key.astype(jnp.bfloat16).astype(jnp.float32), cosine, sine_table)
    grad_stack = jnp.stack([grad_query, grad_key, grad_value], axis=0)
    grad_joined = (
        grad_stack.transpose(2, 0, 1, 3).reshape(tok_count, 3 * model_width).astype(jnp.bfloat16)
    )
    grad_qkv = inner_pairing(tokens, grad_joined, 0, 0)
    grad_tokens = grad_first + inner_pairing(grad_joined, full_qkv, 1, 1)
    totals = reduce_weights((grad_down, grad_gate, grad_up, grad_out, grad_qkv))
    grad_down, grad_gate, grad_up, grad_out, grad_qkv = totals
    vectors = jnp.stack([grad_gain_one, grad_shift_one, grad_gain_two, grad_shift_two])
    vectors = lax.psum(vectors, ("dp", "fsdp"))
    quarter = vectors.shape[1] // lax.axis_size("fsdp")
    vectors = lax.dynamic_slice_in_dim(vectors, lax.axis_index("fsdp") * quarter, quarter, 1)
    return (
        info_loss,
        output.astype(jnp.bfloat16),
        grad_tokens,
        grad_qkv,
        grad_out,
        grad_gate,
        grad_up,
        grad_down,
        vectors[0],
        vectors[1],
        vectors[2],
        vectors[3],
    )


def solution(mesh):
    placed = (
        P(("dp", "fsdp"), None),
        P(("dp", "fsdp"), None),
        P("fsdp", None),
        P("fsdp", None),
        P("fsdp", None),
        P("fsdp", None),
        P("fsdp", None),
        P("fsdp"),
        P("fsdp"),
        P("fsdp"),
        P("fsdp"),
    )
    return jax.shard_map(
        per_device,
        mesh=mesh,
        in_specs=placed,
        out_specs=(
            P(),
            P(("dp", "fsdp"), None),
            P(("dp", "fsdp"), None),
            P("fsdp", None),
            P("fsdp", None),
            P("fsdp", None),
            P("fsdp", None),
            P("fsdp", None),
            P("fsdp"),
            P("fsdp"),
            P("fsdp"),
            P("fsdp"),
        ),
        check_vma=False,
    )
```

```python
import functools

import jax
import jax.numpy as jnp
from jax import lax
from jax.experimental import pallas as pl
from jax.experimental.pallas import tpu as pltpu
from jax.sharding import PartitionSpec as P

HD = 64
PAIRS = 4
LONG = 768
LANES = 128
FEED_TILE = 512
exact_arithmetic = lax.Precision.HIGHEST
eps_norm = 1e-05
eps_embed = 1e-06
logit_divisor = 0.05
rope_base = 1000.0
log2_e = 1.4426950408889634
f32 = jnp.float32
bf16 = jnp.bfloat16
HBM = pl.BlockSpec(memory_space=pl.ANY)


def call(body, out_shapes, *, grid, in_specs, out_specs, scratch=(), vmem, flops, traffic, name):
    return pl.pallas_call(
        body,
        out_shape=out_shapes,
        grid_spec=pltpu.PrefetchScalarGridSpec(
            num_scalar_prefetch=1,
            grid=grid,
            in_specs=in_specs,
            out_specs=out_specs,
            scratch_shapes=list(scratch),
        ),
        compiler_params=pltpu.CompilerParams(vmem_limit_bytes=vmem * 1024 * 1024),
        cost_estimate=pl.CostEstimate(flops=flops, bytes_accessed=traffic, transcendentals=0),
        name=name,
    )


def whole(shape):
    return pl.BlockSpec(shape, lambda *_: (0,) * len(shape))


def shaped(shape, dtype):
    return jax.ShapeDtypeStruct(shape, dtype)


def matmul(left, right, left_dim=1, right_dim=0, precision=None):
    return lax.dot_general(
        left,
        right,
        (((left_dim,), (right_dim,)), ((), ())),
        precision=precision,
        preferred_element_type=f32,
    )


def start_weight(info, parts, full, sem, columns):
    own, core, far_a, far_b, cross_a, cross_b = parts
    me, side = info[0], info[1]
    rows = own.shape[0]
    half = rows // 2
    places = (
        (own, me * rows, rows),
        (core, (me ^ 1) * rows, rows),
        (far_a, (me ^ 2) * rows + side * half, half),
        (far_b, (me ^ 2) * rows + (1 - side) * half, half),
        (cross_a, (me ^ 3) * rows + side * half, half),
        (cross_b, (me ^ 3) * rows + (1 - side) * half, half),
    )
    for piece, start, count in places:
        pltpu.make_async_copy(
            piece.at[:, columns],
            full.at[pl.ds(pl.multiple_of(start, 32), count), columns],
            sem,
        ).start()


def wait_weight(full, sem, columns):
    pltpu.make_async_copy(full.at[:, columns], full.at[:, columns], sem).wait()


def turn_rows(info, turned, target):
    count = turned.shape[0] // 4
    for k in range(4):
        start = pl.multiple_of((info[0] ^ k) * count, 32)
        target[k] = turned[pl.ds(start, count), :]


def sigmoid(value):
    return 0.5 * jnp.tanh(0.5 * value) + 0.5


def roll_body(info, tokens, rolled, turned, scratch):
    count, width = tokens.shape
    shift = lax.rem(count - info[2], count)
    for first in range(0, width, LANES):
        lanes = pl.ds(first, LANES)
        moved = pltpu.roll(tokens[:, lanes].astype(f32), shift, 0).astype(bf16)
        rolled[:, lanes] = moved
        scratch[pl.ds(first, LANES), :] = moved.T
    turn_rows(info, scratch, turned)


def roll_tokens(info, tokens):
    count, width = tokens.shape
    return call(
        roll_body,
        (shaped(tokens.shape, bf16), shaped((4, width // 4, count), bf16)),
        grid=(1,),
        in_specs=[whole(tokens.shape)],
        out_specs=(whole(tokens.shape), whole((4, width // 4, count))),
        scratch=[pltpu.VMEM((width, count), bf16)],
        vmem=12,
        flops=0,
        traffic=count * width * 6,
        name="roll_tokens",
    )(info, tokens)


def unroll_body(info, value, moved):
    count = value.shape[0]
    for first in range(0, value.shape[1], LANES):
        lanes = pl.ds(first, LANES)
        moved[:, lanes] = pltpu.roll(value[:, lanes].astype(f32), info[2], 0).astype(moved.dtype)


def unroll(info, value):
    count, width = value.shape
    tile = 256
    spec = pl.BlockSpec((count, tile), lambda i, *_: (0, i))
    return call(
        unroll_body,
        shaped(value.shape, value.dtype),
        grid=(width // tile,),
        in_specs=[spec],
        out_specs=spec,
        vmem=8,
        flops=0,
        traffic=count * width * 4,
        name="unroll",
    )(info, value)


def rope_lanes(value, cosine, signed_sine):
    lane = lax.broadcasted_iota(jnp.int32, (value.shape[0], LANES), 1)
    first_half = (lane & 32) == 0
    out = []
    for start in range(0, value.shape[1], LANES):
        piece = value[:, start : start + LANES]
        partner = jnp.where(first_half, pltpu.roll(piece, LANES - 32, 1), pltpu.roll(piece, 32, 1))
        out.append(piece * cosine + partner * signed_sine)
    return out[0] if len(out) == 1 else jnp.concatenate(out, axis=1)


def qkv_body(info, rolled, cosine, signed_sine, *rest):
    parts, (joined, kept, full, sems, keep_sem) = rest[:6], rest[6:]
    step = pl.program_id(0)
    steps = pl.num_programs(0)
    tile = joined.shape[1]

    @pl.when(step == 0)
    def _():
        for j in range(full.shape[1] // tile):
            start_weight(info, parts, full, sems.at[j], pl.ds(j * tile, tile))

    columns = pl.ds(pl.multiple_of(step * tile, tile), tile)
    wait_weight(full, sems.at[step], columns)
    pltpu.make_async_copy(full.at[:, columns], kept.at[:, columns], keep_sem.at[step]).start()
    chunk = 512

    @pl.when(step < 2 * steps // 3)
    def _():
        for first in range(0, joined.shape[0], chunk):
            rows = pl.ds(first, chunk)
            product = matmul(rolled[rows, :], full[:, columns])
            turned = rope_lanes(product, cosine[rows, :], signed_sine[rows, :])
            joined[rows, :] = turned.astype(bf16)

    @pl.when(step >= 2 * steps // 3)
    def _():
        for first in range(0, joined.shape[0], chunk):
            rows = pl.ds(first, chunk)
            joined[rows, :] = matmul(rolled[rows, :], full[:, columns]).astype(bf16)

    @pl.when(step == steps - 1)
    def _():
        for j in range(full.shape[1] // tile):
            piece = pl.ds(j * tile, tile)
            pltpu.make_async_copy(full.at[:, piece], kept.at[:, piece], keep_sem.at[j]).wait()


def project_qkv(info, rolled, cosine, signed_sine, parts):
    count, width = rolled.shape
    columns = parts[0].shape[1]
    tile = width
    return call(
        qkv_body,
        (shaped((count, columns), bf16), shaped((width, columns), bf16)),
        grid=(columns // tile,),
        in_specs=[whole(rolled.shape), whole(cosine.shape), whole(cosine.shape)] + [HBM] * 6,
        out_specs=(pl.BlockSpec((count, tile), lambda i, *_: (0, i)), HBM),
        scratch=[
            pltpu.VMEM((width, columns), bf16),
            pltpu.SemaphoreType.DMA((columns // tile,)),
            pltpu.SemaphoreType.DMA((columns // tile,)),
        ],
        vmem=22,
        flops=2 * count * width * columns,
        traffic=2 * (count * width + width * columns + count * columns),
        name="project_qkv",
    )(info, rolled, cosine, signed_sine, *parts)


def attend_body(info, query, key, value, bias, attended, logs):
    pair = pl.program_id(0)
    count = query.shape[0]
    scale = 0.125 * log2_e
    lane = lax.broadcasted_iota(jnp.int32, (1, LANES), 1)

    @pl.when(pair == 0)
    def _():
        logs[...] = jnp.zeros_like(logs)

    def rows_of(first, size, keys, offset):
        rows = pl.ds(first, size)
        ones = jnp.ones((keys.size, LANES), bf16)
        extended = jnp.concatenate([value[keys, :], ones], axis=1)
        picked = []
        kept_logs = logs[rows, :]
        for head in range(2):
            mine = (lane >= HD) if head else (lane < HD)
            masked = jnp.where(mine, query[rows, :], jnp.zeros((), bf16))
            scores = matmul(masked, key[keys, :], 1, 1) * scale
            if offset is not None:
                scores = scores + offset
            top = jnp.max(scores, axis=1, keepdims=True)
            terms = jnp.exp2(scores - top).astype(bf16)
            product = matmul(terms, extended)
            total = product[:, LANES:]
            picked.append(product[:, :LANES] / total)
            kept_logs = jnp.where(lane == 2 * pair + head, top + jnp.log2(total), kept_logs)
        attended[rows, :] = jnp.where(lane < HD, picked[0], picked[1]).astype(bf16)
        logs[rows, :] = kept_logs

    for first in range(0, LONG, 256):
        rows_of(first, 256, pl.ds(0, LONG), None)
    rest = count - LONG
    rows_of(LONG, rest, pl.ds(LONG, rest), bias[...])


def attend(info, joined, bias):
    count, columns = joined.shape
    width = columns // 3
    pairs = width // LANES
    specs = [pl.BlockSpec((count, LANES), lambda i, *_, n=n: (0, n * pairs + i)) for n in range(3)]
    return call(
        attend_body,
        (shaped((count, width), bf16), shaped((count, LANES), f32)),
        grid=(pairs,),
        in_specs=specs + [whole(bias.shape)],
        out_specs=(pl.BlockSpec((count, LANES), lambda i, *_: (0, i)), whole((count, LANES))),
        vmem=16,
        flops=2 * 2 * 256 * 2 * pairs * (LONG * LONG + (count - LONG) ** 2),
        traffic=8 * count * width,
        name="attend",
    )(info, joined, joined, joined, bias)


def norm_parts(value):
    centered = value - jnp.mean(value, axis=1, keepdims=True)
    root = lax.rsqrt(jnp.mean(centered * centered, axis=1, keepdims=True) + eps_norm)
    return centered * root, root


def branch_body(info, attended, rolled, *rest):
    parts, (normed, root, turned, kept, full, scratch, sem, keep_sem) = rest[:6], rest[6:]
    step = pl.program_id(0)

    @pl.when(step == 0)
    def _():
        start_weight(info, parts, full, sem, pl.ds(0, full.shape[1]))
        wait_weight(full, sem, pl.ds(0, full.shape[1]))
        pltpu.make_async_copy(full, kept, keep_sem).start()

    first = rolled[...].astype(f32) + matmul(attended[...], full[...])
    value, inverse = norm_parts(first)
    normed[...] = value
    root[...] = jnp.broadcast_to(inverse, root.shape)
    scratch[...] = attended[...].T
    turn_rows(info, scratch, turned)

    @pl.when(step == pl.num_programs(0) - 1)
    def _():
        pltpu.make_async_copy(full, kept, keep_sem).wait()


def add_branch(info, attended, rolled, parts):
    count, width = attended.shape
    tile = 256
    rows = pl.BlockSpec((tile, width), lambda i, *_: (i, 0))
    return call(
        branch_body,
        (
            shaped((count, width), f32),
            shaped((count, LANES), f32),
            shaped((4, width // 4, count), bf16),
            shaped((width, width), bf16),
        ),
        grid=(count // tile,),
        in_specs=[rows, rows] + [HBM] * 6,
        out_specs=(
            rows,
            pl.BlockSpec((tile, LANES), lambda i, *_: (i, 0)),
            pl.BlockSpec((4, width // 4, tile), lambda i, *_: (0, 0, i)),
            HBM,
        ),
        scratch=[
            pltpu.VMEM((width, width), bf16),
            pltpu.VMEM((width, tile), bf16),
            pltpu.SemaphoreType.DMA,
            pltpu.SemaphoreType.DMA,
        ],
        vmem=14,
        flops=2 * count * width * width,
        traffic=count * width * 10,
        name="add_branch",
    )(info, attended, rolled, *parts)


def gate_body(info, normed, gain, shift, *rest):
    gate_parts, up_parts = rest[:6], rest[6:12]
    (inner, gate_out, up_out, turned, gate_kept, up_kept) = rest[12:18]
    (gate_full, up_full, low, scratch, sems, keep_sems) = rest[18:]
    step = pl.program_id(0)
    steps = pl.num_programs(0)
    tile = inner.shape[1]
    chunk = 512

    @pl.when(step == 0)
    def _():
        for j in range(gate_full.shape[1] // tile):
            columns = pl.ds(j * tile, tile)
            start_weight(info, gate_parts, gate_full, sems.at[0, j], columns)
            start_weight(info, up_parts, up_full, sems.at[1, j], columns)
        for first in range(0, low.shape[0], chunk):
            rows = pl.ds(first, chunk)
            value = (normed[rows, :] * gain[...] + shift[...]).astype(bf16)
            low[rows, :] = value
            scratch[:, rows] = value.T
        turn_rows(info, scratch, turned)

    columns = pl.ds(pl.multiple_of(step * tile, tile), tile)
    wait_weight(gate_full, sems.at[0, step], columns)
    wait_weight(up_full, sems.at[1, step], columns)
    for full, kept, which in ((gate_full, gate_kept, 0), (up_full, up_kept, 1)):
        pltpu.make_async_copy(
            full.at[:, columns], kept.at[:, columns], keep_sems.at[which, step]
        ).start()
    for first in range(0, low.shape[0], chunk):
        rows = pl.ds(first, chunk)
        gate = matmul(low[rows, :], gate_full[:, columns])
        up = matmul(low[rows, :], up_full[:, columns])
        gate_out[rows, :] = gate.astype(bf16)
        up_out[rows, :] = up.astype(bf16)
        inner[rows, :] = (gate * up * sigmoid(gate)).astype(bf16)

    @pl.when(step == steps - 1)
    def _():
        for full, kept, which in ((gate_full, gate_kept, 0), (up_full, up_kept, 1)):
            for j in range(full.shape[1] // tile):
                piece = pl.ds(j * tile, tile)
                pltpu.make_async_copy(
                    full.at[:, piece], kept.at[:, piece], keep_sems.at[which, j]
                ).wait()


def gate_and_up(info, normed, gain, shift, gate_parts, up_parts):
    count, width = normed.shape
    hidden = gate_parts[0].shape[1]
    tile = 512
    columns = pl.BlockSpec((count, tile), lambda i, *_: (0, i))
    return call(
        gate_body,
        (shaped((count, hidden), bf16),) * 3
        + (shaped((4, width // 4, count), bf16),)
        + (shaped((width, hidden), bf16),) * 2,
        grid=(hidden // tile,),
        in_specs=[whole(normed.shape), whole(gain.shape), whole(shift.shape)] + [HBM] * 12,
        out_specs=(columns,) * 3 + (whole((4, width // 4, count)), HBM, HBM),
        scratch=[
            pltpu.VMEM((width, hidden), bf16),
            pltpu.VMEM((width, hidden), bf16),
            pltpu.VMEM((count, width), bf16),
            pltpu.VMEM((width, count), bf16),
            pltpu.SemaphoreType.DMA((2, hidden // tile)),
            pltpu.SemaphoreType.DMA((2, hidden // tile)),
        ],
        vmem=32,
        flops=4 * count * width * hidden,
        traffic=count * hidden * 6 + width * hidden * 8,
        name="gate_and_up",
    )(info, normed, gain, shift, *gate_parts, *up_parts)


def down_body(info, inner, normed, gain_one, shift_one, gain, shift, member, sizes, *rest):
    parts = rest[:6]
    (output, normed_two, root, pooled, embedding, kept) = rest[6:12]
    (full, sem, keep_sem) = rest[12:]
    step = pl.program_id(0)
    steps = pl.num_programs(0)

    @pl.when(step == 0)
    def _():
        start_weight(info, parts, full, sem, pl.ds(0, full.shape[1]))
        pooled[...] = jnp.zeros_like(pooled)
        wait_weight(full, sem, pl.ds(0, full.shape[1]))
        pltpu.make_async_copy(full, kept, keep_sem).start()

    feed = matmul(inner[...], full[...])
    hidden = normed[...] * gain_one[...] + shift_one[...]
    value, inverse = norm_parts(hidden + feed)
    normed_two[...] = value
    root[...] = jnp.broadcast_to(inverse, root.shape)
    result = value * gain[...] + shift[...]
    output[...] = result.astype(bf16)
    pooled[...] += matmul(member[...], result, 0, 0, exact_arithmetic)

    @pl.when(step == steps - 1)
    def _():
        total = pooled[...] / sizes[...]
        pooled[...] = total
        square = jnp.sum(total * total, axis=1, keepdims=True)
        embedding[...] = total * lax.rsqrt(square + eps_embed)
        pltpu.make_async_copy(full, kept, keep_sem).wait()


def down_and_pool(info, inner, normed, gain_one, shift_one, gain, shift, member, sizes, parts):
    count, width = normed.shape
    hidden = inner.shape[1]
    seqs = member.shape[1]
    tile = 256
    rows = pl.BlockSpec((tile, width), lambda i, *_: (i, 0))
    vector = whole((1, width))
    return call(
        down_body,
        (
            shaped((count, width), bf16),
            shaped((count, width), f32),
            shaped((count, LANES), f32),
            shaped((seqs, width), f32),
            shaped((seqs, width), f32),
            shaped((hidden, width), bf16),
        ),
        grid=(count // tile,),
        in_specs=[
            pl.BlockSpec((tile, hidden), lambda i, *_: (i, 0)),
            rows,
            vector,
            vector,
            vector,
            vector,
            pl.BlockSpec((tile, seqs), lambda i, *_: (i, 0)),
            whole(sizes.shape),
        ]
        + [HBM] * 6,
        out_specs=(
            rows,
            rows,
            pl.BlockSpec((tile, LANES), lambda i, *_: (i, 0)),
            whole((seqs, width)),
            whole((seqs, width)),
            HBM,
        ),
        scratch=[
            pltpu.VMEM((hidden, width), bf16),
            pltpu.SemaphoreType.DMA,
            pltpu.SemaphoreType.DMA,
        ],
        vmem=24,
        flops=2 * count * width * hidden,
        traffic=count * hidden * 2 + width * hidden * 4 + count * width * 10,
        name="down_and_pool",
    )(info, inner, normed, gain_one, shift_one, gain, shift, member, sizes, *parts)


def loss_body(info, everyone, pooled, embedding, sizes, member, normed, root, gain, *rest):
    (loss, grad_second, grad_feed, vectors, pulled) = rest
    step = pl.program_id(0)
    seqs, width = embedding.shape
    pairs = seqs // 2

    @pl.when(step == 0)
    def _():
        devices = everyone.shape[0] // seqs
        count = devices * pairs
        blocks = everyone[...].reshape(devices, seqs, width)
        requests = blocks[:, :pairs].reshape(count, width)
        passages = blocks[:, pairs:].reshape(count, width)
        sims = matmul(requests, passages, 1, 1, exact_arithmetic) * (1.0 / logit_divisor)
        top = jnp.max(sims, axis=1, keepdims=True)
        terms = jnp.exp(sims - top)
        total = jnp.sum(terms, axis=1, keepdims=True)
        row = lax.broadcasted_iota(jnp.int32, sims.shape, 0)
        column = lax.broadcasted_iota(jnp.int32, sims.shape, 1)
        diagonal = jnp.sum(jnp.where(row == column, sims, 0.0), axis=1, keepdims=True)
        mean = jnp.sum(top + jnp.log(total) - diagonal, axis=0, keepdims=True) / count
        loss[...] = jnp.broadcast_to(mean, loss.shape)
        pulls = terms / total
        first = info[3] * pairs
        near = lax.broadcasted_iota(jnp.int32, (seqs, count), 0)
        place = lax.broadcasted_iota(jnp.int32, (seqs, count), 1)
        picked = jnp.where(place == first + near, 1.0, 0.0)
        my_rows = matmul(picked, pulls, 1, 0, exact_arithmetic)
        my_columns = matmul(picked, pulls, 1, 1, exact_arithmetic)
        to_requests = matmul(my_rows, passages, 1, 0, exact_arithmetic)
        to_passages = matmul(my_columns, requests, 1, 0, exact_arithmetic)
        own = embedding[...]
        swapped = jnp.concatenate([own[pairs:], own[:pairs]], axis=0)
        gathered = jnp.concatenate([to_requests[:pairs], to_passages[:pairs]], axis=0)
        grad_embed = (gathered - swapped) * (1.0 / (logit_divisor * count))
        means = pooled[...]
        inverse = lax.rsqrt(jnp.sum(means * means, axis=1, keepdims=True) + eps_embed)
        along = jnp.sum(means * grad_embed, axis=1, keepdims=True)
        pulled[...] = (inverse * grad_embed - inverse * inverse * inverse * means * along) / sizes[
            ...
        ]
        vectors[...] = jnp.zeros_like(vectors)

    upstream = matmul(member[...], pulled[...], 1, 0, exact_arithmetic)
    value = normed[...]
    vectors[0:1, :] += jnp.sum(upstream * value, axis=0, keepdims=True)
    vectors[1:2, :] += jnp.sum(upstream, axis=0, keepdims=True)
    result = norm_back(upstream, value, root[:, :1], gain[...])
    grad_second[...] = result
    grad_feed[...] = result.astype(bf16)


def norm_back(upstream, normed, root, gain):
    scaled = upstream * gain
    return root * (
        scaled
        - jnp.mean(scaled, axis=1, keepdims=True)
        - normed * jnp.mean(scaled * normed, axis=1, keepdims=True)
    )


def loss_and_norm(info, everyone, pooled, embedding, sizes, member, normed, root, gain):
    count, width = normed.shape
    seqs = member.shape[1]
    tile = 256
    rows = pl.BlockSpec((tile, width), lambda i, *_: (i, 0))
    return call(
        loss_body,
        (
            shaped((8, LANES), f32),
            shaped((count, width), f32),
            shaped((count, width), bf16),
            shaped((8, width), f32),
        ),
        grid=(count // tile,),
        in_specs=[
            whole(everyone.shape),
            whole(pooled.shape),
            whole(embedding.shape),
            whole(sizes.shape),
            pl.BlockSpec((tile, seqs), lambda i, *_: (i, 0)),
            rows,
            pl.BlockSpec((tile, LANES), lambda i, *_: (i, 0)),
            whole(gain.shape),
        ],
        out_specs=(whole((8, LANES)), rows, rows, whole((8, width))),
        scratch=[pltpu.VMEM((seqs, width), f32)],
        vmem=16 + everyone.shape[0] * width * 24 // 2**20,
        flops=0,
        traffic=count * width * 10,
        name="loss_and_norm",
    )(info, everyone, pooled, embedding, sizes, member, normed, root, gain)


def outer_body(info, left, right, out):
    out[0] = matmul(left[...], right[...], 0, 0).astype(bf16)


def down_gradient(info, inner, grad_feed, order, name):
    count, hidden = inner.shape
    width = grad_feed.shape[1]
    rows = hidden // 4
    first, last = order

    def column(i, info):
        return (0, info[0] ^ jnp.where(i == 0, first, last))

    return call(
        outer_body,
        shaped((2, rows, width), bf16),
        grid=(2,),
        in_specs=[pl.BlockSpec((count, rows), column), whole(grad_feed.shape)],
        out_specs=pl.BlockSpec((1, rows, width), lambda i, *_: (i, 0, 0)),
        vmem=18,
        flops=count * hidden * width,
        traffic=count * hidden + count * width * 2 + hidden * width,
        name=name,
    )(info, inner, grad_feed)


def feed_body(last, info, grad_feed, turned, gate_in, up_in, down, gate_full, up_full, *rest):
    if last:
        held, theirs, own, grad_hidden = rest
    else:
        theirs, own, grad_hidden = rest
    step = pl.program_id(0)
    count = grad_feed.shape[0]
    chunk = 512
    gates, ups = [], []

    @pl.when(step == 0)
    def _():
        grad_hidden[...] = held[...] if last else jnp.zeros_like(grad_hidden)

    for first in range(0, count, chunk):
        rows = pl.ds(first, chunk)
        grad_inner = matmul(grad_feed[rows, :], down[...], 1, 1)
        gate = gate_in[rows, :].astype(f32)
        up = up_in[rows, :].astype(f32)
        share = sigmoid(gate)
        scaled = grad_inner * share
        grad_gate = (scaled * up * (1.0 + gate * (1.0 - share))).astype(bf16)
        grad_up = (scaled * gate).astype(bf16)
        gates.append(grad_gate)
        ups.append(grad_up)
        grad_hidden[rows, :] += matmul(grad_gate, gate_full[...], 1, 1) + matmul(
            grad_up, up_full[...], 1, 1
        )
    for which, pieces in ((0, gates), (1, ups)):
        grad = jnp.concatenate(pieces, axis=0)
        for k, (out, place) in enumerate(((own, 1), (theirs, 1), (own, 0), (theirs, 0))):
            out[place, which] = matmul(turned[k], grad).astype(bf16)


def feed_back(info, grad_feed, turned, gate, up, down, gate_full, up_full, base, steps, held):
    count = gate.shape[0]
    width = grad_feed.shape[1]
    quarter = width // 4
    tile = FEED_TILE
    share = steps * tile
    columns = pl.BlockSpec((count, tile), lambda i, *_: (0, base + i))
    weights = pl.BlockSpec((width, tile), lambda i, *_: (0, base + i))
    outs = pl.BlockSpec((2, 2, quarter, tile), lambda i, *_: (0, 0, 0, i))
    in_specs = [
        whole(grad_feed.shape),
        whole(turned.shape),
        columns,
        columns,
        pl.BlockSpec((tile, width), lambda i, *_: (base + i, 0)),
        weights,
        weights,
    ]
    args = [grad_feed, turned, gate, up, down, gate_full, up_full]
    if held is not None:
        in_specs.append(whole(held.shape))
        args.append(held)
    return call(
        functools.partial(feed_body, held is not None),
        (
            shaped((2, 2, quarter, share), bf16),
            shaped((2, 2, quarter, share), bf16),
            shaped((count, width), f32),
        ),
        grid=(steps,),
        in_specs=in_specs,
        out_specs=(outs, outs, whole((count, width))),
        vmem=40,
        flops=10 * count * width * share,
        traffic=count * share * 4 + width * share * 10 + count * width * 6,
        name=f"feed_back_{base}",
    )(info, *args)


def first_body(info, grad_hidden, grad_second, normed, root, gain, turned, weight, *rest):
    (grad_first, grad_attended, theirs, own, vectors, low) = rest
    step = pl.program_id(0)
    steps = pl.num_programs(0)
    tile = grad_first.shape[0]

    @pl.when(step == 0)
    def _():
        vectors[...] = jnp.zeros_like(vectors)

    upstream = grad_hidden[...] + grad_second[...]
    value = normed[...]
    vectors[0:1, :] += jnp.sum(upstream * value, axis=0, keepdims=True)
    vectors[1:2, :] += jnp.sum(upstream, axis=0, keepdims=True)
    result = norm_back(upstream, value, root[:, :1], gain[...])
    grad_first[...] = result
    branch = result.astype(bf16)
    low[pl.ds(pl.multiple_of(step * tile, tile), tile), :] = branch
    grad_attended[...] = matmul(branch, weight[...], 1, 1).astype(bf16)

    @pl.when(step == steps - 1)
    def _():
        for k, (out, place) in enumerate(((own, 1), (theirs, 1), (own, 0), (theirs, 0))):
            out[place] = matmul(turned[k], low[...]).astype(bf16)


def first_back(info, grad_hidden, grad_second, normed, root, gain, turned, weight):
    count, width = normed.shape
    quarter = width // 4
    tile = 256
    rows = pl.BlockSpec((tile, width), lambda i, *_: (i, 0))
    pieces = shaped((2, quarter, width), bf16)
    return call(
        first_body,
        (
            shaped((count, width), f32),
            shaped((count, width), bf16),
            pieces,
            pieces,
            shaped((8, width), f32),
        ),
        grid=(count // tile,),
        in_specs=[
            rows,
            rows,
            rows,
            pl.BlockSpec((tile, LANES), lambda i, *_: (i, 0)),
            whole(gain.shape),
            whole(turned.shape),
            whole(weight.shape),
        ],
        out_specs=(
            rows,
            rows,
            whole((2, quarter, width)),
            whole((2, quarter, width)),
            whole((8, width)),
        ),
        scratch=[pltpu.VMEM((count, width), bf16)],
        vmem=24,
        flops=4 * count * width * width,
        traffic=count * width * 20,
        name="first_back",
    )(info, grad_hidden, grad_second, normed, root, gain, turned, weight)


def attend_back_body(info, query, key, value, attended, upstream, logs, bias, cosine, sine, *rest):
    (grad_query, grad_key, grad_value, logs_row, sums) = rest
    pair = pl.program_id(0)
    count = query.shape[0]
    scale = 0.125 * log2_e
    lane = lax.broadcasted_iota(jnp.int32, (1, LANES), 1)

    @pl.when(pair == 0)
    def _():
        logs_row[...] = logs[...].T

    both = upstream[...].astype(f32) * attended[...].astype(f32)
    row = lax.broadcasted_iota(jnp.int32, (8, LANES), 0)
    column = lax.broadcasted_iota(jnp.int32, (8, LANES), 1)
    chooser = jnp.where((column // HD) == row, 1.0, 0.0)
    sums[...] = matmul(chooser, both, 1, 1, exact_arithmetic)

    zero = jnp.zeros((), bf16)
    for first, size, offset in ((0, LONG, None), (LONG, count - LONG, bias)):
        rows = pl.ds(first, size)
        key_rows, query_rows, up_rows = key[rows, :], query[rows, :], upstream[rows, :]
        key_grad = value_grad = query_grad = None
        for head in range(2):
            mine = (lane >= HD) if head else (lane < HD)
            masked_query = jnp.where(mine, query_rows, zero)
            masked_up = jnp.where(mine, up_rows, zero)
            masked_key = jnp.where(mine, key_rows, zero)
            log_row = logs_row[pl.ds(2 * pair + head, 1), rows]
            sum_row = sums[head : head + 1, rows]
            key_pieces, value_pieces = [], []
            query_total = None
            for start in range(first, first + size, 256):
                keys = pl.ds(start, 256)
                scores = matmul(key[keys, :], masked_query, 1, 1) * scale
                if offset is not None:
                    scores = scores + offset[...]
                probs = jnp.exp2(scores - log_row)
                grad_probs = matmul(value[keys, :], masked_up, 1, 1)
                grad_scores = (probs * (grad_probs - sum_row)).astype(bf16)
                value_pieces.append(matmul(probs.astype(bf16), masked_up))
                key_pieces.append(matmul(grad_scores, masked_query))
                kept_key = masked_key[start - first : start - first + 256]
                piece = matmul(grad_scores, kept_key, 0, 0)
                query_total = piece if query_total is None else query_total + piece
            key_head = jnp.concatenate(key_pieces, axis=0)
            value_head = jnp.concatenate(value_pieces, axis=0)
            key_grad = key_head if key_grad is None else key_grad + key_head
            value_grad = value_head if value_grad is None else value_grad + value_head
            query_grad = query_total if query_grad is None else query_grad + query_total
        turn_cos, turn_sin = cosine[rows, :], sine[rows, :]
        for grad, target in ((query_grad, grad_query), (key_grad, grad_key)):
            low = (grad * 0.125).astype(bf16).astype(f32)
            target[rows, :] = rope_lanes(low, turn_cos, -turn_sin).astype(bf16)
        grad_value[rows, :] = value_grad.astype(bf16)


def attend_back(info, joined, attended, upstream, logs, bias, cosine, sine):
    count, columns = joined.shape
    width = columns // 3
    pairs = width // LANES
    specs = [pl.BlockSpec((count, LANES), lambda i, *_, n=n: (0, n * pairs + i)) for n in range(3)]
    block = pl.BlockSpec((count, LANES), lambda i, *_: (0, i))
    return call(
        attend_back_body,
        (shaped((count, width), bf16),) * 3,
        grid=(pairs,),
        in_specs=specs
        + [block, block, whole(logs.shape), whole(bias.shape)]
        + [whole(cosine.shape)] * 2,
        out_specs=(block,) * 3,
        scratch=[pltpu.VMEM((LANES, count), f32), pltpu.VMEM((8, count), f32)],
        vmem=32,
        flops=5 * 2 * 256 * 2 * pairs * (LONG * LONG + (count - LONG) ** 2),
        traffic=16 * count * width,
        name="attend_back",
    )(info, joined, joined, joined, attended, upstream, logs, bias, cosine, sine)


def turned_body(info, turned, grad, theirs, own):
    for k, (out, place) in enumerate(((own, 1), (theirs, 1), (own, 0), (theirs, 0))):
        out[place] = matmul(turned[k], grad[...]).astype(bf16)


def weight_gradient(info, turned, grad, name):
    _, quarter, count = turned.shape
    width = grad.shape[1]
    tile = 384
    out = pl.BlockSpec((2, quarter, tile), lambda i, *_: (0, 0, i))
    return call(
        turned_body,
        (shaped((2, quarter, width), bf16),) * 2,
        grid=(width // tile,),
        in_specs=[whole(turned.shape), pl.BlockSpec((count, tile), lambda i, *_: (0, i))],
        out_specs=(out, out),
        vmem=14,
        flops=8 * quarter * count * width,
        traffic=8 * quarter * count + 2 * count * width + 8 * quarter * width,
        name=name,
    )(info, turned, grad)


def tokens_body(info, grad_first, grad_query, grad_key, grad_value, weight, out):
    width = grad_query.shape[1]
    total = grad_first[...]
    for index, grad in enumerate((grad_query, grad_key, grad_value)):
        total = total + matmul(grad[...], weight[:, index * width : (index + 1) * width], 1, 1)
    out[...] = pltpu.roll(total, info[2], 0)


def tokens_gradient(info, grad_first, grad_query, grad_key, grad_value, weight):
    count, width = grad_first.shape
    tile = 256
    block = pl.BlockSpec((count, tile), lambda i, *_: (0, i))
    return call(
        tokens_body,
        shaped((count, width), f32),
        grid=(width // tile,),
        in_specs=[block]
        + [whole(grad_query.shape)] * 3
        + [pl.BlockSpec((tile, weight.shape[1]), lambda i, *_: (i, 0))],
        out_specs=block,
        vmem=24,
        flops=2 * count * width * weight.shape[1],
        traffic=count * width * 14 + 2 * width * weight.shape[1],
        name="tokens_gradient",
    )(info, grad_first, grad_query, grad_key, grad_value, weight)


def swap(value, axis, bit):
    size = lax.axis_size(axis)
    return lax.ppermute(value, axis, [(i, i ^ bit) for i in range(size)])


def choose(value, index):
    return lax.dynamic_index_in_dim(value, index, 0, keepdims=False)


def low_sum(*terms):
    total = terms[0].astype(f32)
    for term in terms[1:]:
        total = total + term.astype(f32)
    return total.astype(bf16)


class Order:
    def __init__(self):
        self.last = None

    def after(self, *values):
        if self.last is not None:
            values = lax.optimization_barrier((*values, self.last))[:-1]
        return values[0] if len(values) == 1 else values

    def done(self, value):
        self.last = value


def gather_weight(shard, side):
    rows, columns = shard.shape
    core = swap(shard, "fsdp", 1)
    far_a = swap(choose(shard.reshape(2, rows // 2, columns), side), "fsdp", 2)
    far_b = swap(far_a, "dp", 1)
    return shard, core, far_a, far_b, swap(far_a, "fsdp", 1), swap(far_b, "fsdp", 1)


def gather_vectors(vectors, me):
    core = swap(vectors, "fsdp", 1)
    far = swap(vectors, "fsdp", 2)
    pieces = jnp.stack([vectors, core, far, swap(far, "fsdp", 1)])
    full = jnp.concatenate([choose(pieces, me ^ q) for q in range(4)], axis=1)
    return [full[i : i + 1].astype(f32) for i in range(vectors.shape[0])]


def gather_blocks(block):
    dp_size, fsdp_size = lax.axis_size("dp"), lax.axis_size("fsdp")
    bits = dp_size.bit_length() - 1
    held = block[None]
    for bit in reversed(range(bits)):
        other = swap(held, "dp", 1 << bit)
        low = ((lax.axis_index("dp") >> bit) & 1) == 0
        held = jnp.where(low, jnp.stack([held, other]), jnp.stack([other, held]))
        held = held.reshape((-1,) + block.shape)
    held = held.reshape((2,) * bits + block.shape)
    held = held.transpose(tuple(range(bits))[::-1] + tuple(range(bits, bits + block.ndim)))
    held = held.reshape((dp_size,) + block.shape)
    held = lax.all_gather(held, "fsdp", axis=1)
    return held.reshape((dp_size * fsdp_size,) + block.shape)


def reduce_steps(order, theirs, own):
    dp = lax.axis_index("dp")
    bits = lax.axis_size("dp").bit_length() - 1
    split = min(bits, 3)
    from_core = swap(order.after(theirs), "fsdp", 1)
    yield None
    total = low_sum(order.after(own)[0], from_core[0])
    order.done(total)
    from_far = swap(total, "fsdp", 2)
    yield None
    held = (order.after(own)[1], from_core[1], from_far)
    for step in range(split):
        side = (dp >> step) & 1
        rows = held[0].shape[0] // 2
        halves = [term.reshape(2, rows, -1) for term in held]
        send = low_sum(*[choose(half, 1 - side) for half in halves])
        order.done(send)
        other = swap(send, "dp", 1 << step)
        yield None
        kept = [choose(half, side) for half in halves]
        kept[0] = order.after(kept[0])
        held = (*kept, other)
    held = low_sum(*held)
    for step in range(split, bits):
        order.done(held)
        other = swap(held, "dp", 1 << step)
        yield None
        held = low_sum(order.after(held), other)
    for step in reversed(range(split)):
        order.done(held)
        other = swap(held, "dp", 1 << step)
        yield None
        side = (dp >> step) & 1
        held = order.after(held)
        held = jnp.where(side == 0, jnp.concatenate([held, other]), jnp.concatenate([other, held]))
    held = held.astype(f32)
    order.done(held)
    yield held


def sum_steps(value):
    for axis, bits in (("fsdp", 2), ("dp", lax.axis_size("dp").bit_length() - 1)):
        for bit in range(bits):
            other = swap(value, axis, 1 << bit)
            yield None
            value = value + other
    yield value


def pack_layout(lengths_row, count):
    ends = jnp.cumsum(lengths_row)
    starts = ends - lengths_row
    shift = jnp.sum(jnp.where(lengths_row == LONG, starts, 0))
    places = lax.rem(lax.iota(jnp.int32, count) + shift, count)
    segment = jnp.sum((places[:, None] >= ends[None, :]).astype(jnp.int32), axis=1)
    member = segment[:, None] == lax.iota(jnp.int32, lengths_row.shape[0])[None, :]
    offset = jnp.sum(jnp.where(member, starts[None, :], 0), axis=1)
    return shift, segment, places - offset, member.astype(f32)


def rotary_tables(position):
    lane = lax.iota(jnp.int32, LANES)
    frequency = rope_base ** (-2.0 * (lane % (HD // 2)).astype(f32) / HD)
    angles = position.astype(f32)[:, None] * frequency[None, :]
    sine = jnp.sin(angles)
    return jnp.cos(angles), jnp.where((lane & (HD // 2)) == 0, -sine, sine)


def per_device(
    tokens, lengths, w_qkv, w_out, w_gate, w_up, w_down, gain_one, shift_one, gain_two, shift_two
):
    count, width = tokens.shape
    me = lax.axis_index("fsdp")
    dp = lax.axis_index("dp")
    side = dp & 1
    order = Order()

    shift, segment, position, member = pack_layout(lengths[0], count)
    sizes = lengths[0].astype(f32)[:, None]
    cosine, sine = rotary_tables(position)
    tail = segment[LONG:]
    bias = jnp.where(tail[:, None] == tail[None, :], 0.0, -1e30).astype(f32)
    info = jnp.stack([me, side, shift, dp * lax.axis_size("fsdp") + me]).astype(jnp.int32)

    qkv_parts = gather_weight(w_qkv, side)
    vectors = jnp.stack([gain_one, shift_one, gain_two, shift_two])
    gain_a, shift_a, gain_b, shift_b = gather_vectors(vectors, me)
    out_parts = gather_weight(w_out, side)
    gate_parts = gather_weight(w_gate, side)
    up_parts = gather_weight(w_up, side)
    down_parts = gather_weight(w_down, side)

    rolled, tokens_turned = roll_tokens(info, tokens)
    joined, full_qkv = project_qkv(info, rolled, cosine, sine, qkv_parts)
    attended, logs = attend(info, joined, bias)
    normed_one, root_one, attended_turned, full_out = add_branch(info, attended, rolled, out_parts)
    inner, gate, up, hidden_turned, full_gate, full_up = gate_and_up(
        info, normed_one, gain_a, shift_a, gate_parts, up_parts
    )
    output, normed_two, root_two, pooled, embedding, full_down = down_and_pool(
        info, inner, normed_one, gain_a, shift_a, gain_b, shift_b, member, sizes, down_parts
    )
    everyone = gather_blocks(embedding).reshape(-1, width)
    output = unroll(info, output)

    loss, grad_second, grad_feed, vectors_two = loss_and_norm(
        info, everyone, pooled, embedding, sizes, member, normed_two, root_two, gain_b
    )
    order.done(grad_feed)
    down_theirs = down_gradient(info, inner, grad_feed, (3, 1), "down_theirs")
    down = None
    order.done(down_theirs)
    down_own = down_gradient(info, order.after(inner), grad_feed, (2, 0), "down_own")
    order.done(down_own)
    down = reduce_steps(order, down_theirs, down_own)
    next(down)
    next(down)
    feed = (info, grad_feed, hidden_turned, gate, up, full_down, full_gate, full_up)
    steps = gate.shape[1] // FEED_TILE
    early = steps // 3

    def rows_of(pieces):
        return pieces.reshape(2, -1, pieces.shape[-1])

    feed = (info, order.after(grad_feed)) + feed[2:]
    theirs, own, grad_hidden = feed_back(*feed, 0, early, None)
    order.done(grad_hidden)
    first_units = reduce_steps(order, rows_of(theirs), rows_of(own))
    next(first_units)
    feed = (info, order.after(grad_feed)) + feed[2:]
    theirs, own, grad_hidden = feed_back(*feed, early, steps - early, grad_hidden)
    order.done(grad_hidden)
    later_units = reduce_steps(order, rows_of(theirs), rows_of(own))
    next(first_units)
    next(later_units)
    grad_first, grad_attended, out_theirs, out_own, vectors_one = first_back(
        info, order.after(grad_hidden), grad_second, normed_one, root_one, gain_a, attended_turned, full_out
    )
    order.done(grad_attended)
    out = reduce_steps(order, out_theirs, out_own)
    vectors = sum_steps(jnp.concatenate([vectors_one[:2], vectors_two[:2]]))
    next(out)
    next(vectors)
    next(later_units)
    next(out)
    next(vectors)
    next(down)
    grad_query, grad_key, grad_value = attend_back(
        info, joined, attended, order.after(grad_attended), logs, bias, cosine, sine
    )
    order.done(grad_query)
    next(down)
    next(first_units)
    pieces = [
        weight_gradient(info, tokens_turned, order.after(grad), name)
        for grad, name in ((grad_query, "query"), (grad_key, "key"), (grad_value, "value"))
    ]
    query_key = reduce_steps(
        order,
        jnp.concatenate([pieces[0][0], pieces[1][0]], axis=1),
        jnp.concatenate([pieces[0][1], pieces[1][1]], axis=1),
    )
    value = reduce_steps(order, *pieces[2])
    grad_tokens = tokens_gradient(info, grad_first, grad_query, grad_key, grad_value, full_qkv)

    running = {
        "down": down, "first": first_units, "later": later_units, "out": out,
        "query_key": query_key, "value": value, "vectors": vectors,
    }
    results = {}
    turns = ["query_key", "value", "query_key", "value"]
    while len(results) < len(running):
        for name in turns or list(running):
            if name in results:
                continue
            result = next(running[name])
            if result is not None:
                results[name] = result
        turns = None

    early_columns = early * FEED_TILE
    quarter = width // 4
    first = results["first"].reshape(2, quarter, early_columns)
    later = results["later"].reshape(2, quarter, -1)
    grad_gate = jnp.concatenate([first[0], later[0]], axis=1)
    grad_up = jnp.concatenate([first[1], later[1]], axis=1)
    pair = results["query_key"].reshape(2, quarter, width)
    grad_qkv = jnp.concatenate([pair[0], pair[1], results["value"]], axis=1)
    sums = lax.dynamic_slice_in_dim(results["vectors"], me * quarter, quarter, 1)
    return (
        loss[0, 0],
        output,
        grad_tokens,
        grad_qkv,
        results["out"],
        grad_gate,
        grad_up,
        results["down"],
        sums[0],
        sums[1],
        sums[2],
        sums[3],
    )


def solution(mesh):
    placed = (
        P(("dp", "fsdp"), None),
        P(("dp", "fsdp"), None),
        P("fsdp", None),
        P("fsdp", None),
        P("fsdp", None),
        P("fsdp", None),
        P("fsdp", None),
        P("fsdp"),
        P("fsdp"),
        P("fsdp"),
        P("fsdp"),
    )
    return jax.shard_map(
        per_device,
        mesh=mesh,
        in_specs=placed,
        out_specs=(
            P(),
            P(("dp", "fsdp"), None),
            P(("dp", "fsdp"), None),
            P("fsdp", None),
            P("fsdp", None),
            P("fsdp", None),
            P("fsdp", None),
            P("fsdp", None),
            P("fsdp"),
            P("fsdp"),
            P("fsdp"),
            P("fsdp"),
        ),
        check_vma=False,
    )
```

```python
import functools

import jax
import jax.numpy as jnp
from jax import lax
from jax.experimental import pallas as pl
from jax.experimental.pallas import tpu as pltpu
from jax.sharding import PartitionSpec as P

HD = 64
PAIRS = 4
LONG = 768
LANES = 128
FEED_TILE = 512
SPARE_ROWS = 64
exact_arithmetic = lax.Precision.HIGHEST
eps_norm = 1e-05
eps_embed = 1e-06
logit_divisor = 0.05
rope_base = 1000.0
log2_e = 1.4426950408889634
f32 = jnp.float32
bf16 = jnp.bfloat16
HBM = pl.BlockSpec(memory_space=pl.ANY)


def call(body, out_shapes, *, grid, in_specs, out_specs, scratch=(), vmem, name):
    return pl.pallas_call(
        body,
        out_shape=out_shapes,
        grid_spec=pltpu.PrefetchScalarGridSpec(
            num_scalar_prefetch=1,
            grid=grid,
            in_specs=in_specs,
            out_specs=out_specs,
            scratch_shapes=list(scratch),
        ),
        compiler_params=pltpu.CompilerParams(vmem_limit_bytes=vmem * 1024 * 1024),
        cost_estimate=pl.CostEstimate(flops=10**11, bytes_accessed=10**8, transcendentals=0),
        name=name,
    )


def whole(shape):
    return pl.BlockSpec(shape, lambda *_: (0,) * len(shape))


def shaped(shape, dtype):
    return pltpu.HBM(shape, dtype)


def close(shape, dtype):
    return jax.ShapeDtypeStruct(shape, dtype)


def pinned(*values):
    return [pltpu.with_memory_space_constraint(value, pltpu.HBM) for value in values]


def matmul(left, right, left_dim=1, right_dim=0, precision=None):
    return lax.dot_general(
        left,
        right,
        (((left_dim,), (right_dim,)), ((), ())),
        precision=precision,
        preferred_element_type=f32,
    )


def start_weight(info, parts, full, sem, columns, each=False):
    for (other, cut, block, base), piece in parts:
        rows = piece.shape[0]
        start = (info[0] ^ other) * (rows * cut)
        if block is not None:
            start = start + block(info) * rows
        target = full.at[pl.ds(pl.multiple_of(start, 16), rows), columns]
        source = piece.at[:, pl.ds(base + columns.start, columns.size)]
        pltpu.make_async_copy(source, target, sem.at[other] if each else sem).start()


def wait_weight(full, sem, columns):
    pltpu.make_async_copy(full.at[:, columns], full.at[:, columns], sem).wait()


def turn_rows(info, turned, target):
    count = turned.shape[0] // 4
    for k in range(4):
        start = pl.multiple_of((info[0] ^ k) * count, 32)
        target[k] = turned[pl.ds(start, count), :]


def sigmoid(value):
    return 0.5 * jnp.tanh(0.5 * value) + 0.5


def roll_body(info, tokens, rolled, turned, scratch):
    count, width = tokens.shape
    shift = lax.rem(count - info[2], count)
    for first in range(0, width, LANES):
        lanes = pl.ds(first, LANES)
        moved = pltpu.roll(tokens[:, lanes].astype(f32), shift, 0).astype(bf16)
        rolled[:, lanes] = moved
        scratch[pl.ds(first, LANES), :] = moved.T
    turn_rows(info, scratch, turned)


def roll_tokens(info, tokens):
    count, width = tokens.shape
    return call(
        roll_body,
        (close(tokens.shape, bf16), shaped((4, width // 4, count), bf16)),
        grid=(1,),
        in_specs=[whole(tokens.shape)],
        out_specs=(whole(tokens.shape), whole((4, width // 4, count))),
        scratch=[pltpu.VMEM((width, count), bf16)],
        vmem=12,
        name="roll_tokens",
    )(info, tokens)


def unroll_body(info, value, moved):
    count = value.shape[0]
    for first in range(0, value.shape[1], LANES):
        lanes = pl.ds(first, LANES)
        moved[:, lanes] = pltpu.roll(value[:, lanes].astype(f32), info[2], 0).astype(moved.dtype)


def unroll(info, value):
    count, width = value.shape
    tile = 256
    spec = pl.BlockSpec((count, tile), lambda i, *_: (0, i))
    return call(
        unroll_body,
        shaped(value.shape, value.dtype),
        grid=(width // tile,),
        in_specs=[spec],
        out_specs=spec,
        vmem=8,
        name="unroll",
    )(info, value)


def rope_lanes(value, cosine, signed_sine):
    lane = lax.broadcasted_iota(jnp.int32, (value.shape[0], LANES), 1)
    first_half = (lane & 32) == 0
    out = []
    for start in range(0, value.shape[1], LANES):
        piece = value[:, start : start + LANES]
        partner = jnp.where(first_half, pltpu.roll(piece, LANES - 32, 1), pltpu.roll(piece, 32, 1))
        out.append(piece * cosine + partner * signed_sine)
    return out[0] if len(out) == 1 else jnp.concatenate(out, axis=1)


def qkv_body(layout, info, rolled, cosine, signed_sine, *rest):
    parts = list(zip(layout, rest))
    joined, kept, full, sems, keep_sem = rest[len(layout) :]
    step = pl.program_id(0)
    steps = pl.num_programs(0)
    tile = joined.shape[1]

    @pl.when(step == 0)
    def _():
        for j in range(full.shape[1] // tile):
            start_weight(info, parts, full, sems.at[j], pl.ds(j * tile, tile))

    columns = pl.ds(pl.multiple_of(step * tile, tile), tile)
    wait_weight(full, sems.at[step], columns)
    pltpu.make_async_copy(full.at[:, columns], kept.at[:, columns], keep_sem.at[step]).start()
    chunk = 512

    @pl.when(step < 2 * steps // 3)
    def _():
        for first in range(0, joined.shape[0], chunk):
            rows = pl.ds(first, chunk)
            product = matmul(rolled[rows, :], full[:, columns])
            turned = rope_lanes(product, cosine[rows, :], signed_sine[rows, :])
            joined[rows, :] = turned.astype(bf16)

    @pl.when(step >= 2 * steps // 3)
    def _():
        for first in range(0, joined.shape[0], chunk):
            rows = pl.ds(first, chunk)
            joined[rows, :] = matmul(rolled[rows, :], full[:, columns]).astype(bf16)

    @pl.when(step == steps - 1)
    def _():
        for j in range(full.shape[1] // tile):
            piece = pl.ds(j * tile, tile)
            pltpu.make_async_copy(full.at[:, piece], kept.at[:, piece], keep_sem.at[j]).wait()


def project_qkv(info, rolled, cosine, signed_sine, weight):
    layout, parts = weight
    count, width = rolled.shape
    columns = parts[0].shape[1]
    tile = width
    return call(
        functools.partial(qkv_body, layout),
        (shaped((count, columns), bf16), shaped((width, columns), bf16)),
        grid=(columns // tile,),
        in_specs=[whole(rolled.shape), whole(cosine.shape), whole(cosine.shape)]
        + [HBM] * len(parts),
        out_specs=(pl.BlockSpec((count, tile), lambda i, *_: (0, i)), HBM),
        scratch=[
            pltpu.VMEM((width, columns), bf16),
            pltpu.SemaphoreType.DMA((columns // tile,)),
            pltpu.SemaphoreType.DMA((columns // tile,)),
        ],
        vmem=22,
        name="project_qkv",
    )(info, rolled, cosine, signed_sine, *pinned(*parts))


def attend_body(info, query, key, value, bias, attended, logs):
    pair = pl.program_id(0)
    count = query.shape[0]
    scale = 0.125 * log2_e
    lane = lax.broadcasted_iota(jnp.int32, (1, LANES), 1)

    @pl.when(pair == 0)
    def _():
        logs[...] = jnp.zeros_like(logs)

    def rows_of(first, size, keys, offset):
        rows = pl.ds(first, size)
        ones = jnp.ones((keys.size, LANES), bf16)
        extended = jnp.concatenate([value[keys, :], ones], axis=1)
        picked = []
        kept_logs = logs[rows, :]
        for head in range(2):
            mine = (lane >= HD) if head else (lane < HD)
            masked = jnp.where(mine, query[rows, :], jnp.zeros((), bf16))
            scores = matmul(masked, key[keys, :], 1, 1) * scale
            if offset is not None:
                scores = scores + offset
            top = jnp.max(scores, axis=1, keepdims=True)
            terms = jnp.exp2(scores - top).astype(bf16)
            product = matmul(terms, extended)
            total = product[:, LANES:]
            picked.append(product[:, :LANES] / total)
            kept_logs = jnp.where(lane == 2 * pair + head, top + jnp.log2(total), kept_logs)
        attended[rows, :] = jnp.where(lane < HD, picked[0], picked[1]).astype(bf16)
        logs[rows, :] = kept_logs

    for first in range(0, LONG, 256):
        rows_of(first, 256, pl.ds(0, LONG), None)
    rest = count - LONG
    rows_of(LONG, rest, pl.ds(LONG, rest), bias[...])


def attend(info, joined, bias):
    count, columns = joined.shape
    width = columns // 3
    pairs = width // LANES
    specs = [pl.BlockSpec((count, LANES), lambda i, *_, n=n: (0, n * pairs + i)) for n in range(3)]
    return call(
        attend_body,
        (close((count, width), bf16), shaped((count, LANES), f32)),
        grid=(pairs,),
        in_specs=specs + [whole(bias.shape)],
        out_specs=(pl.BlockSpec((count, LANES), lambda i, *_: (0, i)), whole((count, LANES))),
        vmem=16,
        name="attend",
    )(info, *pinned(joined, joined, joined), bias)


def norm_parts(value):
    centered = value - jnp.mean(value, axis=1, keepdims=True)
    root = lax.rsqrt(jnp.mean(centered * centered, axis=1, keepdims=True) + eps_norm)
    return centered * root, root


def branch_body(layout, info, attended, rolled, *rest):
    parts = list(zip(layout, rest))
    normed, root, turned, kept, full, scratch, sem, keep_sem = rest[len(layout) :]
    step = pl.program_id(0)

    @pl.when(step == 0)
    def _():
        start_weight(info, parts, full, sem, pl.ds(0, full.shape[1]))
        wait_weight(full, sem, pl.ds(0, full.shape[1]))
        pltpu.make_async_copy(full, kept, keep_sem).start()

    first = rolled[...].astype(f32) + matmul(attended[...], full[...])
    value, inverse = norm_parts(first)
    normed[...] = value
    root[...] = jnp.broadcast_to(inverse, root.shape)
    scratch[...] = attended[...].T
    turn_rows(info, scratch, turned)

    @pl.when(step == pl.num_programs(0) - 1)
    def _():
        pltpu.make_async_copy(full, kept, keep_sem).wait()


def add_branch(info, attended, rolled, weight):
    layout, parts = weight
    count, width = attended.shape
    tile = 256
    rows = pl.BlockSpec((tile, width), lambda i, *_: (i, 0))
    return call(
        functools.partial(branch_body, layout),
        (
            shaped((count, width), f32),
            shaped((count, LANES), f32),
            shaped((4, width // 4, count), bf16),
            shaped((width, width), bf16),
        ),
        grid=(count // tile,),
        in_specs=[rows, rows] + [HBM] * len(parts),
        out_specs=(
            rows,
            pl.BlockSpec((tile, LANES), lambda i, *_: (i, 0)),
            pl.BlockSpec((4, width // 4, tile), lambda i, *_: (0, 0, i)),
            HBM,
        ),
        scratch=[
            pltpu.VMEM((width, width), bf16),
            pltpu.VMEM((width, tile), bf16),
            pltpu.SemaphoreType.DMA,
            pltpu.SemaphoreType.DMA,
        ],
        vmem=14,
        name="add_branch",
    )(info, *pinned(attended, rolled, *parts))


def gate_body(layout, info, normed, gain, shift, *rest):
    parts = list(zip(layout, rest))
    gate, hidden, turned, kept, full, low, scratch, sems, keep_sems = rest[len(layout) :]
    step = pl.program_id(0)
    tile = gate.shape[1]
    tiles = full.shape[1] // tile
    chunk = 512

    @pl.when(step == 0)
    def _():
        for j in range(tiles):
            start_weight(info, parts, full, sems.at[j], pl.ds(j * tile, tile))
        for first in range(0, low.shape[0], chunk):
            rows = pl.ds(first, chunk)
            value = (normed[rows, :] * gain[...] + shift[...]).astype(bf16)
            low[rows, :] = value
            scratch[:, rows] = value.T
        hidden[...] = low[...]
        turn_rows(info, scratch, turned)

    columns = pl.ds(pl.multiple_of(step * tile, tile), tile)
    wait_weight(full, sems.at[step], columns)
    pltpu.make_async_copy(full.at[:, columns], kept.at[:, columns], keep_sems.at[step]).start()
    for first in range(0, low.shape[0], chunk):
        rows = pl.ds(first, chunk)
        gate[rows, :] = matmul(low[rows, :], full[:, columns]).astype(bf16)

    @pl.when(step == tiles - 1)
    def _():
        for j in range(tiles):
            piece = pl.ds(j * tile, tile)
            pltpu.make_async_copy(full.at[:, piece], kept.at[:, piece], keep_sems.at[j]).wait()


def project_gate(info, normed, gain, shift, weight):
    layout, parts = weight
    count, width = normed.shape
    hidden = parts[0].shape[1]
    tile = 512
    columns = pl.BlockSpec((count, tile), lambda i, *_: (0, i))
    return call(
        functools.partial(gate_body, layout),
        (
            shaped((count, hidden), bf16),
            close((count, width), bf16),
            shaped((4, width // 4, count), bf16),
            shaped((width, hidden), bf16),
        ),
        grid=(hidden // tile,),
        in_specs=[whole(normed.shape), whole(gain.shape), whole(shift.shape)]
        + [HBM] * len(layout),
        out_specs=(columns, whole((count, width)), whole((4, width // 4, count)), HBM),
        scratch=[
            pltpu.VMEM((width, hidden), bf16),
            pltpu.VMEM((count, width), bf16),
            pltpu.VMEM((width, count), bf16),
            pltpu.SemaphoreType.DMA((hidden // tile,)),
            pltpu.SemaphoreType.DMA((hidden // tile,)),
        ],
        vmem=26,
        name="project_gate",
    )(info, *pinned(normed), gain, shift, *pinned(*parts))


def up_body(layout, info, low, gate, *rest):
    parts = list(zip(layout, rest))
    inner, up_out, kept, full, sems, keep_sems = rest[len(layout) :]
    step = pl.program_id(0)
    tile = inner.shape[1]
    tiles = full.shape[1] // tile
    chunk = 512

    @pl.when(step == 0)
    def _():
        for j in range(tiles):
            start_weight(info, parts, full, sems.at[j], pl.ds(j * tile, tile))

    columns = pl.ds(pl.multiple_of(step * tile, tile), tile)
    wait_weight(full, sems.at[step], columns)
    pltpu.make_async_copy(full.at[:, columns], kept.at[:, columns], keep_sems.at[step]).start()
    for first in range(0, low.shape[0], chunk):
        rows = pl.ds(first, chunk)
        up = matmul(low[rows, :], full[:, columns])
        up_out[rows, :] = up.astype(bf16)
        value = gate[rows, :].astype(f32)
        inner[rows, :] = (value * up * sigmoid(value)).astype(bf16)

    @pl.when(step == tiles - 1)
    def _():
        for j in range(tiles):
            piece = pl.ds(j * tile, tile)
            pltpu.make_async_copy(full.at[:, piece], kept.at[:, piece], keep_sems.at[j]).wait()


def project_up(info, low, gate, weight):
    layout, parts = weight
    count, width = low.shape
    hidden = parts[0].shape[1]
    tile = 512
    columns = pl.BlockSpec((count, tile), lambda i, *_: (0, i))
    return call(
        functools.partial(up_body, layout),
        (
            shaped((count, hidden), bf16),
            shaped((count, hidden), bf16),
            shaped((width, hidden), bf16),
        ),
        grid=(hidden // tile,),
        in_specs=[whole(low.shape), columns] + [HBM] * len(layout),
        out_specs=(columns, columns, HBM),
        scratch=[
            pltpu.VMEM((width, hidden), bf16),
            pltpu.SemaphoreType.DMA((hidden // tile,)),
            pltpu.SemaphoreType.DMA((hidden // tile,)),
        ],
        vmem=24,
        name="project_up",
    )(info, low, *pinned(gate, *parts))


def down_body(layout, info, inner, normed, gain_one, shift_one, gain, shift, member, sizes, *rest):
    parts = list(zip(layout, rest))
    output, normed_two, root, pooled, embedding, kept, full, feed, sems, keep_sem = rest[len(layout) :]
    step = pl.program_id(0)
    steps = pl.num_programs(0)
    tile = output.shape[0]
    quarter = full.shape[0] // 4

    @pl.when(step == 0)
    def _():
        start_weight(info, parts, full, sems, pl.ds(0, full.shape[1]), each=True)
        pooled[...] = jnp.zeros_like(pooled)
        for other in range(4):
            rows = pl.ds(pl.multiple_of((info[0] ^ other) * quarter, quarter), quarter)
            pltpu.make_async_copy(full.at[rows, :], full.at[rows, :], sems.at[other]).wait()
            product = matmul(inner[:, rows], full[rows, :])
            feed[...] = product if other == 0 else feed[...] + product
        pltpu.make_async_copy(full, kept, keep_sem).start()

    @pl.when(step > 0)
    def _():
        feed[...] = matmul(inner[...], full[...])

    hidden = normed[...] * gain_one[...] + shift_one[...]
    value, inverse = norm_parts(hidden + feed[...])
    normed_two[...] = value
    root[...] = jnp.broadcast_to(inverse, root.shape)
    result = value * gain[...] + shift[...]
    output[...] = result.astype(bf16)

    @pl.when(step < LONG // tile)
    def _():
        pooled[0:1, :] += jnp.sum(result, axis=0, keepdims=True)

    @pl.when(step == steps - 1)
    def _():
        longest = jnp.where(sizes[...] == LONG, pooled[0:1, :], 0.0)
        total = (longest + matmul(member[...], result, 0, 0, exact_arithmetic)) / sizes[...]
        pooled[...] = total
        square = jnp.sum(total * total, axis=1, keepdims=True)
        embedding[...] = total * lax.rsqrt(square + eps_embed)
        pltpu.make_async_copy(full, kept, keep_sem).wait()


def down_and_pool(info, inner, normed, gain_one, shift_one, gain, shift, member, sizes, weight):
    layout, parts = weight
    count, width = normed.shape
    hidden = inner.shape[1]
    seqs = member.shape[1]
    tile = 256
    rows = pl.BlockSpec((tile, width), lambda i, *_: (i, 0))
    vector = whole((1, width))
    return call(
        functools.partial(down_body, layout),
        (
            shaped((count, width), bf16),
            shaped((count, width), f32),
            shaped((count, LANES), f32),
            close((seqs, width), f32),
            close((seqs, width), f32),
            shaped((hidden, width), bf16),
        ),
        grid=(count // tile,),
        in_specs=[
            pl.BlockSpec((tile, hidden), lambda i, *_: (i, 0)),
            rows,
            vector,
            vector,
            vector,
            vector,
            pl.BlockSpec((tile, seqs), lambda i, *_: (LONG // tile, 0)),
            whole(sizes.shape),
        ]
        + [HBM] * len(parts),
        out_specs=(
            rows,
            rows,
            pl.BlockSpec((tile, LANES), lambda i, *_: (i, 0)),
            whole((seqs, width)),
            whole((seqs, width)),
            HBM,
        ),
        scratch=[
            pltpu.VMEM((hidden, width), bf16),
            pltpu.VMEM((tile, width), f32),
            pltpu.SemaphoreType.DMA((4,)),
            pltpu.SemaphoreType.DMA,
        ],
        vmem=24,
        name="down_and_pool",
    )(info, *pinned(inner, normed), gain_one, shift_one, gain, shift, member, sizes, *pinned(*parts))


def loss_body(info, everyone, pooled, embedding, sizes, member, normed, root, gain, *rest):
    loss, grad_second, grad_feed, vectors, pulled, upstreams = rest
    step = pl.program_id(0)
    seqs, width = embedding.shape
    pairs = seqs // 2

    @pl.when(step == 0)
    def _():
        devices = everyone.shape[0] // seqs
        count = devices * pairs
        blocks = everyone[...].reshape(devices, seqs, width)
        requests = blocks[:, :pairs].reshape(count, width)
        passages = blocks[:, pairs:].reshape(count, width)
        sims = matmul(requests, passages, 1, 1, exact_arithmetic) * (1.0 / logit_divisor)
        top = jnp.max(sims, axis=1, keepdims=True)
        terms = jnp.exp(sims - top)
        total = jnp.sum(terms, axis=1, keepdims=True)
        row = lax.broadcasted_iota(jnp.int32, sims.shape, 0)
        column = lax.broadcasted_iota(jnp.int32, sims.shape, 1)
        diagonal = jnp.sum(jnp.where(row == column, sims, 0.0), axis=1, keepdims=True)
        mean = jnp.sum(top + jnp.log(total) - diagonal, axis=0, keepdims=True) / count
        loss[...] = jnp.broadcast_to(mean, loss.shape)
        pulls = terms / total
        first = info[3] * pairs
        near = lax.broadcasted_iota(jnp.int32, (seqs, count), 0)
        place = lax.broadcasted_iota(jnp.int32, (seqs, count), 1)
        picked = jnp.where(place == first + near, 1.0, 0.0)
        my_rows = matmul(picked, pulls, 1, 0, exact_arithmetic)
        my_columns = matmul(picked, pulls, 1, 1, exact_arithmetic)
        to_requests = matmul(my_rows, passages, 1, 0, exact_arithmetic)
        to_passages = matmul(my_columns, requests, 1, 0, exact_arithmetic)
        own = embedding[...]
        swapped = jnp.concatenate([own[pairs:], own[:pairs]], axis=0)
        gathered = jnp.concatenate([to_requests[:pairs], to_passages[:pairs]], axis=0)
        grad_embed = (gathered - swapped) * (1.0 / (logit_divisor * count))
        means = pooled[...]
        inverse = lax.rsqrt(jnp.sum(means * means, axis=1, keepdims=True) + eps_embed)
        along = jnp.sum(means * grad_embed, axis=1, keepdims=True)
        pulled[...] = (inverse * grad_embed - inverse * inverse * inverse * means * along) / sizes[
            ...
        ]
        vectors[...] = jnp.zeros_like(vectors)

    @pl.when(step < LONG // normed.shape[0])
    def _():
        longest = jnp.sum(jnp.where(sizes[...] == LONG, pulled[...], 0.0), axis=0, keepdims=True)
        upstreams[...] = jnp.broadcast_to(longest, upstreams.shape)

    @pl.when(step >= LONG // normed.shape[0])
    def _():
        upstreams[...] = matmul(member[...], pulled[...], 1, 0, exact_arithmetic)

    upstream = upstreams[...]
    value = normed[...]
    vectors[0:1, :] += jnp.sum(upstream * value, axis=0, keepdims=True)
    vectors[1:2, :] += jnp.sum(upstream, axis=0, keepdims=True)
    result = norm_back(upstream, value, root[:, :1], gain[...])
    grad_second[...] = result
    grad_feed[...] = result.astype(bf16)


def norm_back(upstream, normed, root, gain):
    scaled = upstream * gain
    return root * (
        scaled
        - jnp.mean(scaled, axis=1, keepdims=True)
        - normed * jnp.mean(scaled * normed, axis=1, keepdims=True)
    )


def loss_and_norm(info, everyone, pooled, embedding, sizes, member, normed, root, gain):
    count, width = normed.shape
    seqs = member.shape[1]
    tile = 256
    rows = pl.BlockSpec((tile, width), lambda i, *_: (i, 0))
    return call(
        loss_body,
        (
            close((8, LANES), f32),
            shaped((count, width), f32),
            close((count, width), bf16),
            close((8, width), f32),
        ),
        grid=(count // tile,),
        in_specs=[
            whole(everyone.shape),
            whole(pooled.shape),
            whole(embedding.shape),
            whole(sizes.shape),
            pl.BlockSpec((tile, seqs), lambda i, *_: (i, 0)),
            rows,
            pl.BlockSpec((tile, LANES), lambda i, *_: (i, 0)),
            whole(gain.shape),
        ],
        out_specs=(whole((8, LANES)), rows, rows, whole((8, width))),
        scratch=[pltpu.VMEM((seqs, width), f32), pltpu.VMEM((tile, width), f32)],
        vmem=16 + everyone.shape[0] * width * 24 // 2**20,
        name="loss_and_norm",
    )(info, everyone, pooled, embedding, sizes, member, *pinned(normed, root), gain)


def outer_body(theirs, info, left, right, *outs):
    step = pl.program_id(0)
    product = matmul(left[...], right[...], 0, 0).astype(bf16)
    rows = product.shape[0] // 8
    for block in range(8):
        source = slice(block * rows, (block + 1) * rows)
        target = pl.ds(pl.multiple_of(relative_block(info, block) * rows, 16), rows)
        if theirs:
            outs[0][0, target, :] = product[source]
            continue
        for index, out in enumerate(outs):

            @pl.when(step == index)
            def _():
                out[target, :] = product[source]


def down_gradient(info, inner, grad_feed, theirs):
    count, hidden = inner.shape
    width = grad_feed.shape[1]
    rows = hidden // 4
    first, last = (3, 1) if theirs else (2, 0)

    def column(i, info):
        return (0, info[0] ^ jnp.where(i == 0, first, last))

    if theirs:
        outs = (shaped((2, rows, width), bf16),)
        specs = (pl.BlockSpec((1, rows, width), lambda i, *_: (i, 0, 0)),)
    else:
        outs = (shaped((rows, width), bf16),) * 2
        specs = (whole((rows, width)),) * 2
    return call(
        functools.partial(outer_body, theirs),
        outs,
        grid=(2,),
        in_specs=[pl.BlockSpec((count, rows), column), whole(grad_feed.shape)],
        out_specs=specs,
        vmem=20,
        name="down_theirs" if theirs else "down_own",
    )(info, *pinned(inner), grad_feed)


def piece_shapes(rows, columns):
    own = shaped((rows, columns), bf16)
    return shaped((2, rows, columns), bf16), own, own


def piece_specs(rows, tile):
    own = pl.BlockSpec((rows, tile), lambda i, *_: (0, i))
    return pl.BlockSpec((2, rows, tile), lambda i, *_: (0, 0, i)), own, own


def relative_block(info, block):
    place = block ^ info[5]
    return ((place & 1) << 2) | (place & 2) | (place >> 2)


def multiply_into(held, turned, grads, first):
    _, quarter, count = turned.shape
    grad = grads[0] if len(grads) == 1 else jnp.concatenate(grads, axis=1)
    products = matmul(turned[...].reshape(4 * quarter, count), grad).astype(bf16)
    width = held.shape[2]
    for index in range(len(grads)):
        rows = pl.ds((first + index) * quarter, quarter)
        for place in range(4):
            part = slice(place * quarter, (place + 1) * quarter)
            held[place, rows, :] = products[part, index * width : (index + 1) * width]


def write_pieces(info, held, theirs, far, near):
    rows = held.shape[1] // 8
    for block in range(8):
        source = slice(block * rows, (block + 1) * rows)
        target = pl.ds(pl.multiple_of(relative_block(info, block) * rows, 16), rows)
        near[target, :] = held[0, source, :]
        theirs[1, target, :] = held[1, source, :]
        far[target, :] = held[2, source, :]
        theirs[0, target, :] = held[3, source, :]


def feed_body(info, grad_feed, turned, gate_in, up_in, down, gate_full, up_full, held, *outs):
    *pieces, grad_hidden, products = outs
    step = pl.program_id(0)
    count = grad_feed.shape[0]
    chunk = 512
    gates, ups = [], []

    @pl.when(step == 0)
    def _():
        grad_hidden[...] = held[...]

    for first in range(0, count, chunk):
        rows = pl.ds(first, chunk)
        grad_inner = matmul(grad_feed[rows, :], down[...], 1, 1)
        gate = gate_in[rows, :].astype(f32)
        up = up_in[rows, :].astype(f32)
        share = sigmoid(gate)
        scaled = grad_inner * share
        grad_gate = (scaled * up * (1.0 + gate * (1.0 - share))).astype(bf16)
        grad_up = (scaled * gate).astype(bf16)
        gates.append(grad_gate)
        ups.append(grad_up)
        grad_hidden[rows, :] += matmul(grad_gate, gate_full[...], 1, 1) + matmul(
            grad_up, up_full[...], 1, 1
        )
    for which, grads in ((0, gates), (1, ups)):
        multiply_into(products, turned, [jnp.concatenate(grads, axis=0)], which)
    write_pieces(info, products, *pieces)


def feed_back(info, grad_feed, turned, gate, up, down, gate_full, up_full, base, steps, held):
    count = gate.shape[0]
    width = grad_feed.shape[1]
    quarter = width // 4
    tile = FEED_TILE
    share = steps * tile
    columns = pl.BlockSpec((count, tile), lambda i, *_: (0, base + i))
    weights = pl.BlockSpec((width, tile), lambda i, *_: (0, base + i))
    in_specs = [
        whole(grad_feed.shape),
        whole(turned.shape),
        columns,
        columns,
        pl.BlockSpec((tile, width), lambda i, *_: (base + i, 0)),
        weights,
        weights,
    ]
    in_specs.append(whole(held.shape))
    args = [grad_feed, turned, *pinned(gate, up, down, gate_full, up_full, held)]
    return call(
        feed_body,
        piece_shapes(2 * quarter, share) + (shaped((count, width), f32),),
        grid=(steps,),
        in_specs=in_specs,
        out_specs=piece_specs(2 * quarter, tile) + (whole((count, width)),),
        scratch=[pltpu.VMEM((4, 2 * quarter, tile), bf16)],
        vmem=40,
        name=f"feed_back_{base}",
    )(info, *args)


def first_body(info, grad_hidden, normed, root, gain, weight, *outs):
    grad_first, branch, grad_attended, vectors = outs

    @pl.when(pl.program_id(0) == 0)
    def _():
        vectors[...] = jnp.zeros_like(vectors)

    upstream = grad_hidden[...]
    value = normed[...]
    vectors[0:1, :] += jnp.sum(upstream * value, axis=0, keepdims=True)
    vectors[1:2, :] += jnp.sum(upstream, axis=0, keepdims=True)
    result = norm_back(upstream, value, root[:, :1], gain[...])
    grad_first[...] = result
    low = result.astype(bf16)
    branch[...] = low
    grad_attended[...] = matmul(low, weight[...], 1, 1).astype(bf16)


def first_back(info, grad_hidden, normed, root, gain, weight):
    count, width = normed.shape
    tile = 256
    rows = pl.BlockSpec((tile, width), lambda i, *_: (i, 0))
    return call(
        first_body,
        (
            shaped((count, width), f32),
            shaped((count, width), bf16),
            shaped((count, width), bf16),
            close((8, width), f32),
        ),
        grid=(count // tile,),
        in_specs=[
            rows,
            rows,
            pl.BlockSpec((tile, LANES), lambda i, *_: (i, 0)),
            whole(gain.shape),
            whole(weight.shape),
        ],
        out_specs=(rows, rows, rows, whole((8, width))),
        vmem=20,
        name="first_back",
    )(info, *pinned(grad_hidden, normed, root), gain, weight)


def attend_back_body(base, info, query, key, value, attended, upstream, logs, bias, cosine, sine, *rest):
    (grad_query, grad_key, grad_value, logs_row, sums) = rest
    pair = base + pl.program_id(0)
    count = query.shape[0]
    scale = 0.125 * log2_e
    lane = lax.broadcasted_iota(jnp.int32, (1, LANES), 1)

    @pl.when(pl.program_id(0) == 0)
    def _():
        logs_row[...] = logs[...].T

    both = upstream[...].astype(f32) * attended[...].astype(f32)
    row = lax.broadcasted_iota(jnp.int32, (8, LANES), 0)
    column = lax.broadcasted_iota(jnp.int32, (8, LANES), 1)
    chooser = jnp.where((column // HD) == row, 1.0, 0.0)
    sums[...] = matmul(chooser, both, 1, 1, exact_arithmetic)

    zero = jnp.zeros((), bf16)
    for first, size, offset in ((0, LONG, None), (LONG, count - LONG, bias)):
        rows = pl.ds(first, size)
        key_rows, query_rows, up_rows = key[rows, :], query[rows, :], upstream[rows, :]
        key_grad = value_grad = query_grad = None
        for head in range(2):
            mine = (lane >= HD) if head else (lane < HD)
            masked_query = jnp.where(mine, query_rows, zero)
            masked_up = jnp.where(mine, up_rows, zero)
            masked_key = jnp.where(mine, key_rows, zero)
            log_row = logs_row[pl.ds(2 * pair + head, 1), rows]
            sum_row = sums[head : head + 1, rows]
            key_pieces, value_pieces = [], []
            query_total = None
            for start in range(first, first + size, 256):
                keys = pl.ds(start, 256)
                scores = matmul(key[keys, :], masked_query, 1, 1) * scale
                if offset is not None:
                    scores = scores + offset[...]
                probs = jnp.exp2(scores - log_row)
                grad_probs = matmul(value[keys, :], masked_up, 1, 1)
                grad_scores = (probs * (grad_probs - sum_row)).astype(bf16)
                value_pieces.append(matmul(probs.astype(bf16), masked_up))
                key_pieces.append(matmul(grad_scores, masked_query))
                kept_key = masked_key[start - first : start - first + 256]
                piece = matmul(grad_scores, kept_key, 0, 0)
                query_total = piece if query_total is None else query_total + piece
            key_head = jnp.concatenate(key_pieces, axis=0)
            value_head = jnp.concatenate(value_pieces, axis=0)
            key_grad = key_head if key_grad is None else key_grad + key_head
            value_grad = value_head if value_grad is None else value_grad + value_head
            query_grad = query_total if query_grad is None else query_grad + query_total
        turn_cos, turn_sin = cosine[rows, :], sine[rows, :]
        for grad, target in ((query_grad, grad_query), (key_grad, grad_key)):
            low = (grad * 0.125).astype(bf16).astype(f32)
            target[rows, :] = rope_lanes(low, turn_cos, -turn_sin).astype(bf16)
        grad_value[rows, :] = value_grad.astype(bf16)


def attend_back(info, joined, attended, upstream, logs, bias, cosine, sine, base, pairs):
    count, columns = joined.shape
    every = columns // 3 // LANES
    specs = [
        pl.BlockSpec((count, LANES), lambda i, *_, n=n: (0, n * every + base + i)) for n in range(3)
    ]
    block = pl.BlockSpec((count, LANES), lambda i, *_: (0, base + i))
    return call(
        functools.partial(attend_back_body, base),
        (close((count, pairs * LANES), bf16),) * 3,
        grid=(pairs,),
        in_specs=specs
        + [block, block, whole(logs.shape), whole(bias.shape)]
        + [whole(cosine.shape)] * 2,
        out_specs=(pl.BlockSpec((count, LANES), lambda i, *_: (0, i)),) * 3,
        scratch=[pltpu.VMEM((LANES, count), f32), pltpu.VMEM((8, count), f32)],
        vmem=32,
        name=f"attend_back_{base}",
    )(info, *pinned(joined, joined, joined, attended, upstream), logs, bias, cosine, sine)


def turned_body(info, turned_a, turned_b, *rest):
    grads, pieces, held = rest[:-4], rest[-4:-1], rest[-1]
    used = len(grads) * turned_a.shape[1]
    spare = held.shape[1] - used
    if len(grads) > 3:
        extra = grads[-1]
        grads = grads[:-1]
        used = len(grads) * turned_a.shape[1]
        held[:, used:, :] = extra[...]
    else:
        held[:, used:, :] = jnp.zeros((4, spare, held.shape[2]), bf16)
    for turned, first, several in ((turned_a, 0, grads[:3]), (turned_b, 3, grads[3:])):
        if several:
            multiply_into(held, turned, [grad[...] for grad in several], first)
    write_pieces(info, held, *pieces)


def weight_gradients(info, turned_a, turned_b, grads, name, branch=None, extra=None):
    _, quarter, count = turned_a.shape
    width = grads[0].shape[1]
    tile = LANES
    specs = [pl.BlockSpec((count, tile), lambda i, *_: (0, i))] * len(grads)
    rows = len(grads) * quarter + SPARE_ROWS
    args = list(grads)
    if branch is not None:
        specs += [
            pl.BlockSpec((count, tile), lambda i, *_, n=n: (0, n * width // tile + i)) for n in range(2)
        ]
        specs.append(pl.BlockSpec((4, SPARE_ROWS, tile), lambda i, *_: (0, 0, i)))
        args += [branch, branch, extra]
        rows += 2 * quarter
    return call(
        turned_body,
        piece_shapes(rows, width),
        grid=(width // tile,),
        in_specs=[whole(turned_a.shape), whole(turned_b.shape)] + specs,
        out_specs=piece_specs(rows, tile),
        scratch=[pltpu.VMEM((4, rows, tile), bf16)],
        vmem=22,
        name=name,
    )(info, *pinned(turned_a, turned_b, *args))


def tokens_body(info, grad_first, weight, *rest):
    grads, out = rest[:-1], rest[-1]
    total = grad_first[...]
    width = grads[0].shape[1]
    for part in range(2):
        for index in range(3):
            first = (2 * index + part) * width
            grad = grads[3 * part + index]
            total = total + matmul(grad[...], weight[:, first : first + width], 1, 1)
    out[...] = pltpu.roll(total, info[2], 0)


def tokens_gradient(info, grad_first, grads, weight):
    count, width = grad_first.shape
    tile = 256
    block = pl.BlockSpec((count, tile), lambda i, *_: (0, i))
    return call(
        tokens_body,
        shaped((count, width), f32),
        grid=(width // tile,),
        in_specs=[block, pl.BlockSpec((tile, weight.shape[1]), lambda i, *_: (i, 0))]
        + [whole(grad.shape) for grad in grads],
        out_specs=block,
        vmem=26,
        name="tokens_gradient",
    )(info, grad_first, weight, *grads)


def settle(info, mine, other, held, target):
    half = mine.shape[0]
    held[:half, :] = mine[...].astype(f32)
    held[half:, :] = other[...].astype(f32)
    rows = half // 4
    for block in range(8):
        source = pl.ds(pl.multiple_of(relative_block(info, block) * rows, 8), rows)
        target[block * rows : (block + 1) * rows, :] = held[source, :]


def finish_body(info, front_a, front_b, back_a, back_b, grad_qkv, grad_out, vectors, *scratch):
    quarter, width = grad_out.shape
    half = width // 2
    front_held, front, back_held, back = scratch
    settle(info, front_a, front_b, front_held, front)
    settle(info, back_a, back_b, back_held, back)
    for index in range(3):
        rows = slice(index * quarter, (index + 1) * quarter)
        grad_qkv[:, index * width : index * width + half] = front[rows, :]
        grad_qkv[:, index * width + half : (index + 1) * width] = back[rows, :]
    grad_out[:, :half] = front[3 * quarter : 4 * quarter, :]
    grad_out[:, half:] = front[4 * quarter : 5 * quarter, :]
    vectors[...] = front[5 * quarter : 5 * quarter + 8, :]


def finish(info, front, back):
    half = front[0].shape[1]
    rows, back_rows = 2 * front[0].shape[0], 2 * back[0].shape[0]
    quarter = (rows - SPARE_ROWS) // 5
    shapes = ((quarter, 6 * half), (quarter, 2 * half), (8, half))
    return call(
        finish_body,
        tuple(close(shape, f32) for shape in shapes),
        grid=(1,),
        in_specs=[whole(value.shape) for value in (*front, *back)],
        out_specs=tuple(whole(shape) for shape in shapes),
        scratch=[pltpu.VMEM((count, half), f32) for count in (rows, rows, back_rows, back_rows)],
        vmem=20,
        name="finish",
    )(info, *front, *back)


def gates_body(info, first_a, first_b, later_a, later_b, grad_gate, grad_up, held, target):
    quarter = grad_gate.shape[0]
    start = 0
    for mine, other in ((first_a, first_b), (later_a, later_b)):
        settle(info, mine, other, held, target)
        columns = slice(start, start + mine.shape[1])
        grad_gate[:, columns] = target[:quarter, :]
        grad_up[:, columns] = target[quarter:, :]
        start += mine.shape[1]


def finish_gates(info, first, later):
    half, columns = first[0].shape
    shape = (half, 2 * columns)
    return call(
        gates_body,
        (shaped(shape, f32),) * 2,
        grid=(1,),
        in_specs=[whole(first[0].shape)] * 4,
        out_specs=(whole(shape),) * 2,
        scratch=[pltpu.VMEM((2 * half, columns), f32)] * 2,
        vmem=28,
        name="finish_gates",
    )(info, *pinned(*first, *later))


def settle_down_body(info, mine, other, grad_down, held):
    settle(info, mine, other, held, grad_down)


def finish_down(info, down):
    half, columns = down[0].shape
    shape = (2 * half, columns)
    return call(
        settle_down_body,
        shaped(shape, f32),
        grid=(1,),
        in_specs=[whole(down[0].shape)] * 2,
        out_specs=whole(shape),
        scratch=[pltpu.VMEM(shape, f32)],
        vmem=16,
        name="finish_down",
    )(info, *pinned(*down))


def swap(value, axis, bit):
    size = lax.axis_size(axis)
    return lax.ppermute(value, axis, [(i, i ^ bit) for i in range(size)])


def choose(value, index):
    return lax.dynamic_index_in_dim(value, index, 0, keepdims=False)


def low_sum(*terms):
    total = terms[0].astype(f32)
    for term in terms[1:]:
        total = total + term.astype(f32)
    return total.astype(bf16)


PLAN = (
    "loss", "down_theirs", "down", "down_own", "down", "feed_first", "first", "unroll", "first",
    "down", "feed_later", "later", "down", "norm", "later", "first", "down", "attend_front",
    "down", "first", "grad_front", "front", "first", "later", "down", "front", "attend_back",
    "front", "down", "first", "later", "grad_back", "back", "front", "first", "later", "back",
    "tokens", "front", "first", "later", "down", "back", "front", "later", "back", "front",
    "first", "back", "later", "front", "back", "front", "back", "finish_down", "later", "back",
    "gates", "front", "back",
)


class Order:
    def __init__(self):
        self.last = ()

    def after(self, *values):
        if self.last:
            values = lax.optimization_barrier((*values, *self.last))[: len(values)]
        return values[0] if len(values) == 1 else values

    def done(self, *values):
        self.last = values


def cut_rows(shard, blocks):
    rows, columns = shard.shape
    return shard.reshape(blocks, rows // blocks, columns)


def lowest(info):
    return info[4]


def not_lowest(info):
    return 1 - info[4]


def second(info):
    return info[1]


def not_second(info):
    return 1 - info[1]


def whole_pieces(base):
    return ((0, 1, None, 0), (1, 1, None, base), (2, 1, None, 0), (3, 1, None, 0))


def half_pieces(base, here, there):
    far = tuple((place, 2, block, 0) for place in (2, 3) for block in (here, there))
    return ((0, 1, None, 0), (1, 1, None, base)) + far


def join_vectors(pieces, me):
    pieces = jnp.stack(pieces)
    full = jnp.concatenate([choose(pieces, me ^ q) for q in range(4)], axis=1)
    return [full[i : i + 1].astype(f32) for i in range(full.shape[0])]


def gather_blocks(block):
    dp_size, fsdp_size = lax.axis_size("dp"), lax.axis_size("fsdp")
    bits = dp_size.bit_length() - 1
    held = block[None]
    for bit in reversed(range(bits)):
        other = swap(held, "dp", 1 << bit)
        low = ((lax.axis_index("dp") >> bit) & 1) == 0
        held = jnp.where(low, jnp.stack([held, other]), jnp.stack([other, held]))
        held = held.reshape((-1,) + block.shape)
    held = held.reshape((2,) * bits + block.shape)
    held = held.transpose(tuple(range(bits))[::-1] + tuple(range(bits, bits + block.ndim)))
    held = held.reshape((dp_size,) + block.shape)
    held = lax.all_gather(held, "fsdp", axis=1)
    return held.reshape((dp_size * fsdp_size,) + block.shape)


def reduce_steps(order, pieces):
    bits = lax.axis_size("dp").bit_length() - 1
    from_core = swap(order.after(pieces[0]), "fsdp", 1)
    yield None
    far, near = pieces[1:]
    far, from_core = order.after(far, from_core)
    total = low_sum(far, from_core[0])
    order.done(total)
    from_far = swap(total, "fsdp", 2)
    yield None
    terms = order.after(near, from_core, from_far)
    terms = [terms[0], terms[1][1], terms[2]]
    rows = near.shape[0]
    for step in range(3):
        rows //= 2
        send = low_sum(*[term[rows : 2 * rows] for term in terms])
        order.done(send)
        other = swap(send, "dp", 1 << step)
        yield None
        terms = list(order.after(near, from_core, from_far, *terms[3:], other))
        terms[1] = terms[1][1]
    held = low_sum(*[term[:rows] for term in terms])
    for step in range(3, bits):
        order.done(held)
        other = swap(held, "dp", 1 << step)
        yield None
        held = low_sum(*order.after(held, other))
    for step in (2, 1, 0):
        order.done(held)
        other = swap(held, "dp", 1 << step)
        yield None
        held, other = order.after(held, other)
        if step:
            held = jnp.concatenate([held, other])
    order.done(held, other)
    yield held, other


def pack_layout(lengths_row, count):
    ends = jnp.cumsum(lengths_row)
    starts = ends - lengths_row
    shift = jnp.sum(jnp.where(lengths_row == LONG, starts, 0))
    places = lax.rem(lax.iota(jnp.int32, count) + shift, count)
    segment = jnp.sum((places[:, None] >= ends[None, :]).astype(jnp.int32), axis=1)
    member = segment[:, None] == lax.iota(jnp.int32, lengths_row.shape[0])[None, :]
    offset = jnp.sum(jnp.where(member, starts[None, :], 0), axis=1)
    return shift, segment, places - offset, member.astype(f32)


def rotary_tables(position):
    lane = lax.iota(jnp.int32, LANES)
    frequency = rope_base ** (-2.0 * (lane % (HD // 2)).astype(f32) / HD)
    angles = position.astype(f32)[:, None] * frequency[None, :]
    sine = jnp.sin(angles)
    return jnp.cos(angles), jnp.where((lane & (HD // 2)) == 0, -sine, sine)


def per_device(
    tokens, lengths, w_qkv, w_out, w_gate, w_up, w_down, gain_one, shift_one, gain_two, shift_two
):
    count, width = tokens.shape
    me = lax.axis_index("fsdp")
    dp = lax.axis_index("dp")
    side = dp & 1
    order = Order()

    shift, segment, position, member = pack_layout(lengths[0], count)
    sizes = lengths[0].astype(f32)[:, None]
    cosine, sine = rotary_tables(position)
    tail = segment[LONG:]
    bias = jnp.where(tail[:, None] == tail[None, :], 0.0, -1e30).astype(f32)
    device = dp * lax.axis_size("fsdp") + me
    info = jnp.stack([me, (dp >> 1) & 1, shift, device, side, dp & 7]).astype(jnp.int32)

    far_qkv = swap(w_qkv, "fsdp", 2)
    core_qkv = swap(w_qkv, "fsdp", 1)
    vectors = jnp.stack([gain_one, shift_one, gain_two, shift_two])
    core_vectors = swap(vectors, "fsdp", 1)
    far_vectors = swap(vectors, "fsdp", 2)
    half_gate = choose(cut_rows(w_gate, 2), side)
    half_up = choose(cut_rows(w_up, 2), info[1])
    half_down = choose(cut_rows(w_down, 2), side)
    several = jnp.concatenate([w_out, w_gate, w_up], axis=1)
    gate_base, up_base = w_out.shape[1], w_out.shape[1] + w_gate.shape[1]
    rolled, tokens_turned = roll_tokens(info, tokens)
    order.done(rolled, cosine, sine, bias, member, half_gate, half_up, half_down, several)

    far_qkv, core_qkv = order.after(far_qkv, core_qkv)
    order.done(far_qkv)
    far_gate = swap(order.after(half_gate), "fsdp", 2)
    core_several = swap(order.after(several), "fsdp", 1)
    core_down = swap(order.after(w_down), "fsdp", 1)
    cross_qkv = order.after(swap(far_qkv, "fsdp", 1))
    order.done(cross_qkv)
    far_vectors, core_vectors = order.after(far_vectors, core_vectors)
    order.done(far_vectors)
    joined, full_qkv = project_qkv(
        info, order.after(rolled), cosine, sine, (whole_pieces(0), (w_qkv, core_qkv, far_qkv, cross_qkv))
    )
    order.done(joined)
    far_gate, core_several, core_down = order.after(far_gate, core_several, core_down)
    order.done(far_gate)
    far_out = swap(order.after(w_out), "fsdp", 2)
    far_up = swap(order.after(half_up), "fsdp", 2)
    more_gate = swap(far_gate, "dp", 1)
    cross_gate = order.after(swap(far_gate, "fsdp", 1))
    order.done(cross_gate)
    attended, logs = attend(info, order.after(joined), bias)
    order.done(attended)
    far_out = order.after(far_out)
    order.done(far_out)
    cross_out = swap(far_out, "fsdp", 1)
    cross_vectors = swap(order.after(far_vectors), "fsdp", 1)
    more_gate = order.after(more_gate)
    order.done(more_gate)
    more_cross_gate = swap(more_gate, "fsdp", 1)
    far_up, cross_out = order.after(far_up, cross_out)
    order.done(far_up)
    more_up = swap(far_up, "dp", 2)
    cross_up = swap(far_up, "fsdp", 1)
    normed_one, root_one, attended_turned, full_out = add_branch(
        info, order.after(attended), rolled, (whole_pieces(0), (w_out, core_several, far_out, cross_out))
    )
    order.done(normed_one)
    cross_vectors, more_cross_gate, cross_up = order.after(cross_vectors, more_cross_gate, cross_up)
    gain_a, shift_a, gain_b, shift_b = join_vectors([vectors, core_vectors, far_vectors, cross_vectors], me)
    far_down = swap(order.after(half_down), "fsdp", 2)
    gate_pieces = (w_gate, core_several, far_gate, more_gate, cross_gate, more_cross_gate)
    gate, hidden_low, hidden_turned, full_gate = project_gate(
        info, order.after(normed_one), gain_a, shift_a, (half_pieces(gate_base, lowest, not_lowest), gate_pieces)
    )
    order.done(gate)
    more_up = order.after(more_up)
    order.done(more_up)
    more_cross_up = swap(more_up, "fsdp", 1)
    far_down = order.after(far_down)
    order.done(far_down)
    more_down = swap(far_down, "dp", 1)
    cross_down = swap(far_down, "fsdp", 1)
    more_cross_up = order.after(more_cross_up)
    order.done(more_cross_up)
    up_pieces = (w_up, core_several, far_up, more_up, cross_up, more_cross_up)
    inner, up, full_up = project_up(
        info, order.after(hidden_low), gate, (half_pieces(up_base, second, not_second), up_pieces)
    )
    order.done(inner)
    more_down, cross_down = order.after(more_down, cross_down)
    order.done(more_down)
    down_pieces = (w_down, core_down, far_down, more_down, cross_down, swap(more_down, "fsdp", 1))
    output, normed_two, root_two, pooled, embedding, full_down = down_and_pool(
        info, order.after(inner), normed_one, gain_a, shift_a, gain_b, shift_b, member, sizes,
        (half_pieces(0, lowest, not_lowest), down_pieces),
    )
    order.done(embedding)
    everyone = gather_blocks(embedding).reshape(-1, width)

    quarter = width // 4
    tiles = gate.shape[1] // FEED_TILE
    pairs = width // LANES // 2
    had = {}
    pieces = {name: [] for name in ("down", "first", "later", "front", "back")}
    running = {name: reduce_steps(order, pieces[name]) for name in pieces}
    results = {}

    def advance(name):
        if name not in results:
            result = next(running[name])
            if result is not None:
                results[name] = result

    def drained(name):
        while name not in results:
            advance(name)
        return results[name]

    def run_loss():
        had["loss"], had["grad_second"], had["grad_feed"], had["vectors_two"] = loss_and_norm(
            info, everyone, pooled, embedding, sizes, member, normed_two, root_two, gain_b
        )
        order.done(had["grad_feed"])

    def run_down_theirs():
        pieces["down"].extend(down_gradient(info, inner, order.after(had["grad_feed"]), True))
        order.done(*pieces["down"])

    def run_down_own():
        pieces["down"].extend(down_gradient(info, order.after(inner), had["grad_feed"], False))
        order.done(*pieces["down"][1:])

    def run_feed(name, base, steps):
        held = had["grad_second" if base == 0 else "grad_hidden"]
        *made, had["grad_hidden"] = feed_back(
            info, order.after(had["grad_feed"]), hidden_turned, gate, up, full_down, full_gate, full_up,
            base, steps, held,
        )
        pieces[name].extend(made)
        order.done(had["grad_hidden"])

    def run_norm():
        had["grad_first"], had["branch"], had["grad_attended"], vectors_one = first_back(
            info, order.after(had["grad_hidden"]), normed_one, root_one, gain_a, full_out
        )
        order.done(had["grad_attended"])
        vectors = jnp.concatenate([vectors_one[:2], had["vectors_two"][:2]]).astype(bf16)
        vectors = vectors.reshape(4, 4, quarter).transpose(1, 0, 2)
        vectors = jnp.stack([choose(vectors, me ^ k) for k in range(4)])
        vectors = vectors.reshape(4, 2, width // 2)
        had["vectors"] = jnp.pad(vectors, ((0, 0), (0, SPARE_ROWS - 2), (0, 0)))

    def run_attend(name, base):
        had[name] = attend_back(
            info, order.after(joined), attended, had["grad_attended"], logs, bias, cosine, sine, base, pairs
        )
        order.done(*had[name])

    def run_front():
        pieces["front"].extend(
            weight_gradients(
                info, tokens_turned, attended_turned, order.after(*had["grads_front"]), "front",
                had["branch"], had["vectors"],
            )
        )
        order.done(*pieces["front"])

    def run_back():
        pieces["back"].extend(
            weight_gradients(info, tokens_turned, attended_turned, order.after(*had["grads_back"]), "back")
        )
        order.done(*pieces["back"])

    def run_tokens():
        grads = had["grads_front"] + had["grads_back"]
        had["grad_tokens"] = tokens_gradient(info, order.after(had["grad_first"]), grads, full_qkv)
        order.done(had["grad_tokens"])

    def run_unroll():
        had["output"] = unroll(info, order.after(output))
        order.done(had["output"])

    def run_down():
        had["down"] = finish_down(info, order.after(*drained("down")))
        order.done(had["down"])

    def run_gates():
        first, later = drained("first"), drained("later")
        values = order.after(*first, *later)
        had["gates"] = finish_gates(info, values[:2], values[2:])
        order.done(*had["gates"])

    work = {
        "finish_down": run_down,
        "gates": run_gates,
        "loss": run_loss,
        "down_theirs": run_down_theirs,
        "down_own": run_down_own,
        "feed_first": lambda: run_feed("first", 0, tiles // 2),
        "feed_later": lambda: run_feed("later", tiles // 2, tiles - tiles // 2),
        "norm": run_norm,
        "attend_front": lambda: run_attend("grads_front", 0),
        "attend_back": lambda: run_attend("grads_back", pairs),
        "grad_front": run_front,
        "grad_back": run_back,
        "tokens": run_tokens,
        "unroll": run_unroll,
    }
    for name in PLAN:
        work.get(name, functools.partial(advance, name))()

    grad_qkv, grad_out, sums = finish(info, drained("front"), drained("back"))
    sums = sums[:2].reshape(4, quarter)
    return (
        had["loss"][0, 0],
        had["output"],
        had["grad_tokens"],
        grad_qkv,
        grad_out,
        had["gates"][0],
        had["gates"][1],
        had["down"],
        sums[0],
        sums[1],
        sums[2],
        sums[3],
    )


def solution(mesh):
    placed = (
        P(("dp", "fsdp"), None),
        P(("dp", "fsdp"), None),
        P("fsdp", None),
        P("fsdp", None),
        P("fsdp", None),
        P("fsdp", None),
        P("fsdp", None),
        P("fsdp"),
        P("fsdp"),
        P("fsdp"),
        P("fsdp"),
    )
    return jax.shard_map(
        per_device,
        mesh=mesh,
        in_specs=placed,
        out_specs=(
            P(),
            P(("dp", "fsdp"), None),
            P(("dp", "fsdp"), None),
            P("fsdp", None),
            P("fsdp", None),
            P("fsdp", None),
            P("fsdp", None),
            P("fsdp", None),
            P("fsdp"),
            P("fsdp"),
            P("fsdp"),
            P("fsdp"),
        ),
        check_vma=False,
    )
```

```python
import functools
import types

import jax
import jax.numpy as jnp
from jax import lax
from jax.experimental import pallas as pl
from jax.experimental.pallas import tpu as pltpu
from jax.sharding import PartitionSpec as P

HD = 64
PAIRS = 4
LONG = 768
LANES = 128
FEED_TILE = 512
SPARE_ROWS = 64
exact_arithmetic = lax.Precision.HIGHEST
eps_norm = 1e-05
eps_embed = 1e-06
logit_divisor = 0.05
rope_base = 1000.0
log2_e = 1.4426950408889634
f32 = jnp.float32
bf16 = jnp.bfloat16
HBM = pl.BlockSpec(memory_space=pl.ANY)


def call(body, out_shapes, *, grid, in_specs, out_specs, scratch=(), vmem, name):
    return pl.pallas_call(
        body,
        out_shape=out_shapes,
        grid_spec=pltpu.PrefetchScalarGridSpec(
            num_scalar_prefetch=1,
            grid=grid,
            in_specs=in_specs,
            out_specs=out_specs,
            scratch_shapes=list(scratch),
        ),
        compiler_params=pltpu.CompilerParams(vmem_limit_bytes=vmem * 1024 * 1024),
        cost_estimate=pl.CostEstimate(flops=10**11, bytes_accessed=10**8, transcendentals=0),
        name=name,
    )


def whole(shape):
    return pl.BlockSpec(shape, lambda *_: (0,) * len(shape))


def shaped(shape, dtype):
    return pltpu.HBM(shape, dtype)


def close(shape, dtype):
    return jax.ShapeDtypeStruct(shape, dtype)


def pinned(*values):
    return [pltpu.with_memory_space_constraint(value, pltpu.HBM) for value in values]


def matmul(left, right, left_dim=1, right_dim=0, precision=None):
    return lax.dot_general(
        left,
        right,
        (((left_dim,), (right_dim,)), ((), ())),
        precision=precision,
        preferred_element_type=f32,
    )


def start_weight(info, parts, full, sem, columns, each=False):
    for (other, cut, block, base), piece in parts:
        rows = piece.shape[0]
        start = (info[0] ^ other) * (rows * cut)
        if block is not None:
            start = start + block(info) * rows
        target = full.at[pl.ds(pl.multiple_of(start, 16), rows), columns]
        source = piece.at[:, pl.ds(base + columns.start, columns.size)]
        pltpu.make_async_copy(source, target, sem.at[other] if each else sem).start()


def wait_weight(full, sem, columns):
    pltpu.make_async_copy(full.at[:, columns], full.at[:, columns], sem).wait()


def turn_rows(info, turned, target):
    count = turned.shape[0] // 4
    for k in range(4):
        start = pl.multiple_of((info[0] ^ k) * count, 32)
        target[k] = turned[pl.ds(start, count), :]


def sigmoid(value):
    return 0.5 * jnp.tanh(0.5 * value) + 0.5


def roll_body(info, tokens, rolled, turned, scratch):
    count, width = tokens.shape
    shift = lax.rem(count - info[2], count)
    for first in range(0, width, LANES):
        lanes = pl.ds(first, LANES)
        moved = pltpu.roll(tokens[:, lanes].astype(f32), shift, 0).astype(bf16)
        rolled[:, lanes] = moved
        scratch[pl.ds(first, LANES), :] = moved.T
    turn_rows(info, scratch, turned)


def roll_tokens(info, tokens):
    count, width = tokens.shape
    return call(
        roll_body,
        (close(tokens.shape, bf16), shaped((4, width // 4, count), bf16)),
        grid=(1,),
        in_specs=[whole(tokens.shape)],
        out_specs=(whole(tokens.shape), whole((4, width // 4, count))),
        scratch=[pltpu.VMEM((width, count), bf16)],
        vmem=12,
        name="roll_tokens",
    )(info, tokens)


def unroll_body(info, value, moved):
    count = value.shape[0]
    for first in range(0, value.shape[1], LANES):
        lanes = pl.ds(first, LANES)
        moved[:, lanes] = pltpu.roll(value[:, lanes].astype(f32), info[2], 0).astype(moved.dtype)


def unroll(info, value):
    count, width = value.shape
    tile = 256
    spec = pl.BlockSpec((count, tile), lambda i, *_: (0, i))
    return call(
        unroll_body,
        shaped(value.shape, value.dtype),
        grid=(width // tile,),
        in_specs=[spec],
        out_specs=spec,
        vmem=8,
        name="unroll",
    )(info, value)


def rope_lanes(value, cosine, signed_sine):
    lane = lax.broadcasted_iota(jnp.int32, (value.shape[0], LANES), 1)
    first_half = (lane & 32) == 0
    out = []
    for start in range(0, value.shape[1], LANES):
        piece = value[:, start : start + LANES]
        partner = jnp.where(first_half, pltpu.roll(piece, LANES - 32, 1), pltpu.roll(piece, 32, 1))
        out.append(piece * cosine + partner * signed_sine)
    return out[0] if len(out) == 1 else jnp.concatenate(out, axis=1)


def qkv_body(layout, info, rolled, cosine, signed_sine, *rest):
    parts = list(zip(layout, rest))
    joined, kept, full, sems, keep_sem = rest[len(layout) :]
    step = pl.program_id(0)
    steps = pl.num_programs(0)
    tile = joined.shape[1]

    @pl.when(step == 0)
    def _():
        for j in range(full.shape[1] // tile):
            start_weight(info, parts, full, sems.at[j], pl.ds(j * tile, tile))

    columns = pl.ds(pl.multiple_of(step * tile, tile), tile)
    wait_weight(full, sems.at[step], columns)
    pltpu.make_async_copy(full.at[:, columns], kept.at[:, columns], keep_sem.at[step]).start()
    chunk = 512

    @pl.when(step < 2 * steps // 3)
    def _():
        for first in range(0, joined.shape[0], chunk):
            rows = pl.ds(first, chunk)
            product = matmul(rolled[rows, :], full[:, columns])
            turned = rope_lanes(product, cosine[rows, :], signed_sine[rows, :])
            joined[rows, :] = turned.astype(bf16)

    @pl.when(step >= 2 * steps // 3)
    def _():
        for first in range(0, joined.shape[0], chunk):
            rows = pl.ds(first, chunk)
            joined[rows, :] = matmul(rolled[rows, :], full[:, columns]).astype(bf16)

    @pl.when(step == steps - 1)
    def _():
        for j in range(full.shape[1] // tile):
            piece = pl.ds(j * tile, tile)
            pltpu.make_async_copy(full.at[:, piece], kept.at[:, piece], keep_sem.at[j]).wait()


def project_qkv(info, rolled, cosine, signed_sine, weight):
    layout, parts = weight
    count, width = rolled.shape
    columns = parts[0].shape[1]
    tile = width
    return call(
        functools.partial(qkv_body, layout),
        (shaped((count, columns), bf16), shaped((width, columns), bf16)),
        grid=(columns // tile,),
        in_specs=[whole(rolled.shape), whole(cosine.shape), whole(cosine.shape)]
        + [HBM] * len(parts),
        out_specs=(pl.BlockSpec((count, tile), lambda i, *_: (0, i)), HBM),
        scratch=[
            pltpu.VMEM((width, columns), bf16),
            pltpu.SemaphoreType.DMA((columns // tile,)),
            pltpu.SemaphoreType.DMA((columns // tile,)),
        ],
        vmem=22,
        name="project_qkv",
    )(info, rolled, cosine, signed_sine, *pinned(*parts))


def attend_body(info, query, key, value, bias, attended, logs):
    pair = pl.program_id(0)
    count = query.shape[0]
    scale = 0.125 * log2_e
    lane = lax.broadcasted_iota(jnp.int32, (1, LANES), 1)

    @pl.when(pair == 0)
    def _():
        logs[...] = jnp.zeros_like(logs)

    def rows_of(first, size, keys, offset):
        rows = pl.ds(first, size)
        ones = jnp.ones((keys.size, LANES), bf16)
        extended = jnp.concatenate([value[keys, :], ones], axis=1)
        picked = []
        kept_logs = logs[rows, :]
        for head in range(2):
            mine = (lane >= HD) if head else (lane < HD)
            masked = jnp.where(mine, query[rows, :], jnp.zeros((), bf16))
            scores = matmul(masked, key[keys, :], 1, 1) * scale
            if offset is not None:
                scores = scores + offset
            top = jnp.max(scores, axis=1, keepdims=True)
            terms = jnp.exp2(scores - top).astype(bf16)
            product = matmul(terms, extended)
            total = product[:, LANES:]
            picked.append(product[:, :LANES] / total)
            kept_logs = jnp.where(lane == 2 * pair + head, top + jnp.log2(total), kept_logs)
        attended[rows, :] = jnp.where(lane < HD, picked[0], picked[1]).astype(bf16)
        logs[rows, :] = kept_logs

    for first in range(0, LONG, 256):
        rows_of(first, 256, pl.ds(0, LONG), None)
    rest = count - LONG
    rows_of(LONG, rest, pl.ds(LONG, rest), bias[...])


def attend(info, joined, bias):
    count, columns = joined.shape
    width = columns // 3
    pairs = width // LANES
    specs = [pl.BlockSpec((count, LANES), lambda i, *_, n=n: (0, n * pairs + i)) for n in range(3)]
    return call(
        attend_body,
        (close((count, width), bf16), shaped((count, LANES), f32)),
        grid=(pairs,),
        in_specs=specs + [whole(bias.shape)],
        out_specs=(pl.BlockSpec((count, LANES), lambda i, *_: (0, i)), whole((count, LANES))),
        vmem=16,
        name="attend",
    )(info, *pinned(joined, joined, joined), bias)


def norm_parts(value):
    centered = value - jnp.mean(value, axis=1, keepdims=True)
    root = lax.rsqrt(jnp.mean(centered * centered, axis=1, keepdims=True) + eps_norm)
    return centered * root, root


def branch_body(layout, info, attended, rolled, *rest):
    parts = list(zip(layout, rest))
    normed, root, turned, kept, full, scratch, sem, keep_sem = rest[len(layout) :]
    step = pl.program_id(0)

    @pl.when(step == 0)
    def _():
        start_weight(info, parts, full, sem, pl.ds(0, full.shape[1]))
        wait_weight(full, sem, pl.ds(0, full.shape[1]))
        pltpu.make_async_copy(full, kept, keep_sem).start()

    first = rolled[...].astype(f32) + matmul(attended[...], full[...])
    value, inverse = norm_parts(first)
    normed[...] = value
    root[...] = jnp.broadcast_to(inverse, root.shape)
    scratch[...] = attended[...].T
    turn_rows(info, scratch, turned)

    @pl.when(step == pl.num_programs(0) - 1)
    def _():
        pltpu.make_async_copy(full, kept, keep_sem).wait()


def add_branch(info, attended, rolled, weight):
    layout, parts = weight
    count, width = attended.shape
    tile = 256
    rows = pl.BlockSpec((tile, width), lambda i, *_: (i, 0))
    return call(
        functools.partial(branch_body, layout),
        (
            shaped((count, width), f32),
            shaped((count, LANES), f32),
            shaped((4, width // 4, count), bf16),
            shaped((width, width), bf16),
        ),
        grid=(count // tile,),
        in_specs=[rows, rows] + [HBM] * len(parts),
        out_specs=(
            rows,
            pl.BlockSpec((tile, LANES), lambda i, *_: (i, 0)),
            pl.BlockSpec((4, width // 4, tile), lambda i, *_: (0, 0, i)),
            HBM,
        ),
        scratch=[
            pltpu.VMEM((width, width), bf16),
            pltpu.VMEM((width, tile), bf16),
            pltpu.SemaphoreType.DMA,
            pltpu.SemaphoreType.DMA,
        ],
        vmem=14,
        name="add_branch",
    )(info, *pinned(attended, rolled, *parts))


def gate_body(layout, info, normed, gain, shift, *rest):
    parts = list(zip(layout, rest))
    gate, hidden, turned, kept, full, low, scratch, sems, keep_sems = rest[len(layout) :]
    step = pl.program_id(0)
    tile = gate.shape[1]
    tiles = full.shape[1] // tile
    chunk = 512

    @pl.when(step == 0)
    def _():
        for j in range(tiles):
            start_weight(info, parts, full, sems.at[j], pl.ds(j * tile, tile))
        for first in range(0, low.shape[0], chunk):
            rows = pl.ds(first, chunk)
            value = (normed[rows, :] * gain[...] + shift[...]).astype(bf16)
            low[rows, :] = value
            scratch[:, rows] = value.T
        hidden[...] = low[...]
        turn_rows(info, scratch, turned)

    columns = pl.ds(pl.multiple_of(step * tile, tile), tile)
    wait_weight(full, sems.at[step], columns)
    pltpu.make_async_copy(full.at[:, columns], kept.at[:, columns], keep_sems.at[step]).start()
    for first in range(0, low.shape[0], chunk):
        rows = pl.ds(first, chunk)
        gate[rows, :] = matmul(low[rows, :], full[:, columns]).astype(bf16)

    @pl.when(step == tiles - 1)
    def _():
        for j in range(tiles):
            piece = pl.ds(j * tile, tile)
            pltpu.make_async_copy(full.at[:, piece], kept.at[:, piece], keep_sems.at[j]).wait()


def project_gate(info, normed, gain, shift, weight):
    layout, parts = weight
    count, width = normed.shape
    hidden = parts[0].shape[1]
    tile = 512
    columns = pl.BlockSpec((count, tile), lambda i, *_: (0, i))
    return call(
        functools.partial(gate_body, layout),
        (
            shaped((count, hidden), bf16),
            close((count, width), bf16),
            shaped((4, width // 4, count), bf16),
            shaped((width, hidden), bf16),
        ),
        grid=(hidden // tile,),
        in_specs=[whole(normed.shape), whole(gain.shape), whole(shift.shape)]
        + [HBM] * len(layout),
        out_specs=(columns, whole((count, width)), whole((4, width // 4, count)), HBM),
        scratch=[
            pltpu.VMEM((width, hidden), bf16),
            pltpu.VMEM((count, width), bf16),
            pltpu.VMEM((width, count), bf16),
            pltpu.SemaphoreType.DMA((hidden // tile,)),
            pltpu.SemaphoreType.DMA((hidden // tile,)),
        ],
        vmem=26,
        name="project_gate",
    )(info, *pinned(normed), gain, shift, *pinned(*parts))


def up_body(layout, info, low, gate, *rest):
    parts = list(zip(layout, rest))
    inner, up_out, kept, full, sems, keep_sems = rest[len(layout) :]
    step = pl.program_id(0)
    tile = inner.shape[1]
    tiles = full.shape[1] // tile
    chunk = 512

    @pl.when(step == 0)
    def _():
        for j in range(tiles):
            start_weight(info, parts, full, sems.at[j], pl.ds(j * tile, tile))

    columns = pl.ds(pl.multiple_of(step * tile, tile), tile)
    wait_weight(full, sems.at[step], columns)
    pltpu.make_async_copy(full.at[:, columns], kept.at[:, columns], keep_sems.at[step]).start()
    for first in range(0, low.shape[0], chunk):
        rows = pl.ds(first, chunk)
        up = matmul(low[rows, :], full[:, columns])
        up_out[rows, :] = up.astype(bf16)
        value = gate[rows, :].astype(f32)
        inner[rows, :] = (value * up * sigmoid(value)).astype(bf16)

    @pl.when(step == tiles - 1)
    def _():
        for j in range(tiles):
            piece = pl.ds(j * tile, tile)
            pltpu.make_async_copy(full.at[:, piece], kept.at[:, piece], keep_sems.at[j]).wait()


def project_up(info, low, gate, weight):
    layout, parts = weight
    count, width = low.shape
    hidden = parts[0].shape[1]
    tile = 512
    columns = pl.BlockSpec((count, tile), lambda i, *_: (0, i))
    return call(
        functools.partial(up_body, layout),
        (
            shaped((count, hidden), bf16),
            shaped((count, hidden), bf16),
            shaped((width, hidden), bf16),
        ),
        grid=(hidden // tile,),
        in_specs=[whole(low.shape), columns] + [HBM] * len(layout),
        out_specs=(columns, columns, HBM),
        scratch=[
            pltpu.VMEM((width, hidden), bf16),
            pltpu.SemaphoreType.DMA((hidden // tile,)),
            pltpu.SemaphoreType.DMA((hidden // tile,)),
        ],
        vmem=24,
        name="project_up",
    )(info, low, *pinned(gate, *parts))


def down_body(layout, info, inner, normed, gain_one, shift_one, gain, shift, member, sizes, *rest):
    parts = list(zip(layout, rest))
    output, normed_two, root, pooled, embedding, kept, full, feed, sems, keep_sem = rest[len(layout) :]
    step = pl.program_id(0)
    steps = pl.num_programs(0)
    tile = output.shape[0]
    quarter = full.shape[0] // 4

    @pl.when(step == 0)
    def _():
        start_weight(info, parts, full, sems, pl.ds(0, full.shape[1]), each=True)
        pooled[...] = jnp.zeros_like(pooled)
        for other in range(4):
            rows = pl.ds(pl.multiple_of((info[0] ^ other) * quarter, quarter), quarter)
            pltpu.make_async_copy(full.at[rows, :], full.at[rows, :], sems.at[other]).wait()
            product = matmul(inner[:, rows], full[rows, :])
            feed[...] = product if other == 0 else feed[...] + product
        pltpu.make_async_copy(full, kept, keep_sem).start()

    @pl.when(step > 0)
    def _():
        feed[...] = matmul(inner[...], full[...])

    hidden = normed[...] * gain_one[...] + shift_one[...]
    value, inverse = norm_parts(hidden + feed[...])
    normed_two[...] = value
    root[...] = jnp.broadcast_to(inverse, root.shape)
    result = value * gain[...] + shift[...]
    output[...] = result.astype(bf16)

    @pl.when(step < LONG // tile)
    def _():
        pooled[0:1, :] += jnp.sum(result, axis=0, keepdims=True)

    @pl.when(step == steps - 1)
    def _():
        longest = jnp.where(sizes[...] == LONG, pooled[0:1, :], 0.0)
        total = (longest + matmul(member[...], result, 0, 0, exact_arithmetic)) / sizes[...]
        pooled[...] = total
        square = jnp.sum(total * total, axis=1, keepdims=True)
        embedding[...] = total * lax.rsqrt(square + eps_embed)
        pltpu.make_async_copy(full, kept, keep_sem).wait()


def down_and_pool(info, inner, normed, gain_one, shift_one, gain, shift, member, sizes, weight):
    layout, parts = weight
    count, width = normed.shape
    hidden = inner.shape[1]
    seqs = member.shape[1]
    tile = 256
    rows = pl.BlockSpec((tile, width), lambda i, *_: (i, 0))
    vector = whole((1, width))
    return call(
        functools.partial(down_body, layout),
        (
            shaped((count, width), bf16),
            shaped((count, width), f32),
            shaped((count, LANES), f32),
            close((seqs, width), f32),
            close((seqs, width), f32),
            shaped((hidden, width), bf16),
        ),
        grid=(count // tile,),
        in_specs=[
            pl.BlockSpec((tile, hidden), lambda i, *_: (i, 0)),
            rows,
            vector,
            vector,
            vector,
            vector,
            pl.BlockSpec((tile, seqs), lambda i, *_: (LONG // tile, 0)),
            whole(sizes.shape),
        ]
        + [HBM] * len(parts),
        out_specs=(
            rows,
            rows,
            pl.BlockSpec((tile, LANES), lambda i, *_: (i, 0)),
            whole((seqs, width)),
            whole((seqs, width)),
            HBM,
        ),
        scratch=[
            pltpu.VMEM((hidden, width), bf16),
            pltpu.VMEM((tile, width), f32),
            pltpu.SemaphoreType.DMA((4,)),
            pltpu.SemaphoreType.DMA,
        ],
        vmem=24,
        name="down_and_pool",
    )(info, *pinned(inner, normed), gain_one, shift_one, gain, shift, member, sizes, *pinned(*parts))


def loss_body(info, everyone, pooled, embedding, sizes, member, normed, root, gain, *rest):
    loss, grad_second, grad_feed, vectors, pulled, upstreams = rest
    step = pl.program_id(0)
    seqs, width = embedding.shape
    pairs = seqs // 2

    @pl.when(step == 0)
    def _():
        devices = everyone.shape[0] // seqs
        count = devices * pairs
        blocks = everyone[...].reshape(devices, seqs, width)
        requests = blocks[:, :pairs].reshape(count, width)
        passages = blocks[:, pairs:].reshape(count, width)
        sims = matmul(requests, passages, 1, 1, exact_arithmetic) * (1.0 / logit_divisor)
        top = jnp.max(sims, axis=1, keepdims=True)
        terms = jnp.exp(sims - top)
        total = jnp.sum(terms, axis=1, keepdims=True)
        row = lax.broadcasted_iota(jnp.int32, sims.shape, 0)
        column = lax.broadcasted_iota(jnp.int32, sims.shape, 1)
        diagonal = jnp.sum(jnp.where(row == column, sims, 0.0), axis=1, keepdims=True)
        mean = jnp.sum(top + jnp.log(total) - diagonal, axis=0, keepdims=True) / count
        loss[...] = jnp.broadcast_to(mean, loss.shape)
        pulls = terms / total
        first = info[3] * pairs
        near = lax.broadcasted_iota(jnp.int32, (seqs, count), 0)
        place = lax.broadcasted_iota(jnp.int32, (seqs, count), 1)
        picked = jnp.where(place == first + near, 1.0, 0.0)
        my_rows = matmul(picked, pulls, 1, 0, exact_arithmetic)
        my_columns = matmul(picked, pulls, 1, 1, exact_arithmetic)
        to_requests = matmul(my_rows, passages, 1, 0, exact_arithmetic)
        to_passages = matmul(my_columns, requests, 1, 0, exact_arithmetic)
        own = embedding[...]
        swapped = jnp.concatenate([own[pairs:], own[:pairs]], axis=0)
        gathered = jnp.concatenate([to_requests[:pairs], to_passages[:pairs]], axis=0)
        grad_embed = (gathered - swapped) * (1.0 / (logit_divisor * count))
        means = pooled[...]
        inverse = lax.rsqrt(jnp.sum(means * means, axis=1, keepdims=True) + eps_embed)
        along = jnp.sum(means * grad_embed, axis=1, keepdims=True)
        pulled[...] = (inverse * grad_embed - inverse * inverse * inverse * means * along) / sizes[
            ...
        ]
        vectors[...] = jnp.zeros_like(vectors)

    @pl.when(step < LONG // normed.shape[0])
    def _():
        longest = jnp.sum(jnp.where(sizes[...] == LONG, pulled[...], 0.0), axis=0, keepdims=True)
        upstreams[...] = jnp.broadcast_to(longest, upstreams.shape)

    @pl.when(step >= LONG // normed.shape[0])
    def _():
        upstreams[...] = matmul(member[...], pulled[...], 1, 0, exact_arithmetic)

    upstream = upstreams[...]
    value = normed[...]
    vectors[0:1, :] += jnp.sum(upstream * value, axis=0, keepdims=True)
    vectors[1:2, :] += jnp.sum(upstream, axis=0, keepdims=True)
    result = norm_back(upstream, value, root[:, :1], gain[...])
    grad_second[...] = result
    grad_feed[...] = result.astype(bf16)


def norm_back(upstream, normed, root, gain):
    scaled = upstream * gain
    return root * (
        scaled
        - jnp.mean(scaled, axis=1, keepdims=True)
        - normed * jnp.mean(scaled * normed, axis=1, keepdims=True)
    )


def loss_and_norm(info, everyone, pooled, embedding, sizes, member, normed, root, gain):
    count, width = normed.shape
    seqs = member.shape[1]
    tile = 256
    rows = pl.BlockSpec((tile, width), lambda i, *_: (i, 0))
    return call(
        loss_body,
        (
            close((8, LANES), f32),
            shaped((count, width), f32),
            close((count, width), bf16),
            close((8, width), f32),
        ),
        grid=(count // tile,),
        in_specs=[
            whole(everyone.shape),
            whole(pooled.shape),
            whole(embedding.shape),
            whole(sizes.shape),
            pl.BlockSpec((tile, seqs), lambda i, *_: (i, 0)),
            rows,
            pl.BlockSpec((tile, LANES), lambda i, *_: (i, 0)),
            whole(gain.shape),
        ],
        out_specs=(whole((8, LANES)), rows, rows, whole((8, width))),
        scratch=[pltpu.VMEM((seqs, width), f32), pltpu.VMEM((tile, width), f32)],
        vmem=16 + everyone.shape[0] * width * 24 // 2**20,
        name="loss_and_norm",
    )(info, everyone, pooled, embedding, sizes, member, *pinned(normed, root), gain)


def outer_body(theirs, info, left, right, *outs):
    step = pl.program_id(0)
    product = matmul(left[...], right[...], 0, 0).astype(bf16)
    rows = product.shape[0] // 8
    for block in range(8):
        source = slice(block * rows, (block + 1) * rows)
        target = pl.ds(pl.multiple_of(relative_block(info, block) * rows, 16), rows)
        if theirs:
            outs[0][0, target, :] = product[source]
            continue
        for index, out in enumerate(outs):

            @pl.when(step == index)
            def _():
                out[target, :] = product[source]


def down_gradient(info, inner, grad_feed, theirs):
    count, hidden = inner.shape
    width = grad_feed.shape[1]
    rows = hidden // 4
    first, last = (3, 1) if theirs else (2, 0)

    def column(i, info):
        return (0, info[0] ^ jnp.where(i == 0, first, last))

    if theirs:
        outs = (shaped((2, rows, width), bf16),)
        specs = (pl.BlockSpec((1, rows, width), lambda i, *_: (i, 0, 0)),)
    else:
        outs = (shaped((rows, width), bf16),) * 2
        specs = (whole((rows, width)),) * 2
    return call(
        functools.partial(outer_body, theirs),
        outs,
        grid=(2,),
        in_specs=[pl.BlockSpec((count, rows), column), whole(grad_feed.shape)],
        out_specs=specs,
        vmem=20,
        name="down_theirs" if theirs else "down_own",
    )(info, *pinned(inner), grad_feed)


def piece_shapes(rows, columns):
    own = shaped((rows, columns), bf16)
    return shaped((2, rows, columns), bf16), own, own


def piece_specs(rows, tile):
    own = pl.BlockSpec((rows, tile), lambda i, *_: (0, i))
    return pl.BlockSpec((2, rows, tile), lambda i, *_: (0, 0, i)), own, own


def relative_block(info, block):
    place = block ^ info[5]
    return ((place & 1) << 2) | (place & 2) | (place >> 2)


def multiply_into(held, turned, grads, first):
    _, quarter, count = turned.shape
    grad = grads[0] if len(grads) == 1 else jnp.concatenate(grads, axis=1)
    products = matmul(turned[...].reshape(4 * quarter, count), grad).astype(bf16)
    width = held.shape[2]
    for index in range(len(grads)):
        rows = pl.ds((first + index) * quarter, quarter)
        for place in range(4):
            part = slice(place * quarter, (place + 1) * quarter)
            held[place, rows, :] = products[part, index * width : (index + 1) * width]


def write_pieces(info, held, theirs, far, near):
    rows = held.shape[1] // 8
    for block in range(8):
        source = slice(block * rows, (block + 1) * rows)
        target = pl.ds(pl.multiple_of(relative_block(info, block) * rows, 16), rows)
        near[target, :] = held[0, source, :]
        theirs[1, target, :] = held[1, source, :]
        far[target, :] = held[2, source, :]
        theirs[0, target, :] = held[3, source, :]


def feed_body(info, grad_feed, turned, gate_in, up_in, down, gate_full, up_full, held, *outs):
    *pieces, grad_hidden, products, turned_here, held_here, total, turned_sem, held_sem, out_sems = outs
    step = pl.program_id(0)
    last = step == pl.num_programs(0) - 1
    count = grad_feed.shape[0]
    chunk = 512
    gates, ups = [], []
    turned_copy = pltpu.make_async_copy(turned, turned_here, turned_sem)
    held_copy = pltpu.make_async_copy(held, held_here, held_sem)

    def out_copy(index):
        rows = pl.ds(index * chunk, chunk)
        return pltpu.make_async_copy(total.at[rows, :], grad_hidden.at[rows, :], out_sems.at[index])

    @pl.when(step == 0)
    def _():
        turned_copy.start()
        held_copy.start()
        total[...] = jnp.zeros_like(total)

    @pl.when(last)
    def _():
        held_copy.wait()
        total[...] += held_here[...]

    for index in range(count // chunk):
        rows = pl.ds(index * chunk, chunk)
        grad_inner = matmul(grad_feed[rows, :], down[...], 1, 1)
        gate = gate_in[rows, :].astype(f32)
        up = up_in[rows, :].astype(f32)
        share = sigmoid(gate)
        scaled = grad_inner * share
        grad_gate = (scaled * up * (1.0 + gate * (1.0 - share))).astype(bf16)
        grad_up = (scaled * gate).astype(bf16)
        gates.append(grad_gate)
        ups.append(grad_up)
        total[rows, :] += matmul(grad_gate, gate_full[...], 1, 1) + matmul(grad_up, up_full[...], 1, 1)

        @pl.when(last)
        def _():
            out_copy(index).start()

    @pl.when(step == 0)
    def _():
        turned_copy.wait()

    for which, grads in ((0, gates), (1, ups)):
        multiply_into(products, turned_here, [jnp.concatenate(grads, axis=0)], which)
    write_pieces(info, products, *pieces)

    @pl.when(last)
    def _():
        for index in range(count // chunk):
            out_copy(index).wait()


def feed_back(info, grad_feed, turned, gate, up, down, gate_full, up_full, base, steps, held):
    count = gate.shape[0]
    width = grad_feed.shape[1]
    quarter = width // 4
    tile = FEED_TILE
    columns = pl.BlockSpec((count, tile), lambda i, *_: (0, base + i))
    weights = pl.BlockSpec((width, tile), lambda i, *_: (0, base + i))
    return call(
        feed_body,
        piece_shapes(2 * quarter, steps * tile) + (shaped((count, width), f32),),
        grid=(steps,),
        in_specs=[
            whole(grad_feed.shape),
            HBM,
            columns,
            columns,
            pl.BlockSpec((tile, width), lambda i, *_: (base + i, 0)),
            weights,
            weights,
            HBM,
        ],
        out_specs=piece_specs(2 * quarter, tile) + (HBM,),
        scratch=[
            pltpu.VMEM((4, 2 * quarter, tile), bf16),
            pltpu.VMEM(turned.shape, bf16),
            pltpu.VMEM((count, width), f32),
            pltpu.VMEM((count, width), f32),
            pltpu.SemaphoreType.DMA,
            pltpu.SemaphoreType.DMA,
            pltpu.SemaphoreType.DMA((2,)),
        ],
        vmem=40,
        name=f"feed_back_{base}",
    )(info, grad_feed, *pinned(turned, gate, up, down, gate_full, up_full, held))


def first_body(info, grad_hidden, normed, root, gain, weight, *outs):
    grad_first, branch, grad_attended, vectors = outs

    @pl.when(pl.program_id(0) == 0)
    def _():
        vectors[...] = jnp.zeros_like(vectors)

    upstream = grad_hidden[...]
    value = normed[...]
    vectors[0:1, :] += jnp.sum(upstream * value, axis=0, keepdims=True)
    vectors[1:2, :] += jnp.sum(upstream, axis=0, keepdims=True)
    result = norm_back(upstream, value, root[:, :1], gain[...])
    grad_first[...] = result
    low = result.astype(bf16)
    branch[...] = low
    grad_attended[...] = matmul(low, weight[...], 1, 1).astype(bf16)


def first_back(info, grad_hidden, normed, root, gain, weight):
    count, width = normed.shape
    tile = 256
    rows = pl.BlockSpec((tile, width), lambda i, *_: (i, 0))
    return call(
        first_body,
        (
            shaped((count, width), f32),
            shaped((count, width), bf16),
            shaped((count, width), bf16),
            close((8, width), f32),
        ),
        grid=(count // tile,),
        in_specs=[
            rows,
            rows,
            pl.BlockSpec((tile, LANES), lambda i, *_: (i, 0)),
            whole(gain.shape),
            whole(weight.shape),
        ],
        out_specs=(rows, rows, rows, whole((8, width))),
        vmem=20,
        name="first_back",
    )(info, *pinned(grad_hidden, normed, root), gain, weight)


def attend_back_body(base, info, query, key, value, attended, upstream, logs, bias, cosine, sine, *rest):
    (grad_query, grad_key, grad_value, logs_row, sums) = rest
    pair = base + pl.program_id(0)
    count = query.shape[0]
    scale = 0.125 * log2_e
    lane = lax.broadcasted_iota(jnp.int32, (1, LANES), 1)

    @pl.when(pl.program_id(0) == 0)
    def _():
        logs_row[...] = logs[...].T

    both = upstream[...].astype(f32) * attended[...].astype(f32)
    row = lax.broadcasted_iota(jnp.int32, (8, LANES), 0)
    column = lax.broadcasted_iota(jnp.int32, (8, LANES), 1)
    chooser = jnp.where((column // HD) == row, 1.0, 0.0)
    sums[...] = matmul(chooser, both, 1, 1, exact_arithmetic)

    zero = jnp.zeros((), bf16)
    for first, size, offset in ((0, LONG, None), (LONG, count - LONG, bias)):
        rows = pl.ds(first, size)
        key_rows, query_rows, up_rows = key[rows, :], query[rows, :], upstream[rows, :]
        key_grad = value_grad = query_grad = None
        for head in range(2):
            mine = (lane >= HD) if head else (lane < HD)
            masked_query = jnp.where(mine, query_rows, zero)
            masked_up = jnp.where(mine, up_rows, zero)
            masked_key = jnp.where(mine, key_rows, zero)
            log_row = logs_row[pl.ds(2 * pair + head, 1), rows]
            sum_row = sums[head : head + 1, rows]
            key_pieces, value_pieces = [], []
            query_total = None
            for start in range(first, first + size, 256):
                keys = pl.ds(start, 256)
                scores = matmul(key[keys, :], masked_query, 1, 1) * scale
                if offset is not None:
                    scores = scores + offset[...]
                probs = jnp.exp2(scores - log_row)
                grad_probs = matmul(value[keys, :], masked_up, 1, 1)
                grad_scores = (probs * (grad_probs - sum_row)).astype(bf16)
                value_pieces.append(matmul(probs.astype(bf16), masked_up))
                key_pieces.append(matmul(grad_scores, masked_query))
                kept_key = masked_key[start - first : start - first + 256]
                piece = matmul(grad_scores, kept_key, 0, 0)
                query_total = piece if query_total is None else query_total + piece
            key_head = jnp.concatenate(key_pieces, axis=0)
            value_head = jnp.concatenate(value_pieces, axis=0)
            key_grad = key_head if key_grad is None else key_grad + key_head
            value_grad = value_head if value_grad is None else value_grad + value_head
            query_grad = query_total if query_grad is None else query_grad + query_total
        turn_cos, turn_sin = cosine[rows, :], sine[rows, :]
        for grad, target in ((query_grad, grad_query), (key_grad, grad_key)):
            low = (grad * 0.125).astype(bf16).astype(f32)
            target[rows, :] = rope_lanes(low, turn_cos, -turn_sin).astype(bf16)
        grad_value[rows, :] = value_grad.astype(bf16)


def attend_back(info, joined, attended, upstream, logs, bias, cosine, sine, base, pairs):
    count, columns = joined.shape
    every = columns // 3 // LANES
    specs = [
        pl.BlockSpec((count, LANES), lambda i, *_, n=n: (0, n * every + base + i)) for n in range(3)
    ]
    block = pl.BlockSpec((count, LANES), lambda i, *_: (0, base + i))
    return call(
        functools.partial(attend_back_body, base),
        (close((count, pairs * LANES), bf16),) * 3,
        grid=(pairs,),
        in_specs=specs
        + [block, block, whole(logs.shape), whole(bias.shape)]
        + [whole(cosine.shape)] * 2,
        out_specs=(pl.BlockSpec((count, LANES), lambda i, *_: (0, i)),) * 3,
        scratch=[pltpu.VMEM((LANES, count), f32), pltpu.VMEM((8, count), f32)],
        vmem=32,
        name=f"attend_back_{base}",
    )(info, *pinned(joined, joined, joined, attended, upstream), logs, bias, cosine, sine)


def turned_body(info, turned_a, turned_b, *rest):
    grads, pieces, held = rest[:-4], rest[-4:-1], rest[-1]
    used = len(grads) * turned_a.shape[1]
    spare = held.shape[1] - used
    if len(grads) > 3:
        extra = grads[-1]
        grads = grads[:-1]
        used = len(grads) * turned_a.shape[1]
        held[:, used:, :] = extra[...]
    else:
        held[:, used:, :] = jnp.zeros((4, spare, held.shape[2]), bf16)
    for turned, first, several in ((turned_a, 0, grads[:3]), (turned_b, 3, grads[3:])):
        if several:
            multiply_into(held, turned, [grad[...] for grad in several], first)
    write_pieces(info, held, *pieces)


def weight_gradients(info, turned_a, turned_b, grads, name, branch=None, extra=None):
    _, quarter, count = turned_a.shape
    width = grads[0].shape[1]
    tile = LANES
    specs = [pl.BlockSpec((count, tile), lambda i, *_: (0, i))] * len(grads)
    rows = len(grads) * quarter + SPARE_ROWS
    args = list(grads)
    if branch is not None:
        specs += [
            pl.BlockSpec((count, tile), lambda i, *_, n=n: (0, n * width // tile + i)) for n in range(2)
        ]
        specs.append(pl.BlockSpec((4, SPARE_ROWS, tile), lambda i, *_: (0, 0, i)))
        args += [branch, branch, extra]
        rows += 2 * quarter
    return call(
        turned_body,
        piece_shapes(rows, width),
        grid=(width // tile,),
        in_specs=[whole(turned_a.shape), whole(turned_b.shape)] + specs,
        out_specs=piece_specs(rows, tile),
        scratch=[pltpu.VMEM((4, rows, tile), bf16)],
        vmem=22,
        name=name,
    )(info, *pinned(turned_a, turned_b, *args))


def tokens_body(info, grad_first, weight, *rest):
    grads, out = rest[:-1], rest[-1]
    total = grad_first[...]
    width = grads[0].shape[1]
    for part in range(2):
        for index in range(3):
            first = (2 * index + part) * width
            grad = grads[3 * part + index]
            total = total + matmul(grad[...], weight[:, first : first + width], 1, 1)
    out[...] = pltpu.roll(total, info[2], 0)


def tokens_gradient(info, grad_first, grads, weight):
    count, width = grad_first.shape
    tile = 256
    block = pl.BlockSpec((count, tile), lambda i, *_: (0, i))
    return call(
        tokens_body,
        shaped((count, width), f32),
        grid=(width // tile,),
        in_specs=[block, pl.BlockSpec((tile, weight.shape[1]), lambda i, *_: (i, 0))]
        + [whole(grad.shape) for grad in grads],
        out_specs=block,
        vmem=26,
        name="tokens_gradient",
    )(info, grad_first, weight, *grads)


def settle(info, mine, other, held, target):
    half = mine.shape[0]
    held[:half, :] = mine[...].astype(f32)
    held[half:, :] = other[...].astype(f32)
    rows = half // 4
    for block in range(8):
        source = pl.ds(pl.multiple_of(relative_block(info, block) * rows, 8), rows)
        target[block * rows : (block + 1) * rows, :] = held[source, :]


def finish_body(info, front_a, front_b, back_a, back_b, grad_qkv, grad_out, vectors, *scratch):
    quarter, width = grad_out.shape
    half = width // 2
    front_held, front, back_held, back = scratch
    settle(info, front_a, front_b, front_held, front)
    settle(info, back_a, back_b, back_held, back)
    for index in range(3):
        rows = slice(index * quarter, (index + 1) * quarter)
        grad_qkv[:, index * width : index * width + half] = front[rows, :]
        grad_qkv[:, index * width + half : (index + 1) * width] = back[rows, :]
    grad_out[:, :half] = front[3 * quarter : 4 * quarter, :]
    grad_out[:, half:] = front[4 * quarter : 5 * quarter, :]
    vectors[...] = front[5 * quarter : 5 * quarter + 8, :]


def finish(info, front, back):
    half = front[0].shape[1]
    rows, back_rows = 2 * front[0].shape[0], 2 * back[0].shape[0]
    quarter = (rows - SPARE_ROWS) // 5
    shapes = ((quarter, 6 * half), (quarter, 2 * half), (8, half))
    return call(
        finish_body,
        tuple(close(shape, f32) for shape in shapes),
        grid=(1,),
        in_specs=[whole(value.shape) for value in (*front, *back)],
        out_specs=tuple(whole(shape) for shape in shapes),
        scratch=[pltpu.VMEM((count, half), f32) for count in (rows, rows, back_rows, back_rows)],
        vmem=20,
        name="finish",
    )(info, *front, *back)


def gates_body(info, first_a, first_b, later_a, later_b, grad_gate, grad_up, held, target):
    quarter = grad_gate.shape[0]
    start = 0
    for mine, other in ((first_a, first_b), (later_a, later_b)):
        settle(info, mine, other, held, target)
        columns = slice(start, start + mine.shape[1])
        grad_gate[:, columns] = target[:quarter, :]
        grad_up[:, columns] = target[quarter:, :]
        start += mine.shape[1]


def finish_gates(info, first, later):
    half, columns = first[0].shape
    shape = (half, 2 * columns)
    return call(
        gates_body,
        (shaped(shape, f32),) * 2,
        grid=(1,),
        in_specs=[whole(first[0].shape)] * 4,
        out_specs=(whole(shape),) * 2,
        scratch=[pltpu.VMEM((2 * half, columns), f32)] * 2,
        vmem=28,
        name="finish_gates",
    )(info, *pinned(*first, *later))


def settle_down_body(info, mine, other, grad_down, held):
    settle(info, mine, other, held, grad_down)


def finish_down(info, down):
    half, columns = down[0].shape
    shape = (2 * half, columns)
    return call(
        settle_down_body,
        shaped(shape, f32),
        grid=(1,),
        in_specs=[whole(down[0].shape)] * 2,
        out_specs=whole(shape),
        scratch=[pltpu.VMEM(shape, f32)],
        vmem=16,
        name="finish_down",
    )(info, *pinned(*down))


def swap(value, axis, bit):
    size = lax.axis_size(axis)
    return lax.ppermute(value, axis, [(i, i ^ bit) for i in range(size)])


def choose(value, index):
    return lax.dynamic_index_in_dim(value, index, 0, keepdims=False)


def low_sum(*terms):
    total = terms[0].astype(f32)
    for term in terms[1:]:
        total = total + term.astype(f32)
    return total.astype(bf16)


class Order:
    def __init__(self):
        self.last = ()

    def after(self, *values):
        if self.last:
            values = lax.optimization_barrier((*values, *self.last))[: len(values)]
        return values[0] if len(values) == 1 else values

    def done(self, *values):
        self.last = values


def cut_rows(shard, blocks):
    rows, columns = shard.shape
    return shard.reshape(blocks, rows // blocks, columns)


def lowest(info):
    return info[4]


def not_lowest(info):
    return 1 - info[4]


def second(info):
    return info[1]


def not_second(info):
    return 1 - info[1]


def whole_pieces(base):
    return ((0, 1, None, 0), (1, 1, None, base), (2, 1, None, 0), (3, 1, None, 0))


def half_pieces(base, here, there):
    far = tuple((place, 2, block, 0) for place in (2, 3) for block in (here, there))
    return ((0, 1, None, 0), (1, 1, None, base)) + far


def join_vectors(pieces, me):
    pieces = jnp.stack(pieces)
    full = jnp.concatenate([choose(pieces, me ^ q) for q in range(4)], axis=1)
    return [full[i : i + 1].astype(f32) for i in range(full.shape[0])]


def gather_blocks(block):
    dp_size, fsdp_size = lax.axis_size("dp"), lax.axis_size("fsdp")
    bits = dp_size.bit_length() - 1
    held = block[None]
    for bit in reversed(range(bits)):
        other = swap(held, "dp", 1 << bit)
        low = ((lax.axis_index("dp") >> bit) & 1) == 0
        held = jnp.where(low, jnp.stack([held, other]), jnp.stack([other, held]))
        held = held.reshape((-1,) + block.shape)
    held = held.reshape((2,) * bits + block.shape)
    held = held.transpose(tuple(range(bits))[::-1] + tuple(range(bits, bits + block.ndim)))
    held = held.reshape((dp_size,) + block.shape)
    held = lax.all_gather(held, "fsdp", axis=1)
    return held.reshape((dp_size * fsdp_size,) + block.shape)


def reduce_steps(order, pieces):
    bits = lax.axis_size("dp").bit_length() - 1
    from_core = swap(order.after(pieces[0]), "fsdp", 1)
    yield None
    far, near = pieces[1:]
    far, from_core = order.after(far, from_core)
    total = low_sum(far, from_core[0])
    order.done(total)
    from_far = swap(total, "fsdp", 2)
    yield None
    terms = order.after(near, from_core, from_far)
    terms = [terms[0], terms[1][1], terms[2]]
    rows = near.shape[0]
    for step in range(3):
        rows //= 2
        send = low_sum(*[term[rows : 2 * rows] for term in terms])
        order.done(send)
        other = swap(send, "dp", 1 << step)
        yield None
        terms = list(order.after(near, from_core, from_far, *terms[3:], other))
        terms[1] = terms[1][1]
    held = low_sum(*[term[:rows] for term in terms])
    for step in range(3, bits):
        order.done(held)
        other = swap(held, "dp", 1 << step)
        yield None
        held = low_sum(*order.after(held, other))
    for step in (2, 1, 0):
        order.done(held)
        other = swap(held, "dp", 1 << step)
        yield None
        held, other = order.after(held, other)
        if step:
            held = jnp.concatenate([held, other])
    order.done(held, other)
    yield held, other


class Unit:
    def __init__(self, order):
        self.pieces = []
        self.steps = reduce_steps(order, self.pieces)
        self.result = None

    def step(self):
        if self.result is None:
            self.result = next(self.steps)

    def drained(self):
        while self.result is None:
            self.step()
        return self.result


def pack_layout(lengths_row, count):
    ends = jnp.cumsum(lengths_row)
    starts = ends - lengths_row
    shift = jnp.sum(jnp.where(lengths_row == LONG, starts, 0))
    places = lax.rem(lax.iota(jnp.int32, count) + shift, count)
    segment = jnp.sum((places[:, None] >= ends[None, :]).astype(jnp.int32), axis=1)
    member = segment[:, None] == lax.iota(jnp.int32, lengths_row.shape[0])[None, :]
    offset = jnp.sum(jnp.where(member, starts[None, :], 0), axis=1)
    return shift, segment, places - offset, member.astype(f32)


def rotary_tables(position):
    lane = lax.iota(jnp.int32, LANES)
    frequency = rope_base ** (-2.0 * (lane % (HD // 2)).astype(f32) / HD)
    angles = position.astype(f32)[:, None] * frequency[None, :]
    sine = jnp.sin(angles)
    return jnp.cos(angles), jnp.where((lane & (HD // 2)) == 0, -sine, sine)


def per_device(
    tokens, lengths, w_qkv, w_out, w_gate, w_up, w_down, gain_one, shift_one, gain_two, shift_two
):
    count, width = tokens.shape
    me = lax.axis_index("fsdp")
    dp = lax.axis_index("dp")
    side = dp & 1
    order = Order()

    shift, segment, position, member = pack_layout(lengths[0], count)
    sizes = lengths[0].astype(f32)[:, None]
    cosine, sine = rotary_tables(position)
    tail = segment[LONG:]
    bias = jnp.where(tail[:, None] == tail[None, :], 0.0, -1e30).astype(f32)
    device = dp * lax.axis_size("fsdp") + me
    info = jnp.stack([me, (dp >> 1) & 1, shift, device, side, dp & 7]).astype(jnp.int32)

    far_qkv = swap(w_qkv, "fsdp", 2)
    core_qkv = swap(w_qkv, "fsdp", 1)
    vectors = jnp.stack([gain_one, shift_one, gain_two, shift_two])
    core_vectors = swap(vectors, "fsdp", 1)
    far_vectors = swap(vectors, "fsdp", 2)
    half_gate = choose(cut_rows(w_gate, 2), side)
    half_up = choose(cut_rows(w_up, 2), info[1])
    half_down = choose(cut_rows(w_down, 2), side)
    several = jnp.concatenate([w_out, w_gate, w_up], axis=1)
    gate_base, up_base = w_out.shape[1], w_out.shape[1] + w_gate.shape[1]
    rolled, tokens_turned = roll_tokens(info, tokens)
    order.done(rolled, cosine, sine, bias, member, half_gate, half_up, half_down, several)

    far_qkv, core_qkv = order.after(far_qkv, core_qkv)
    order.done(far_qkv)
    far_gate = swap(order.after(half_gate), "fsdp", 2)
    core_several = swap(order.after(several), "fsdp", 1)
    core_down = swap(order.after(w_down), "fsdp", 1)
    cross_qkv = order.after(swap(far_qkv, "fsdp", 1))
    order.done(cross_qkv)
    far_vectors, core_vectors = order.after(far_vectors, core_vectors)
    order.done(far_vectors)
    joined, full_qkv = project_qkv(
        info, order.after(rolled), cosine, sine, (whole_pieces(0), (w_qkv, core_qkv, far_qkv, cross_qkv))
    )
    order.done(joined)
    far_gate, core_several, core_down = order.after(far_gate, core_several, core_down)
    order.done(far_gate)
    far_out = swap(order.after(w_out), "fsdp", 2)
    far_up = swap(order.after(half_up), "fsdp", 2)
    more_gate = swap(far_gate, "dp", 1)
    cross_gate = order.after(swap(far_gate, "fsdp", 1))
    order.done(cross_gate)
    attended, logs = attend(info, order.after(joined), bias)
    order.done(attended)
    far_out = order.after(far_out)
    order.done(far_out)
    cross_out = swap(far_out, "fsdp", 1)
    cross_vectors = swap(order.after(far_vectors), "fsdp", 1)
    more_gate = order.after(more_gate)
    order.done(more_gate)
    more_cross_gate = swap(more_gate, "fsdp", 1)
    far_up, cross_out = order.after(far_up, cross_out)
    order.done(far_up)
    more_up = swap(far_up, "dp", 2)
    cross_up = swap(far_up, "fsdp", 1)
    normed_one, root_one, attended_turned, full_out = add_branch(
        info, order.after(attended), rolled, (whole_pieces(0), (w_out, core_several, far_out, cross_out))
    )
    order.done(normed_one)
    cross_vectors, more_cross_gate, cross_up = order.after(cross_vectors, more_cross_gate, cross_up)
    gain_a, shift_a, gain_b, shift_b = join_vectors([vectors, core_vectors, far_vectors, cross_vectors], me)
    far_down = swap(order.after(half_down), "fsdp", 2)
    gate_pieces = (w_gate, core_several, far_gate, more_gate, cross_gate, more_cross_gate)
    gate, hidden_low, hidden_turned, full_gate = project_gate(
        info, order.after(normed_one), gain_a, shift_a, (half_pieces(gate_base, lowest, not_lowest), gate_pieces)
    )
    order.done(gate)
    more_up = order.after(more_up)
    order.done(more_up)
    more_cross_up = swap(more_up, "fsdp", 1)
    far_down = order.after(far_down)
    order.done(far_down)
    more_down = swap(far_down, "dp", 1)
    cross_down = swap(far_down, "fsdp", 1)
    more_cross_up = order.after(more_cross_up)
    order.done(more_cross_up)
    up_pieces = (w_up, core_several, far_up, more_up, cross_up, more_cross_up)
    inner, up, full_up = project_up(
        info, order.after(hidden_low), gate, (half_pieces(up_base, second, not_second), up_pieces)
    )
    order.done(inner)
    more_down, cross_down = order.after(more_down, cross_down)
    order.done(more_down)
    down_pieces = (w_down, core_down, far_down, more_down, cross_down, swap(more_down, "fsdp", 1))
    output, normed_two, root_two, pooled, embedding, full_down = down_and_pool(
        info, order.after(inner), normed_one, gain_a, shift_a, gain_b, shift_b, member, sizes,
        (half_pieces(0, lowest, not_lowest), down_pieces),
    )
    order.done(embedding)
    everyone = gather_blocks(embedding).reshape(-1, width)

    quarter = width // 4
    tiles = gate.shape[1] // FEED_TILE
    pairs = width // LANES // 2
    had = types.SimpleNamespace()
    down, first, later, front, back = [Unit(order) for _ in range(5)]

    def run_loss():
        had.loss, had.grad_second, had.grad_feed, had.vectors_two = loss_and_norm(
            info, everyone, pooled, embedding, sizes, member, normed_two, root_two, gain_b
        )
        order.done(had.grad_feed)

    def run_down_theirs():
        down.pieces.extend(down_gradient(info, inner, order.after(had.grad_feed), True))
        order.done(*down.pieces)

    def run_down_own():
        down.pieces.extend(down_gradient(info, order.after(inner), had.grad_feed, False))
        order.done(*down.pieces[1:])

    def run_feed(unit, held, base, steps):
        *made, had.grad_hidden = feed_back(
            info, order.after(had.grad_feed), hidden_turned, gate, up, full_down, full_gate, full_up,
            base, steps, held,
        )
        unit.pieces.extend(made)
        order.done(had.grad_hidden)

    def run_norm():
        had.grad_first, had.branch, had.grad_attended, vectors_one = first_back(
            info, order.after(had.grad_hidden), normed_one, root_one, gain_a, full_out
        )
        order.done(had.grad_attended)
        vectors = jnp.concatenate([vectors_one[:2], had.vectors_two[:2]]).astype(bf16)
        vectors = vectors.reshape(4, 4, quarter).transpose(1, 0, 2)
        vectors = jnp.stack([choose(vectors, me ^ k) for k in range(4)])
        vectors = vectors.reshape(4, 2, width // 2)
        had.vectors = jnp.pad(vectors, ((0, 0), (0, SPARE_ROWS - 2), (0, 0)))

    def run_attend(base):
        grads = attend_back(
            info, order.after(joined), attended, had.grad_attended, logs, bias, cosine, sine, base, pairs
        )
        order.done(*grads)
        return grads

    def run_front():
        front.pieces.extend(
            weight_gradients(
                info, tokens_turned, attended_turned, order.after(*had.grads_front), "front",
                had.branch, had.vectors,
            )
        )
        order.done(*front.pieces)

    def run_back():
        back.pieces.extend(
            weight_gradients(info, tokens_turned, attended_turned, order.after(*had.grads_back), "back")
        )
        order.done(*back.pieces)

    def run_tokens():
        grads = had.grads_front + had.grads_back
        had.grad_tokens = tokens_gradient(info, order.after(had.grad_first), grads, full_qkv)
        order.done(had.grad_tokens)

    def run_unroll():
        had.output = unroll(info, order.after(output))
        order.done(had.output)

    def run_down():
        had.grad_down = finish_down(info, order.after(*down.drained()))
        order.done(had.grad_down)

    def run_gates():
        values = order.after(*first.drained(), *later.drained())
        had.gates = finish_gates(info, values[:2], values[2:])
        order.done(*had.gates)

    def run_feed_first():
        run_feed(first, had.grad_second, 0, tiles // 2)

    def run_feed_later():
        run_feed(later, had.grad_hidden, tiles // 2, tiles - tiles // 2)

    def run_attend_front():
        had.grads_front = run_attend(0)

    def run_attend_back():
        had.grads_back = run_attend(pairs)

    for run in (
        run_loss, run_down_theirs, down.step, run_down_own, down.step, run_feed_first, first.step,
        run_unroll, first.step, down.step, run_feed_later, later.step, down.step, run_norm,
        later.step, first.step, down.step, run_attend_front, down.step, first.step, run_front,
        down.step, first.step, front.step, later.step, front.step, run_attend_back, front.step,
        down.step, first.step, later.step, run_back, front.step, back.step, first.step, later.step,
        back.step, run_tokens, front.step, later.step, back.step, first.step, down.step,
        front.step, later.step, back.step, front.step, back.step, later.step, front.step,
        back.step, run_down, first.step, back.step, back.step, later.step, run_gates, front.step,
        back.step,
    ):
        run()

    grad_qkv, grad_out, sums = finish(info, front.drained(), back.drained())
    sums = sums[:2].reshape(4, quarter)
    return (
        had.loss[0, 0],
        had.output,
        had.grad_tokens,
        grad_qkv,
        grad_out,
        had.gates[0],
        had.gates[1],
        had.grad_down,
        sums[0],
        sums[1],
        sums[2],
        sums[3],
    )


def solution(mesh):
    placed = (
        P(("dp", "fsdp"), None),
        P(("dp", "fsdp"), None),
        P("fsdp", None),
        P("fsdp", None),
        P("fsdp", None),
        P("fsdp", None),
        P("fsdp", None),
        P("fsdp"),
        P("fsdp"),
        P("fsdp"),
        P("fsdp"),
    )
    return jax.shard_map(
        per_device,
        mesh=mesh,
        in_specs=placed,
        out_specs=(
            P(),
            P(("dp", "fsdp"), None),
            P(("dp", "fsdp"), None),
            P("fsdp", None),
            P("fsdp", None),
            P("fsdp", None),
            P("fsdp", None),
            P("fsdp", None),
            P("fsdp"),
            P("fsdp"),
            P("fsdp"),
            P("fsdp"),
        ),
        check_vma=False,
    )
```

```python
import functools
import types

import jax
import jax.numpy as jnp
from jax import lax
from jax.experimental import pallas as pl
from jax.experimental.pallas import tpu as pltpu
from jax.sharding import PartitionSpec as P

HD = 64
PAIRS = 4
LONG = 768
LANES = 128
FEED_TILE = 512
SPARE_ROWS = 64
exact_arithmetic = lax.Precision.HIGHEST
eps_norm = 1e-05
eps_embed = 1e-06
logit_divisor = 0.05
rope_base = 1000.0
log2_e = 1.4426950408889634
f32 = jnp.float32
bf16 = jnp.bfloat16
HBM = pl.BlockSpec(memory_space=pl.ANY)


def call(body, out_shapes, *, grid, in_specs, out_specs, scratch=(), vmem, name):
    return pl.pallas_call(
        body,
        out_shape=out_shapes,
        grid_spec=pltpu.PrefetchScalarGridSpec(
            num_scalar_prefetch=1,
            grid=grid,
            in_specs=in_specs,
            out_specs=out_specs,
            scratch_shapes=list(scratch),
        ),
        compiler_params=pltpu.CompilerParams(vmem_limit_bytes=vmem * 1024 * 1024),
        cost_estimate=pl.CostEstimate(flops=10**11, bytes_accessed=10**8, transcendentals=0),
        name=name,
    )


def whole(shape):
    return pl.BlockSpec(shape, lambda *_: (0,) * len(shape))


def shaped(shape, dtype):
    return pltpu.HBM(shape, dtype)


def close(shape, dtype):
    return jax.ShapeDtypeStruct(shape, dtype)


def pinned(*values):
    return [pltpu.with_memory_space_constraint(value, pltpu.HBM) for value in values]


def matmul(left, right, left_dim=1, right_dim=0, precision=None):
    return lax.dot_general(
        left,
        right,
        (((left_dim,), (right_dim,)), ((), ())),
        precision=precision,
        preferred_element_type=f32,
    )


def start_weight(info, parts, full, sem, columns, each=False):
    for (other, cut, block, base), piece in parts:
        rows = piece.shape[0]
        start = (info[0] ^ other) * (rows * cut)
        if block is not None:
            start = start + block(info) * rows
        target = full.at[pl.ds(pl.multiple_of(start, 16), rows), columns]
        source = piece.at[:, pl.ds(base + columns.start, columns.size)]
        pltpu.make_async_copy(source, target, sem.at[other] if each else sem).start()


def wait_weight(full, sem, columns):
    pltpu.make_async_copy(full.at[:, columns], full.at[:, columns], sem).wait()


def turn_rows(info, turned, target):
    count = turned.shape[0] // 4
    for k in range(4):
        start = pl.multiple_of((info[0] ^ k) * count, 32)
        target[k] = turned[pl.ds(start, count), :]


def sigmoid(value):
    return 0.5 * jnp.tanh(0.5 * value) + 0.5


def roll_body(info, tokens, rolled, turned, scratch):
    count, width = tokens.shape
    shift = lax.rem(count - info[2], count)
    for first in range(0, width, LANES):
        lanes = pl.ds(first, LANES)
        moved = pltpu.roll(tokens[:, lanes].astype(f32), shift, 0).astype(bf16)
        rolled[:, lanes] = moved
        scratch[pl.ds(first, LANES), :] = moved.T
    turn_rows(info, scratch, turned)


def roll_tokens(info, tokens):
    count, width = tokens.shape
    return call(
        roll_body,
        (close(tokens.shape, bf16), shaped((4, width // 4, count), bf16)),
        grid=(1,),
        in_specs=[whole(tokens.shape)],
        out_specs=(whole(tokens.shape), whole((4, width // 4, count))),
        scratch=[pltpu.VMEM((width, count), bf16)],
        vmem=12,
        name="roll_tokens",
    )(info, tokens)


def unroll_body(info, value, moved):
    count = value.shape[0]
    for first in range(0, value.shape[1], LANES):
        lanes = pl.ds(first, LANES)
        moved[:, lanes] = pltpu.roll(value[:, lanes].astype(f32), info[2], 0).astype(moved.dtype)


def unroll(info, value):
    count, width = value.shape
    tile = 256
    spec = pl.BlockSpec((count, tile), lambda i, *_: (0, i))
    return call(
        unroll_body,
        shaped(value.shape, value.dtype),
        grid=(width // tile,),
        in_specs=[spec],
        out_specs=spec,
        vmem=8,
        name="unroll",
    )(info, value)


def rope_lanes(value, cosine, signed_sine):
    lane = lax.broadcasted_iota(jnp.int32, (value.shape[0], LANES), 1)
    first_half = (lane & 32) == 0
    out = []
    for start in range(0, value.shape[1], LANES):
        piece = value[:, start : start + LANES]
        partner = jnp.where(first_half, pltpu.roll(piece, LANES - 32, 1), pltpu.roll(piece, 32, 1))
        out.append(piece * cosine + partner * signed_sine)
    return out[0] if len(out) == 1 else jnp.concatenate(out, axis=1)


def qkv_body(layout, info, rolled, cosine, signed_sine, *rest):
    parts = list(zip(layout, rest))
    joined, kept, full, sems, keep_sem = rest[len(layout) :]
    step = pl.program_id(0)
    steps = pl.num_programs(0)
    tile = joined.shape[1]

    @pl.when(step == 0)
    def _():
        for j in range(full.shape[1] // tile):
            start_weight(info, parts, full, sems.at[j], pl.ds(j * tile, tile))

    columns = pl.ds(pl.multiple_of(step * tile, tile), tile)
    wait_weight(full, sems.at[step], columns)
    pltpu.make_async_copy(full.at[:, columns], kept.at[:, columns], keep_sem.at[step]).start()
    chunk = 512

    @pl.when(step < 2 * steps // 3)
    def _():
        for first in range(0, joined.shape[0], chunk):
            rows = pl.ds(first, chunk)
            product = matmul(rolled[rows, :], full[:, columns])
            turned = rope_lanes(product, cosine[rows, :], signed_sine[rows, :])
            joined[rows, :] = turned.astype(bf16)

    @pl.when(step >= 2 * steps // 3)
    def _():
        for first in range(0, joined.shape[0], chunk):
            rows = pl.ds(first, chunk)
            joined[rows, :] = matmul(rolled[rows, :], full[:, columns]).astype(bf16)

    @pl.when(step == steps - 1)
    def _():
        for j in range(full.shape[1] // tile):
            piece = pl.ds(j * tile, tile)
            pltpu.make_async_copy(full.at[:, piece], kept.at[:, piece], keep_sem.at[j]).wait()


def project_qkv(info, rolled, cosine, signed_sine, weight):
    layout, parts = weight
    count, width = rolled.shape
    columns = parts[0].shape[1]
    tile = width
    return call(
        functools.partial(qkv_body, layout),
        (shaped((count, columns), bf16), shaped((width, columns), bf16)),
        grid=(columns // tile,),
        in_specs=[whole(rolled.shape), whole(cosine.shape), whole(cosine.shape)]
        + [HBM] * len(parts),
        out_specs=(pl.BlockSpec((count, tile), lambda i, *_: (0, i)), HBM),
        scratch=[
            pltpu.VMEM((width, columns), bf16),
            pltpu.SemaphoreType.DMA((columns // tile,)),
            pltpu.SemaphoreType.DMA((columns // tile,)),
        ],
        vmem=22,
        name="project_qkv",
    )(info, rolled, cosine, signed_sine, *pinned(*parts))


def attend_body(info, query, key, value, bias, attended, logs):
    pair = pl.program_id(0)
    count = query.shape[0]
    scale = 0.125 * log2_e
    lane = lax.broadcasted_iota(jnp.int32, (1, LANES), 1)

    @pl.when(pair == 0)
    def _():
        logs[...] = jnp.zeros_like(logs)

    def rows_of(first, size, keys, offset):
        rows = pl.ds(first, size)
        ones = jnp.ones((keys.size, LANES), bf16)
        extended = jnp.concatenate([value[keys, :], ones], axis=1)
        picked = []
        kept_logs = logs[rows, :]
        for head in range(2):
            mine = (lane >= HD) if head else (lane < HD)
            masked = jnp.where(mine, query[rows, :], jnp.zeros((), bf16))
            scores = matmul(masked, key[keys, :], 1, 1) * scale
            if offset is not None:
                scores = scores + offset
            top = jnp.max(scores, axis=1, keepdims=True)
            terms = jnp.exp2(scores - top).astype(bf16)
            product = matmul(terms, extended)
            total = product[:, LANES:]
            picked.append(product[:, :LANES] / total)
            kept_logs = jnp.where(lane == 2 * pair + head, top + jnp.log2(total), kept_logs)
        attended[rows, :] = jnp.where(lane < HD, picked[0], picked[1]).astype(bf16)
        logs[rows, :] = kept_logs

    for first in range(0, LONG, 256):
        rows_of(first, 256, pl.ds(0, LONG), None)
    rest = count - LONG
    rows_of(LONG, rest, pl.ds(LONG, rest), bias[...])


def attend(info, joined, bias):
    count, columns = joined.shape
    width = columns // 3
    pairs = width // LANES
    specs = [pl.BlockSpec((count, LANES), lambda i, *_, n=n: (0, n * pairs + i)) for n in range(3)]
    return call(
        attend_body,
        (close((count, width), bf16), shaped((count, LANES), f32)),
        grid=(pairs,),
        in_specs=specs + [whole(bias.shape)],
        out_specs=(pl.BlockSpec((count, LANES), lambda i, *_: (0, i)), whole((count, LANES))),
        vmem=16,
        name="attend",
    )(info, *pinned(joined, joined, joined), bias)


def norm_parts(value):
    centered = value - jnp.mean(value, axis=1, keepdims=True)
    root = lax.rsqrt(jnp.mean(centered * centered, axis=1, keepdims=True) + eps_norm)
    return centered * root, root


def branch_body(layout, info, attended, rolled, *rest):
    parts = list(zip(layout, rest))
    normed, root, turned, kept, full, scratch, sem, keep_sem = rest[len(layout) :]
    step = pl.program_id(0)

    @pl.when(step == 0)
    def _():
        start_weight(info, parts, full, sem, pl.ds(0, full.shape[1]))
        wait_weight(full, sem, pl.ds(0, full.shape[1]))
        pltpu.make_async_copy(full, kept, keep_sem).start()

    first = rolled[...].astype(f32) + matmul(attended[...], full[...])
    value, inverse = norm_parts(first)
    normed[...] = value
    root[...] = jnp.broadcast_to(inverse, root.shape)
    scratch[...] = attended[...].T
    turn_rows(info, scratch, turned)

    @pl.when(step == pl.num_programs(0) - 1)
    def _():
        pltpu.make_async_copy(full, kept, keep_sem).wait()


def add_branch(info, attended, rolled, weight):
    layout, parts = weight
    count, width = attended.shape
    tile = 256
    rows = pl.BlockSpec((tile, width), lambda i, *_: (i, 0))
    return call(
        functools.partial(branch_body, layout),
        (
            shaped((count, width), f32),
            shaped((count, LANES), f32),
            shaped((4, width // 4, count), bf16),
            shaped((width, width), bf16),
        ),
        grid=(count // tile,),
        in_specs=[rows, rows] + [HBM] * len(parts),
        out_specs=(
            rows,
            pl.BlockSpec((tile, LANES), lambda i, *_: (i, 0)),
            pl.BlockSpec((4, width // 4, tile), lambda i, *_: (0, 0, i)),
            HBM,
        ),
        scratch=[
            pltpu.VMEM((width, width), bf16),
            pltpu.VMEM((width, tile), bf16),
            pltpu.SemaphoreType.DMA,
            pltpu.SemaphoreType.DMA,
        ],
        vmem=14,
        name="add_branch",
    )(info, *pinned(attended, rolled, *parts))


def gate_body(layout, info, normed, gain, shift, *rest):
    parts = list(zip(layout, rest))
    gate, hidden, turned, kept, full, low, scratch, sems, keep_sems = rest[len(layout) :]
    step = pl.program_id(0)
    tile = gate.shape[1]
    tiles = full.shape[1] // tile
    chunk = 512

    @pl.when(step == 0)
    def _():
        for j in range(tiles):
            start_weight(info, parts, full, sems.at[j], pl.ds(j * tile, tile))
        for first in range(0, low.shape[0], chunk):
            rows = pl.ds(first, chunk)
            value = (normed[rows, :] * gain[...] + shift[...]).astype(bf16)
            low[rows, :] = value
            scratch[:, rows] = value.T
        hidden[...] = low[...]
        turn_rows(info, scratch, turned)

    columns = pl.ds(pl.multiple_of(step * tile, tile), tile)
    wait_weight(full, sems.at[step], columns)
    pltpu.make_async_copy(full.at[:, columns], kept.at[:, columns], keep_sems.at[step]).start()
    for first in range(0, low.shape[0], chunk):
        rows = pl.ds(first, chunk)
        gate[rows, :] = matmul(low[rows, :], full[:, columns]).astype(bf16)

    @pl.when(step == tiles - 1)
    def _():
        for j in range(tiles):
            piece = pl.ds(j * tile, tile)
            pltpu.make_async_copy(full.at[:, piece], kept.at[:, piece], keep_sems.at[j]).wait()


def project_gate(info, normed, gain, shift, weight):
    layout, parts = weight
    count, width = normed.shape
    hidden = parts[0].shape[1]
    tile = 512
    columns = pl.BlockSpec((count, tile), lambda i, *_: (0, i))
    return call(
        functools.partial(gate_body, layout),
        (
            shaped((count, hidden), bf16),
            close((count, width), bf16),
            shaped((4, width // 4, count), bf16),
            shaped((width, hidden), bf16),
        ),
        grid=(hidden // tile,),
        in_specs=[whole(normed.shape), whole(gain.shape), whole(shift.shape)]
        + [HBM] * len(layout),
        out_specs=(columns, whole((count, width)), whole((4, width // 4, count)), HBM),
        scratch=[
            pltpu.VMEM((width, hidden), bf16),
            pltpu.VMEM((count, width), bf16),
            pltpu.VMEM((width, count), bf16),
            pltpu.SemaphoreType.DMA((hidden // tile,)),
            pltpu.SemaphoreType.DMA((hidden // tile,)),
        ],
        vmem=26,
        name="project_gate",
    )(info, *pinned(normed), gain, shift, *pinned(*parts))


def up_body(layout, info, low, gate, *rest):
    parts = list(zip(layout, rest))
    inner, up_out, kept, full, sems, keep_sems = rest[len(layout) :]
    step = pl.program_id(0)
    tile = inner.shape[1]
    tiles = full.shape[1] // tile
    chunk = 512

    @pl.when(step == 0)
    def _():
        for j in range(tiles):
            start_weight(info, parts, full, sems.at[j], pl.ds(j * tile, tile))

    columns = pl.ds(pl.multiple_of(step * tile, tile), tile)
    wait_weight(full, sems.at[step], columns)
    pltpu.make_async_copy(full.at[:, columns], kept.at[:, columns], keep_sems.at[step]).start()
    for first in range(0, low.shape[0], chunk):
        rows = pl.ds(first, chunk)
        up = matmul(low[rows, :], full[:, columns])
        up_out[rows, :] = up.astype(bf16)
        value = gate[rows, :].astype(f32)
        inner[rows, :] = (value * up * sigmoid(value)).astype(bf16)

    @pl.when(step == tiles - 1)
    def _():
        for j in range(tiles):
            piece = pl.ds(j * tile, tile)
            pltpu.make_async_copy(full.at[:, piece], kept.at[:, piece], keep_sems.at[j]).wait()


def project_up(info, low, gate, weight):
    layout, parts = weight
    count, width = low.shape
    hidden = parts[0].shape[1]
    tile = 512
    columns = pl.BlockSpec((count, tile), lambda i, *_: (0, i))
    return call(
        functools.partial(up_body, layout),
        (
            shaped((count, hidden), bf16),
            shaped((count, hidden), bf16),
            shaped((width, hidden), bf16),
        ),
        grid=(hidden // tile,),
        in_specs=[whole(low.shape), columns] + [HBM] * len(layout),
        out_specs=(columns, columns, HBM),
        scratch=[
            pltpu.VMEM((width, hidden), bf16),
            pltpu.SemaphoreType.DMA((hidden // tile,)),
            pltpu.SemaphoreType.DMA((hidden // tile,)),
        ],
        vmem=24,
        name="project_up",
    )(info, low, *pinned(gate, *parts))


def down_body(layout, info, inner, normed, gain_one, shift_one, gain, shift, member, sizes, *rest):
    parts = list(zip(layout, rest))
    output, normed_two, root, pooled, embedding, kept, full, feed, sems, keep_sem = rest[len(layout) :]
    step = pl.program_id(0)
    steps = pl.num_programs(0)
    tile = output.shape[0]
    quarter = full.shape[0] // 4

    @pl.when(step == 0)
    def _():
        start_weight(info, parts, full, sems, pl.ds(0, full.shape[1]), each=True)
        pooled[...] = jnp.zeros_like(pooled)
        for other in range(4):
            rows = pl.ds(pl.multiple_of((info[0] ^ other) * quarter, quarter), quarter)
            pltpu.make_async_copy(full.at[rows, :], full.at[rows, :], sems.at[other]).wait()
            product = matmul(inner[:, rows], full[rows, :])
            feed[...] = product if other == 0 else feed[...] + product
        pltpu.make_async_copy(full, kept, keep_sem).start()

    @pl.when(step > 0)
    def _():
        feed[...] = matmul(inner[...], full[...])

    hidden = normed[...] * gain_one[...] + shift_one[...]
    value, inverse = norm_parts(hidden + feed[...])
    normed_two[...] = value
    root[...] = jnp.broadcast_to(inverse, root.shape)
    result = value * gain[...] + shift[...]
    output[...] = result.astype(bf16)

    @pl.when(step < LONG // tile)
    def _():
        pooled[0:1, :] += jnp.sum(result, axis=0, keepdims=True)

    @pl.when(step == steps - 1)
    def _():
        longest = jnp.where(sizes[...] == LONG, pooled[0:1, :], 0.0)
        total = (longest + matmul(member[...], result, 0, 0, exact_arithmetic)) / sizes[...]
        pooled[...] = total
        square = jnp.sum(total * total, axis=1, keepdims=True)
        embedding[...] = total * lax.rsqrt(square + eps_embed)
        pltpu.make_async_copy(full, kept, keep_sem).wait()


def down_and_pool(info, inner, normed, gain_one, shift_one, gain, shift, member, sizes, weight):
    layout, parts = weight
    count, width = normed.shape
    hidden = inner.shape[1]
    seqs = member.shape[1]
    tile = 256
    rows = pl.BlockSpec((tile, width), lambda i, *_: (i, 0))
    vector = whole((1, width))
    return call(
        functools.partial(down_body, layout),
        (
            shaped((count, width), bf16),
            shaped((count, width), f32),
            shaped((count, LANES), f32),
            close((seqs, width), f32),
            close((seqs, width), f32),
            shaped((hidden, width), bf16),
        ),
        grid=(count // tile,),
        in_specs=[
            pl.BlockSpec((tile, hidden), lambda i, *_: (i, 0)),
            rows,
            vector,
            vector,
            vector,
            vector,
            pl.BlockSpec((tile, seqs), lambda i, *_: (LONG // tile, 0)),
            whole(sizes.shape),
        ]
        + [HBM] * len(parts),
        out_specs=(
            rows,
            rows,
            pl.BlockSpec((tile, LANES), lambda i, *_: (i, 0)),
            whole((seqs, width)),
            whole((seqs, width)),
            HBM,
        ),
        scratch=[
            pltpu.VMEM((hidden, width), bf16),
            pltpu.VMEM((tile, width), f32),
            pltpu.SemaphoreType.DMA((4,)),
            pltpu.SemaphoreType.DMA,
        ],
        vmem=24,
        name="down_and_pool",
    )(info, *pinned(inner, normed), gain_one, shift_one, gain, shift, member, sizes, *pinned(*parts))


def loss_body(info, everyone, pooled, embedding, sizes, member, normed, root, gain, *rest):
    loss, grad_second, grad_feed, vectors, pulled, upstreams = rest
    step = pl.program_id(0)
    seqs, width = embedding.shape
    pairs = seqs // 2

    @pl.when(step == 0)
    def _():
        devices = everyone.shape[0] // seqs
        count = devices * pairs
        blocks = everyone[...].reshape(devices, seqs, width)
        requests = blocks[:, :pairs].reshape(count, width)
        passages = blocks[:, pairs:].reshape(count, width)
        sims = matmul(requests, passages, 1, 1, exact_arithmetic) * (1.0 / logit_divisor)
        top = jnp.max(sims, axis=1, keepdims=True)
        terms = jnp.exp(sims - top)
        total = jnp.sum(terms, axis=1, keepdims=True)
        row = lax.broadcasted_iota(jnp.int32, sims.shape, 0)
        column = lax.broadcasted_iota(jnp.int32, sims.shape, 1)
        diagonal = jnp.sum(jnp.where(row == column, sims, 0.0), axis=1, keepdims=True)
        mean = jnp.sum(top + jnp.log(total) - diagonal, axis=0, keepdims=True) / count
        loss[...] = jnp.broadcast_to(mean, loss.shape)
        pulls = terms / total
        first = info[3] * pairs
        near = lax.broadcasted_iota(jnp.int32, (seqs, count), 0)
        place = lax.broadcasted_iota(jnp.int32, (seqs, count), 1)
        picked = jnp.where(place == first + near, 1.0, 0.0)
        my_rows = matmul(picked, pulls, 1, 0, exact_arithmetic)
        my_columns = matmul(picked, pulls, 1, 1, exact_arithmetic)
        to_requests = matmul(my_rows, passages, 1, 0, exact_arithmetic)
        to_passages = matmul(my_columns, requests, 1, 0, exact_arithmetic)
        own = embedding[...]
        swapped = jnp.concatenate([own[pairs:], own[:pairs]], axis=0)
        gathered = jnp.concatenate([to_requests[:pairs], to_passages[:pairs]], axis=0)
        grad_embed = (gathered - swapped) * (1.0 / (logit_divisor * count))
        means = pooled[...]
        inverse = lax.rsqrt(jnp.sum(means * means, axis=1, keepdims=True) + eps_embed)
        along = jnp.sum(means * grad_embed, axis=1, keepdims=True)
        pulled[...] = (inverse * grad_embed - inverse * inverse * inverse * means * along) / sizes[
            ...
        ]
        vectors[...] = jnp.zeros_like(vectors)

    @pl.when(step < LONG // normed.shape[0])
    def _():
        longest = jnp.sum(jnp.where(sizes[...] == LONG, pulled[...], 0.0), axis=0, keepdims=True)
        upstreams[...] = jnp.broadcast_to(longest, upstreams.shape)

    @pl.when(step >= LONG // normed.shape[0])
    def _():
        upstreams[...] = matmul(member[...], pulled[...], 1, 0, exact_arithmetic)

    upstream = upstreams[...]
    value = normed[...]
    vectors[0:1, :] += jnp.sum(upstream * value, axis=0, keepdims=True)
    vectors[1:2, :] += jnp.sum(upstream, axis=0, keepdims=True)
    result = norm_back(upstream, value, root[:, :1], gain[...])
    grad_second[...] = result
    grad_feed[...] = result.astype(bf16)


def norm_back(upstream, normed, root, gain):
    scaled = upstream * gain
    return root * (
        scaled
        - jnp.mean(scaled, axis=1, keepdims=True)
        - normed * jnp.mean(scaled * normed, axis=1, keepdims=True)
    )


def loss_and_norm(info, everyone, pooled, embedding, sizes, member, normed, root, gain):
    count, width = normed.shape
    seqs = member.shape[1]
    tile = 256
    rows = pl.BlockSpec((tile, width), lambda i, *_: (i, 0))
    return call(
        loss_body,
        (
            close((8, LANES), f32),
            shaped((count, width), f32),
            close((count, width), bf16),
            close((8, width), f32),
        ),
        grid=(count // tile,),
        in_specs=[
            whole(everyone.shape),
            whole(pooled.shape),
            whole(embedding.shape),
            whole(sizes.shape),
            pl.BlockSpec((tile, seqs), lambda i, *_: (i, 0)),
            rows,
            pl.BlockSpec((tile, LANES), lambda i, *_: (i, 0)),
            whole(gain.shape),
        ],
        out_specs=(whole((8, LANES)), rows, rows, whole((8, width))),
        scratch=[pltpu.VMEM((seqs, width), f32), pltpu.VMEM((tile, width), f32)],
        vmem=16 + everyone.shape[0] * width * 24 // 2**20,
        name="loss_and_norm",
    )(info, everyone, pooled, embedding, sizes, member, *pinned(normed, root), gain)


def outer_body(theirs, info, left, right, *outs):
    step = pl.program_id(0)
    product = matmul(left[...], right[...], 0, 0).astype(bf16)
    rows = product.shape[0] // 8
    for block in range(8):
        source = slice(block * rows, (block + 1) * rows)
        target = pl.ds(pl.multiple_of(relative_block(info, block) * rows, 16), rows)
        if theirs:
            outs[0][0, target, :] = product[source]
            continue
        for index, out in enumerate(outs):

            @pl.when(step == index)
            def _():
                out[target, :] = product[source]


def down_gradient(info, inner, grad_feed, theirs):
    count, hidden = inner.shape
    width = grad_feed.shape[1]
    rows = hidden // 4
    first, last = (3, 1) if theirs else (2, 0)

    def column(i, info):
        return (0, info[0] ^ jnp.where(i == 0, first, last))

    if theirs:
        outs = (shaped((2, rows, width), bf16),)
        specs = (pl.BlockSpec((1, rows, width), lambda i, *_: (i, 0, 0)),)
    else:
        outs = (shaped((rows, width), bf16),) * 2
        specs = (whole((rows, width)),) * 2
    return call(
        functools.partial(outer_body, theirs),
        outs,
        grid=(2,),
        in_specs=[pl.BlockSpec((count, rows), column), whole(grad_feed.shape)],
        out_specs=specs,
        vmem=20,
        name="down_theirs" if theirs else "down_own",
    )(info, *pinned(inner), grad_feed)


def piece_shapes(rows, columns):
    own = shaped((rows, columns), bf16)
    return shaped((2, rows, columns), bf16), own, own


def piece_specs(rows, tile):
    own = pl.BlockSpec((rows, tile), lambda i, *_: (0, i))
    return pl.BlockSpec((2, rows, tile), lambda i, *_: (0, 0, i)), own, own


def relative_block(info, block):
    place = block ^ info[5]
    return ((place & 1) << 2) | (place & 2) | (place >> 2)


def multiply_into(held, turned, grads, first):
    _, quarter, count = turned.shape
    grad = grads[0] if len(grads) == 1 else jnp.concatenate(grads, axis=1)
    products = matmul(turned[...].reshape(4 * quarter, count), grad).astype(bf16)
    width = held.shape[2]
    for index in range(len(grads)):
        rows = pl.ds((first + index) * quarter, quarter)
        for place in range(4):
            part = slice(place * quarter, (place + 1) * quarter)
            held[place, rows, :] = products[part, index * width : (index + 1) * width]


def write_pieces(info, held, theirs, far, near):
    rows = held.shape[1] // 8
    for block in range(8):
        source = slice(block * rows, (block + 1) * rows)
        target = pl.ds(pl.multiple_of(relative_block(info, block) * rows, 16), rows)
        near[target, :] = held[0, source, :]
        theirs[1, target, :] = held[1, source, :]
        far[target, :] = held[2, source, :]
        theirs[0, target, :] = held[3, source, :]


def feed_body(info, grad_feed, turned, gate_in, up_in, down, gate_full, up_full, held, *outs):
    *pieces, grad_hidden, products, turned_here, held_here, total, turned_sem, held_sem, out_sems = outs
    step = pl.program_id(0)
    last = step == pl.num_programs(0) - 1
    count = grad_feed.shape[0]
    chunk = 512
    gates, ups = [], []
    turned_copy = pltpu.make_async_copy(turned, turned_here, turned_sem)
    held_copy = pltpu.make_async_copy(held, held_here, held_sem)

    def out_copy(index):
        rows = pl.ds(index * chunk, chunk)
        return pltpu.make_async_copy(total.at[rows, :], grad_hidden.at[rows, :], out_sems.at[index])

    @pl.when(step == 0)
    def _():
        turned_copy.start()
        held_copy.start()
        total[...] = jnp.zeros_like(total)

    @pl.when(last)
    def _():
        held_copy.wait()
        total[...] += held_here[...]

    for index in range(count // chunk):
        rows = pl.ds(index * chunk, chunk)
        grad_inner = matmul(grad_feed[rows, :], down[...], 1, 1)
        gate = gate_in[rows, :].astype(f32)
        up = up_in[rows, :].astype(f32)
        share = sigmoid(gate)
        scaled = grad_inner * share
        grad_gate = (scaled * up * (1.0 + gate * (1.0 - share))).astype(bf16)
        grad_up = (scaled * gate).astype(bf16)
        gates.append(grad_gate)
        ups.append(grad_up)
        total[rows, :] += matmul(grad_gate, gate_full[...], 1, 1) + matmul(grad_up, up_full[...], 1, 1)

        @pl.when(last)
        def _():
            out_copy(index).start()

    @pl.when(step == 0)
    def _():
        turned_copy.wait()

    for which, grads in ((0, gates), (1, ups)):
        multiply_into(products, turned_here, [jnp.concatenate(grads, axis=0)], which)
    write_pieces(info, products, *pieces)

    @pl.when(last)
    def _():
        for index in range(count // chunk):
            out_copy(index).wait()


def feed_back(info, grad_feed, turned, gate, up, down, gate_full, up_full, base, steps, held):
    count = gate.shape[0]
    width = grad_feed.shape[1]
    quarter = width // 4
    tile = FEED_TILE
    columns = pl.BlockSpec((count, tile), lambda i, *_: (0, base + i))
    weights = pl.BlockSpec((width, tile), lambda i, *_: (0, base + i))
    return call(
        feed_body,
        piece_shapes(2 * quarter, steps * tile) + (shaped((count, width), f32),),
        grid=(steps,),
        in_specs=[
            whole(grad_feed.shape),
            HBM,
            columns,
            columns,
            pl.BlockSpec((tile, width), lambda i, *_: (base + i, 0)),
            weights,
            weights,
            HBM,
        ],
        out_specs=piece_specs(2 * quarter, tile) + (HBM,),
        scratch=[
            pltpu.VMEM((4, 2 * quarter, tile), bf16),
            pltpu.VMEM(turned.shape, bf16),
            pltpu.VMEM((count, width), f32),
            pltpu.VMEM((count, width), f32),
            pltpu.SemaphoreType.DMA,
            pltpu.SemaphoreType.DMA,
            pltpu.SemaphoreType.DMA((2,)),
        ],
        vmem=40,
        name=f"feed_back_{base}",
    )(info, grad_feed, *pinned(turned, gate, up, down, gate_full, up_full, held))


def first_body(info, grad_hidden, normed, root, gain, weight, *outs):
    grad_first, branch, grad_attended, vectors = outs

    @pl.when(pl.program_id(0) == 0)
    def _():
        vectors[...] = jnp.zeros_like(vectors)

    upstream = grad_hidden[...]
    value = normed[...]
    vectors[0:1, :] += jnp.sum(upstream * value, axis=0, keepdims=True)
    vectors[1:2, :] += jnp.sum(upstream, axis=0, keepdims=True)
    result = norm_back(upstream, value, root[:, :1], gain[...])
    grad_first[...] = result
    low = result.astype(bf16)
    branch[...] = low
    grad_attended[...] = matmul(low, weight[...], 1, 1).astype(bf16)


def first_back(info, grad_hidden, normed, root, gain, weight):
    count, width = normed.shape
    tile = 256
    rows = pl.BlockSpec((tile, width), lambda i, *_: (i, 0))
    return call(
        first_body,
        (
            shaped((count, width), f32),
            shaped((count, width), bf16),
            shaped((count, width), bf16),
            close((8, width), f32),
        ),
        grid=(count // tile,),
        in_specs=[
            rows,
            rows,
            pl.BlockSpec((tile, LANES), lambda i, *_: (i, 0)),
            whole(gain.shape),
            whole(weight.shape),
        ],
        out_specs=(rows, rows, rows, whole((8, width))),
        vmem=20,
        name="first_back",
    )(info, *pinned(grad_hidden, normed, root), gain, weight)


def attend_back_body(base, info, query, key, value, attended, upstream, logs, bias, cosine, sine, *rest):
    (grad_query, grad_key, grad_value, logs_row, sums) = rest
    pair = base + pl.program_id(0)
    count = query.shape[0]
    scale = 0.125 * log2_e
    lane = lax.broadcasted_iota(jnp.int32, (1, LANES), 1)

    @pl.when(pl.program_id(0) == 0)
    def _():
        logs_row[...] = logs[...].T

    both = upstream[...].astype(f32) * attended[...].astype(f32)
    row = lax.broadcasted_iota(jnp.int32, (8, LANES), 0)
    column = lax.broadcasted_iota(jnp.int32, (8, LANES), 1)
    chooser = jnp.where((column // HD) == row, 1.0, 0.0)
    sums[...] = matmul(chooser, both, 1, 1, exact_arithmetic)

    zero = jnp.zeros((), bf16)
    for first, size, offset in ((0, LONG, None), (LONG, count - LONG, bias)):
        rows = pl.ds(first, size)
        key_rows, query_rows, up_rows = key[rows, :], query[rows, :], upstream[rows, :]
        key_grad = value_grad = query_grad = None
        for head in range(2):
            mine = (lane >= HD) if head else (lane < HD)
            masked_query = jnp.where(mine, query_rows, zero)
            masked_up = jnp.where(mine, up_rows, zero)
            masked_key = jnp.where(mine, key_rows, zero)
            log_row = logs_row[pl.ds(2 * pair + head, 1), rows]
            sum_row = sums[head : head + 1, rows]
            key_pieces, value_pieces = [], []
            query_total = None
            for start in range(first, first + size, 256):
                keys = pl.ds(start, 256)
                scores = matmul(key[keys, :], masked_query, 1, 1) * scale
                if offset is not None:
                    scores = scores + offset[...]
                probs = jnp.exp2(scores - log_row)
                grad_probs = matmul(value[keys, :], masked_up, 1, 1)
                grad_scores = (probs * (grad_probs - sum_row)).astype(bf16)
                value_pieces.append(matmul(probs.astype(bf16), masked_up))
                key_pieces.append(matmul(grad_scores, masked_query))
                kept_key = masked_key[start - first : start - first + 256]
                piece = matmul(grad_scores, kept_key, 0, 0)
                query_total = piece if query_total is None else query_total + piece
            key_head = jnp.concatenate(key_pieces, axis=0)
            value_head = jnp.concatenate(value_pieces, axis=0)
            key_grad = key_head if key_grad is None else key_grad + key_head
            value_grad = value_head if value_grad is None else value_grad + value_head
            query_grad = query_total if query_grad is None else query_grad + query_total
        turn_cos, turn_sin = cosine[rows, :], sine[rows, :]
        for grad, target in ((query_grad, grad_query), (key_grad, grad_key)):
            low = (grad * 0.125).astype(bf16).astype(f32)
            target[rows, :] = rope_lanes(low, turn_cos, -turn_sin).astype(bf16)
        grad_value[rows, :] = value_grad.astype(bf16)


def attend_back(info, joined, attended, upstream, logs, bias, cosine, sine, base, pairs):
    count, columns = joined.shape
    every = columns // 3 // LANES
    specs = [
        pl.BlockSpec((count, LANES), lambda i, *_, n=n: (0, n * every + base + i)) for n in range(3)
    ]
    block = pl.BlockSpec((count, LANES), lambda i, *_: (0, base + i))
    return call(
        functools.partial(attend_back_body, base),
        (close((count, pairs * LANES), bf16),) * 3,
        grid=(pairs,),
        in_specs=specs
        + [block, block, whole(logs.shape), whole(bias.shape)]
        + [whole(cosine.shape)] * 2,
        out_specs=(pl.BlockSpec((count, LANES), lambda i, *_: (0, i)),) * 3,
        scratch=[pltpu.VMEM((LANES, count), f32), pltpu.VMEM((8, count), f32)],
        vmem=32,
        name=f"attend_back_{base}",
    )(info, *pinned(joined, joined, joined, attended, upstream), logs, bias, cosine, sine)


def turned_body(info, turned_a, turned_b, *rest):
    grads, pieces, held = rest[:-4], rest[-4:-1], rest[-1]
    used = len(grads) * turned_a.shape[1]
    spare = held.shape[1] - used
    if len(grads) > 3:
        extra = grads[-1]
        grads = grads[:-1]
        used = len(grads) * turned_a.shape[1]
        held[:, used:, :] = extra[...]
    else:
        held[:, used:, :] = jnp.zeros((4, spare, held.shape[2]), bf16)
    for turned, first, several in ((turned_a, 0, grads[:3]), (turned_b, 3, grads[3:])):
        if several:
            multiply_into(held, turned, [grad[...] for grad in several], first)
    write_pieces(info, held, *pieces)


def weight_gradients(info, turned_a, turned_b, grads, name, branch=None, extra=None):
    _, quarter, count = turned_a.shape
    width = grads[0].shape[1]
    tile = LANES
    specs = [pl.BlockSpec((count, tile), lambda i, *_: (0, i))] * len(grads)
    rows = len(grads) * quarter + SPARE_ROWS
    args = list(grads)
    if branch is not None:
        specs += [
            pl.BlockSpec((count, tile), lambda i, *_, n=n: (0, n * width // tile + i)) for n in range(2)
        ]
        specs.append(pl.BlockSpec((4, SPARE_ROWS, tile), lambda i, *_: (0, 0, i)))
        args += [branch, branch, extra]
        rows += 2 * quarter
    return call(
        turned_body,
        piece_shapes(rows, width),
        grid=(width // tile,),
        in_specs=[whole(turned_a.shape), whole(turned_b.shape)] + specs,
        out_specs=piece_specs(rows, tile),
        scratch=[pltpu.VMEM((4, rows, tile), bf16)],
        vmem=22,
        name=name,
    )(info, *pinned(turned_a, turned_b, *args))


def tokens_body(info, grad_first, weight, *rest):
    grads, out = rest[:-1], rest[-1]
    total = grad_first[...]
    width = grads[0].shape[1]
    for part in range(2):
        for index in range(3):
            first = (2 * index + part) * width
            grad = grads[3 * part + index]
            total = total + matmul(grad[...], weight[:, first : first + width], 1, 1)
    out[...] = pltpu.roll(total, info[2], 0)


def tokens_gradient(info, grad_first, grads, weight):
    count, width = grad_first.shape
    tile = 256
    block = pl.BlockSpec((count, tile), lambda i, *_: (0, i))
    return call(
        tokens_body,
        shaped((count, width), f32),
        grid=(width // tile,),
        in_specs=[block, pl.BlockSpec((tile, weight.shape[1]), lambda i, *_: (i, 0))]
        + [whole(grad.shape) for grad in grads],
        out_specs=block,
        vmem=26,
        name="tokens_gradient",
    )(info, grad_first, weight, *grads)


def settle(info, mine, other, held, target):
    half = mine.shape[0]
    held[:half, :] = mine[...].astype(f32)
    held[half:, :] = other[...].astype(f32)
    rows = half // 4
    for block in range(8):
        source = pl.ds(pl.multiple_of(relative_block(info, block) * rows, 8), rows)
        target[block * rows : (block + 1) * rows, :] = held[source, :]


def finish_body(info, front_a, front_b, back_a, back_b, grad_qkv, grad_out, vectors, *scratch):
    quarter, width = grad_out.shape
    half = width // 2
    front_held, front, back_held, back = scratch
    settle(info, front_a, front_b, front_held, front)
    settle(info, back_a, back_b, back_held, back)
    for index in range(3):
        rows = slice(index * quarter, (index + 1) * quarter)
        grad_qkv[:, index * width : index * width + half] = front[rows, :]
        grad_qkv[:, index * width + half : (index + 1) * width] = back[rows, :]
    grad_out[:, :half] = front[3 * quarter : 4 * quarter, :]
    grad_out[:, half:] = front[4 * quarter : 5 * quarter, :]
    vectors[...] = front[5 * quarter : 5 * quarter + 8, :]


def finish(info, front, back):
    half = front[0].shape[1]
    rows, back_rows = 2 * front[0].shape[0], 2 * back[0].shape[0]
    quarter = (rows - SPARE_ROWS) // 5
    shapes = ((quarter, 6 * half), (quarter, 2 * half), (8, half))
    return call(
        finish_body,
        tuple(close(shape, f32) for shape in shapes),
        grid=(1,),
        in_specs=[whole(value.shape) for value in (*front, *back)],
        out_specs=tuple(whole(shape) for shape in shapes),
        scratch=[pltpu.VMEM((count, half), f32) for count in (rows, rows, back_rows, back_rows)],
        vmem=20,
        name="finish",
    )(info, *front, *back)


def gates_body(info, first_a, first_b, later_a, later_b, grad_gate, grad_up, held, target):
    quarter = grad_gate.shape[0]
    start = 0
    for mine, other in ((first_a, first_b), (later_a, later_b)):
        settle(info, mine, other, held, target)
        columns = slice(start, start + mine.shape[1])
        grad_gate[:, columns] = target[:quarter, :]
        grad_up[:, columns] = target[quarter:, :]
        start += mine.shape[1]


def finish_gates(info, first, later):
    half, columns = first[0].shape
    shape = (half, 2 * columns)
    return call(
        gates_body,
        (shaped(shape, f32),) * 2,
        grid=(1,),
        in_specs=[whole(first[0].shape)] * 4,
        out_specs=(whole(shape),) * 2,
        scratch=[pltpu.VMEM((2 * half, columns), f32)] * 2,
        vmem=28,
        name="finish_gates",
    )(info, *pinned(*first, *later))


def settle_down_body(info, mine, other, grad_down, held):
    settle(info, mine, other, held, grad_down)


def finish_down(info, down):
    half, columns = down[0].shape
    shape = (2 * half, columns)
    return call(
        settle_down_body,
        shaped(shape, f32),
        grid=(1,),
        in_specs=[whole(down[0].shape)] * 2,
        out_specs=whole(shape),
        scratch=[pltpu.VMEM(shape, f32)],
        vmem=16,
        name="finish_down",
    )(info, *pinned(*down))


def swap(value, axis, bit):
    size = lax.axis_size(axis)
    return lax.ppermute(value, axis, [(i, i ^ bit) for i in range(size)])


def choose(value, index):
    return lax.dynamic_index_in_dim(value, index, 0, keepdims=False)


def low_sum(*terms):
    total = terms[0].astype(f32)
    for term in terms[1:]:
        total = total + term.astype(f32)
    return total.astype(bf16)


class Order:
    def __init__(self):
        self.last = ()

    def after(self, *values):
        if self.last:
            values = lax.optimization_barrier((*values, *self.last))[: len(values)]
        return values[0] if len(values) == 1 else values

    def done(self, *values):
        self.last = values


def cut_rows(shard, blocks):
    rows, columns = shard.shape
    return shard.reshape(blocks, rows // blocks, columns)


def lowest(info):
    return info[4]


def not_lowest(info):
    return 1 - info[4]


def second(info):
    return info[1]


def not_second(info):
    return 1 - info[1]


def whole_pieces(base):
    return ((0, 1, None, 0), (1, 1, None, base), (2, 1, None, 0), (3, 1, None, 0))


def half_pieces(base, here, there):
    far = tuple((place, 2, block, 0) for place in (2, 3) for block in (here, there))
    return ((0, 1, None, 0), (1, 1, None, base)) + far


def join_vectors(pieces, me):
    pieces = jnp.stack(pieces)
    full = jnp.concatenate([choose(pieces, me ^ q) for q in range(4)], axis=1)
    return [full[i : i + 1].astype(f32) for i in range(full.shape[0])]


def gather_blocks(block):
    dp_size, fsdp_size = lax.axis_size("dp"), lax.axis_size("fsdp")
    bits = dp_size.bit_length() - 1
    held = block[None]
    for bit in reversed(range(bits)):
        other = swap(held, "dp", 1 << bit)
        low = ((lax.axis_index("dp") >> bit) & 1) == 0
        held = jnp.where(low, jnp.stack([held, other]), jnp.stack([other, held]))
        held = held.reshape((-1,) + block.shape)
    held = held.reshape((2,) * bits + block.shape)
    held = held.transpose(tuple(range(bits))[::-1] + tuple(range(bits, bits + block.ndim)))
    held = held.reshape((dp_size,) + block.shape)
    held = lax.all_gather(held, "fsdp", axis=1)
    return held.reshape((dp_size * fsdp_size,) + block.shape)


def reduce_steps(order, pieces):
    bits = lax.axis_size("dp").bit_length() - 1
    from_core = swap(order.after(pieces[0]), "fsdp", 1)
    yield None
    far, near = pieces[1:]
    far, from_core = order.after(far, from_core)
    total = low_sum(far, from_core[0])
    order.done(total)
    from_far = swap(total, "fsdp", 2)
    yield None
    terms = order.after(near, from_core, from_far)
    terms = [terms[0], terms[1][1], terms[2]]
    rows = near.shape[0]
    for step in range(3):
        rows //= 2
        send = low_sum(*[term[rows : 2 * rows] for term in terms])
        order.done(send)
        other = swap(send, "dp", 1 << step)
        yield None
        terms = list(order.after(near, from_core, from_far, *terms[3:], other))
        terms[1] = terms[1][1]
    held = low_sum(*[term[:rows] for term in terms])
    for step in range(3, bits):
        order.done(held)
        other = swap(held, "dp", 1 << step)
        yield None
        held = low_sum(*order.after(held, other))
    for step in (2, 1, 0):
        order.done(held)
        other = swap(held, "dp", 1 << step)
        yield None
        held, other = order.after(held, other)
        if step:
            held = jnp.concatenate([held, other])
    order.done(held, other)
    yield held, other


class Unit:
    def __init__(self, order):
        self.pieces = []
        self.steps = reduce_steps(order, self.pieces)
        self.result = None

    def step(self):
        if self.result is None:
            self.result = next(self.steps)

    def drained(self):
        while self.result is None:
            self.step()
        return self.result


def pack_layout(lengths_row, count):
    ends = jnp.cumsum(lengths_row)
    starts = ends - lengths_row
    shift = jnp.sum(jnp.where(lengths_row == LONG, starts, 0))
    places = lax.rem(lax.iota(jnp.int32, count) + shift, count)
    segment = jnp.sum((places[:, None] >= ends[None, :]).astype(jnp.int32), axis=1)
    member = segment[:, None] == lax.iota(jnp.int32, lengths_row.shape[0])[None, :]
    offset = jnp.sum(jnp.where(member, starts[None, :], 0), axis=1)
    return shift, segment, places - offset, member.astype(f32)


def rotary_tables(position):
    lane = lax.iota(jnp.int32, LANES)
    frequency = rope_base ** (-2.0 * (lane % (HD // 2)).astype(f32) / HD)
    angles = position.astype(f32)[:, None] * frequency[None, :]
    sine = jnp.sin(angles)
    return jnp.cos(angles), jnp.where((lane & (HD // 2)) == 0, -sine, sine)


def per_device(
    tokens, lengths, w_qkv, w_out, w_gate, w_up, w_down, gain_one, shift_one, gain_two, shift_two
):
    count, width = tokens.shape
    me = lax.axis_index("fsdp")
    dp = lax.axis_index("dp")
    side = dp & 1
    order = Order()

    shift, segment, position, member = pack_layout(lengths[0], count)
    sizes = lengths[0].astype(f32)[:, None]
    cosine, sine = rotary_tables(position)
    tail = segment[LONG:]
    bias = jnp.where(tail[:, None] == tail[None, :], 0.0, -1e30).astype(f32)
    device = dp * lax.axis_size("fsdp") + me
    info = jnp.stack([me, (dp >> 1) & 1, shift, device, side, dp & 7]).astype(jnp.int32)

    far_qkv = swap(w_qkv, "fsdp", 2)
    core_qkv = swap(w_qkv, "fsdp", 1)
    vectors = jnp.stack([gain_one, shift_one, gain_two, shift_two])
    core_vectors = swap(vectors, "fsdp", 1)
    far_vectors = swap(vectors, "fsdp", 2)
    half_gate = choose(cut_rows(w_gate, 2), side)
    half_up = choose(cut_rows(w_up, 2), info[1])
    half_down = choose(cut_rows(w_down, 2), side)
    several = jnp.concatenate([w_out, w_gate, w_up], axis=1)
    gate_base, up_base = w_out.shape[1], w_out.shape[1] + w_gate.shape[1]
    rolled, tokens_turned = roll_tokens(info, tokens)
    order.done(rolled, cosine, sine, bias, member, half_gate, half_up, half_down, several)

    far_qkv, core_qkv = order.after(far_qkv, core_qkv)
    order.done(far_qkv)
    far_gate = swap(order.after(half_gate), "fsdp", 2)
    core_several = swap(order.after(several), "fsdp", 1)
    core_down = swap(order.after(w_down), "fsdp", 1)
    cross_qkv = order.after(swap(far_qkv, "fsdp", 1))
    order.done(cross_qkv)
    far_vectors, core_vectors = order.after(far_vectors, core_vectors)
    order.done(far_vectors)
    joined, full_qkv = project_qkv(
        info, order.after(rolled), cosine, sine, (whole_pieces(0), (w_qkv, core_qkv, far_qkv, cross_qkv))
    )
    order.done(joined)
    far_gate, core_several, core_down = order.after(far_gate, core_several, core_down)
    order.done(far_gate)
    far_out = swap(order.after(w_out), "fsdp", 2)
    far_up = swap(order.after(half_up), "fsdp", 2)
    more_gate = swap(far_gate, "dp", 1)
    cross_gate = order.after(swap(far_gate, "fsdp", 1))
    order.done(cross_gate)
    attended, logs = attend(info, order.after(joined), bias)
    order.done(attended)
    far_out = order.after(far_out)
    order.done(far_out)
    cross_out = swap(far_out, "fsdp", 1)
    cross_vectors = swap(order.after(far_vectors), "fsdp", 1)
    more_gate = order.after(more_gate)
    order.done(more_gate)
    more_cross_gate = swap(more_gate, "fsdp", 1)
    far_up, cross_out = order.after(far_up, cross_out)
    order.done(far_up)
    more_up = swap(far_up, "dp", 2)
    cross_up = swap(far_up, "fsdp", 1)
    normed_one, root_one, attended_turned, full_out = add_branch(
        info, order.after(attended), rolled, (whole_pieces(0), (w_out, core_several, far_out, cross_out))
    )
    order.done(normed_one)
    cross_vectors, more_cross_gate, cross_up = order.after(cross_vectors, more_cross_gate, cross_up)
    gain_a, shift_a, gain_b, shift_b = join_vectors([vectors, core_vectors, far_vectors, cross_vectors], me)
    far_down = swap(order.after(half_down), "fsdp", 2)
    gate_pieces = (w_gate, core_several, far_gate, more_gate, cross_gate, more_cross_gate)
    gate, hidden_low, hidden_turned, full_gate = project_gate(
        info, order.after(normed_one), gain_a, shift_a, (half_pieces(gate_base, lowest, not_lowest), gate_pieces)
    )
    order.done(gate)
    more_up = order.after(more_up)
    order.done(more_up)
    more_cross_up = swap(more_up, "fsdp", 1)
    far_down = order.after(far_down)
    order.done(far_down)
    more_down = swap(far_down, "dp", 1)
    cross_down = swap(far_down, "fsdp", 1)
    more_cross_up = order.after(more_cross_up)
    order.done(more_cross_up)
    up_pieces = (w_up, core_several, far_up, more_up, cross_up, more_cross_up)
    inner, up, full_up = project_up(
        info, order.after(hidden_low), gate, (half_pieces(up_base, second, not_second), up_pieces)
    )
    order.done(inner)
    more_down, cross_down = order.after(more_down, cross_down)
    order.done(more_down)
    down_pieces = (w_down, core_down, far_down, more_down, cross_down, swap(more_down, "fsdp", 1))
    output, normed_two, root_two, pooled, embedding, full_down = down_and_pool(
        info, order.after(inner), normed_one, gain_a, shift_a, gain_b, shift_b, member, sizes,
        (half_pieces(0, lowest, not_lowest), down_pieces),
    )
    order.done(embedding)
    everyone = gather_blocks(embedding).reshape(-1, width)

    quarter = width // 4
    tiles = gate.shape[1] // FEED_TILE
    pairs = width // LANES // 2
    had = types.SimpleNamespace()
    down, first, later, front, back = [Unit(order) for _ in range(5)]

    def run_loss():
        had.loss, had.grad_second, had.grad_feed, had.vectors_two = loss_and_norm(
            info, everyone, pooled, embedding, sizes, member, normed_two, root_two, gain_b
        )
        order.done(had.grad_feed)

    def run_down_theirs():
        down.pieces.extend(down_gradient(info, inner, order.after(had.grad_feed), True))
        order.done(*down.pieces)

    def run_down_own():
        down.pieces.extend(down_gradient(info, order.after(inner), had.grad_feed, False))
        order.done(*down.pieces[1:])

    def run_feed(unit, held, base, steps):
        *made, had.grad_hidden = feed_back(
            info, order.after(had.grad_feed), hidden_turned, gate, up, full_down, full_gate, full_up,
            base, steps, held,
        )
        unit.pieces.extend(made)
        order.done(had.grad_hidden)

    def run_norm():
        had.grad_first, had.branch, had.grad_attended, vectors_one = first_back(
            info, order.after(had.grad_hidden), normed_one, root_one, gain_a, full_out
        )
        order.done(had.grad_attended)
        vectors = jnp.concatenate([vectors_one[:2], had.vectors_two[:2]]).astype(bf16)
        vectors = vectors.reshape(4, 4, quarter).transpose(1, 0, 2)
        vectors = jnp.stack([choose(vectors, me ^ k) for k in range(4)])
        vectors = vectors.reshape(4, 2, width // 2)
        had.vectors = jnp.pad(vectors, ((0, 0), (0, SPARE_ROWS - 2), (0, 0)))

    def run_attend(base):
        grads = attend_back(
            info, order.after(joined), attended, had.grad_attended, logs, bias, cosine, sine, base, pairs
        )
        order.done(*grads)
        return grads

    def run_front():
        front.pieces.extend(
            weight_gradients(
                info, tokens_turned, attended_turned, order.after(*had.grads_front), "front",
                had.branch, had.vectors,
            )
        )
        order.done(*front.pieces)

    def run_back():
        back.pieces.extend(
            weight_gradients(info, tokens_turned, attended_turned, order.after(*had.grads_back), "back")
        )
        order.done(*back.pieces)

    def run_tokens():
        grads = had.grads_front + had.grads_back
        had.grad_tokens = tokens_gradient(info, order.after(had.grad_first), grads, full_qkv)
        order.done(had.grad_tokens)

    def run_unroll():
        had.output = unroll(info, order.after(output))
        order.done(had.output)

    def run_down():
        had.grad_down = finish_down(info, order.after(*down.drained()))
        order.done(had.grad_down)

    def run_gates():
        values = order.after(*first.drained(), *later.drained())
        had.gates = finish_gates(info, values[:2], values[2:])
        order.done(*had.gates)

    def run_feed_first():
        run_feed(first, had.grad_second, 0, tiles // 2)

    def run_feed_later():
        run_feed(later, had.grad_hidden, tiles // 2, tiles - tiles // 2)

    def run_attend_front():
        had.grads_front = run_attend(0)

    def run_attend_back():
        had.grads_back = run_attend(pairs)

    for run in (
        run_loss, run_down_theirs, down.step, run_down_own, down.step, run_feed_first, first.step,
        run_unroll, first.step, down.step, run_feed_later, later.step, down.step, run_norm,
        later.step, first.step, down.step, run_attend_front, down.step, first.step, run_front,
        down.step, first.step, front.step, later.step, front.step, run_attend_back, front.step,
        first.step, later.step, run_back, front.step, back.step, down.step, first.step, later.step,
        back.step, run_tokens, front.step, later.step, back.step, first.step, back.step, down.step,
        front.step, later.step, back.step, front.step, later.step, back.step, front.step, run_down,
        first.step, back.step, back.step, later.step, run_gates, front.step, back.step,
    ):
        run()

    grad_qkv, grad_out, sums = finish(info, front.drained(), back.drained())
    sums = sums[:2].reshape(4, quarter)
    return (
        had.loss[0, 0],
        had.output,
        had.grad_tokens,
        grad_qkv,
        grad_out,
        had.gates[0],
        had.gates[1],
        had.grad_down,
        sums[0],
        sums[1],
        sums[2],
        sums[3],
    )


def solution(mesh):
    placed = (
        P(("dp", "fsdp"), None),
        P(("dp", "fsdp"), None),
        P("fsdp", None),
        P("fsdp", None),
        P("fsdp", None),
        P("fsdp", None),
        P("fsdp", None),
        P("fsdp"),
        P("fsdp"),
        P("fsdp"),
        P("fsdp"),
    )
    return jax.shard_map(
        per_device,
        mesh=mesh,
        in_specs=placed,
        out_specs=(
            P(),
            P(("dp", "fsdp"), None),
            P(("dp", "fsdp"), None),
            P("fsdp", None),
            P("fsdp", None),
            P("fsdp", None),
            P("fsdp", None),
            P("fsdp", None),
            P("fsdp"),
            P("fsdp"),
            P("fsdp"),
            P("fsdp"),
        ),
        check_vma=False,
    )
```

```python
import functools
import types

import jax
import jax.numpy as jnp
from jax import lax
from jax.experimental import pallas as pl
from jax.experimental.pallas import tpu as pltpu
from jax.sharding import PartitionSpec as P

HD = 64
PAIRS = 4
LONG = 768
LANES = 128
FEED_TILE = 512
SPARE_ROWS = 64
exact_arithmetic = lax.Precision.HIGHEST
eps_norm = 1e-05
eps_embed = 1e-06
logit_divisor = 0.05
rope_base = 1000.0
log2_e = 1.4426950408889634
f32 = jnp.float32
bf16 = jnp.bfloat16
HBM = pl.BlockSpec(memory_space=pl.ANY)


def call(body, out_shapes, *, grid, in_specs, out_specs, scratch=(), vmem, name):
    return pl.pallas_call(
        body,
        out_shape=out_shapes,
        grid_spec=pltpu.PrefetchScalarGridSpec(
            num_scalar_prefetch=1,
            grid=grid,
            in_specs=in_specs,
            out_specs=out_specs,
            scratch_shapes=list(scratch),
        ),
        compiler_params=pltpu.CompilerParams(vmem_limit_bytes=vmem * 1024 * 1024),
        cost_estimate=pl.CostEstimate(flops=10**11, bytes_accessed=10**8, transcendentals=0),
        name=name,
    )


def whole(shape):
    return pl.BlockSpec(shape, lambda *_: (0,) * len(shape))


def shaped(shape, dtype):
    return pltpu.HBM(shape, dtype)


def close(shape, dtype):
    return jax.ShapeDtypeStruct(shape, dtype)


def pinned(*values):
    return [pltpu.with_memory_space_constraint(value, pltpu.HBM) for value in values]


def matmul(left, right, left_dim=1, right_dim=0, precision=None):
    return lax.dot_general(
        left,
        right,
        (((left_dim,), (right_dim,)), ((), ())),
        precision=precision,
        preferred_element_type=f32,
    )


def start_weight(info, parts, full, sem, columns, each=False):
    for (other, cut, block, base), piece in parts:
        rows = piece.shape[0]
        start = (info[0] ^ other) * (rows * cut)
        if block is not None:
            start = start + block(info) * rows
        target = full.at[pl.ds(pl.multiple_of(start, 16), rows), columns]
        source = piece.at[:, pl.ds(base + columns.start, columns.size)]
        pltpu.make_async_copy(source, target, sem.at[other] if each else sem).start()


def wait_weight(full, sem, columns):
    pltpu.make_async_copy(full.at[:, columns], full.at[:, columns], sem).wait()


def turn_rows(info, turned, target):
    count = turned.shape[0] // 4
    for k in range(4):
        start = pl.multiple_of((info[0] ^ k) * count, 32)
        target[k] = turned[pl.ds(start, count), :]


def sigmoid(value):
    return 0.5 * jnp.tanh(0.5 * value) + 0.5


def roll_body(info, tokens, rolled, turned, scratch):
    count, width = tokens.shape
    shift = lax.rem(count - info[2], count)
    for first in range(0, width, LANES):
        lanes = pl.ds(first, LANES)
        moved = pltpu.roll(tokens[:, lanes].astype(f32), shift, 0).astype(bf16)
        rolled[:, lanes] = moved
        scratch[pl.ds(first, LANES), :] = moved.T
    turn_rows(info, scratch, turned)


def roll_tokens(info, tokens):
    count, width = tokens.shape
    return call(
        roll_body,
        (close(tokens.shape, bf16), shaped((4, width // 4, count), bf16)),
        grid=(1,),
        in_specs=[whole(tokens.shape)],
        out_specs=(whole(tokens.shape), whole((4, width // 4, count))),
        scratch=[pltpu.VMEM((width, count), bf16)],
        vmem=12,
        name="roll_tokens",
    )(info, tokens)


def unroll_body(info, value, moved):
    count = value.shape[0]
    for first in range(0, value.shape[1], LANES):
        lanes = pl.ds(first, LANES)
        moved[:, lanes] = pltpu.roll(value[:, lanes].astype(f32), info[2], 0).astype(moved.dtype)


def unroll(info, value):
    count, width = value.shape
    tile = 256
    spec = pl.BlockSpec((count, tile), lambda i, *_: (0, i))
    return call(
        unroll_body,
        shaped(value.shape, value.dtype),
        grid=(width // tile,),
        in_specs=[spec],
        out_specs=spec,
        vmem=8,
        name="unroll",
    )(info, value)


def rope_lanes(value, cosine, signed_sine):
    lane = lax.broadcasted_iota(jnp.int32, (value.shape[0], LANES), 1)
    first_half = (lane & 32) == 0
    out = []
    for start in range(0, value.shape[1], LANES):
        piece = value[:, start : start + LANES]
        partner = jnp.where(first_half, pltpu.roll(piece, LANES - 32, 1), pltpu.roll(piece, 32, 1))
        out.append(piece * cosine + partner * signed_sine)
    return out[0] if len(out) == 1 else jnp.concatenate(out, axis=1)


def qkv_body(layout, info, rolled, cosine, signed_sine, *rest):
    parts = list(zip(layout, rest))
    joined, kept, full, sems, keep_sem = rest[len(layout) :]
    step = pl.program_id(0)
    steps = pl.num_programs(0)
    tile = joined.shape[1]

    @pl.when(step == 0)
    def _():
        for j in range(full.shape[1] // tile):
            start_weight(info, parts, full, sems.at[j], pl.ds(j * tile, tile))

    columns = pl.ds(pl.multiple_of(step * tile, tile), tile)
    wait_weight(full, sems.at[step], columns)
    pltpu.make_async_copy(full.at[:, columns], kept.at[:, columns], keep_sem.at[step]).start()
    chunk = 512

    @pl.when(step < 2 * steps // 3)
    def _():
        for first in range(0, joined.shape[0], chunk):
            rows = pl.ds(first, chunk)
            product = matmul(rolled[rows, :], full[:, columns])
            turned = rope_lanes(product, cosine[rows, :], signed_sine[rows, :])
            joined[rows, :] = turned.astype(bf16)

    @pl.when(step >= 2 * steps // 3)
    def _():
        for first in range(0, joined.shape[0], chunk):
            rows = pl.ds(first, chunk)
            joined[rows, :] = matmul(rolled[rows, :], full[:, columns]).astype(bf16)

    @pl.when(step == steps - 1)
    def _():
        for j in range(full.shape[1] // tile):
            piece = pl.ds(j * tile, tile)
            pltpu.make_async_copy(full.at[:, piece], kept.at[:, piece], keep_sem.at[j]).wait()


def project_qkv(info, rolled, cosine, signed_sine, weight):
    layout, parts = weight
    count, width = rolled.shape
    columns = parts[0].shape[1]
    tile = width
    return call(
        functools.partial(qkv_body, layout),
        (shaped((count, columns), bf16), shaped((width, columns), bf16)),
        grid=(columns // tile,),
        in_specs=[whole(rolled.shape), whole(cosine.shape), whole(cosine.shape)]
        + [HBM] * len(parts),
        out_specs=(pl.BlockSpec((count, tile), lambda i, *_: (0, i)), HBM),
        scratch=[
            pltpu.VMEM((width, columns), bf16),
            pltpu.SemaphoreType.DMA((columns // tile,)),
            pltpu.SemaphoreType.DMA((columns // tile,)),
        ],
        vmem=22,
        name="project_qkv",
    )(info, rolled, cosine, signed_sine, *pinned(*parts))


def attend_body(info, query, key, value, bias, attended, logs):
    pair = pl.program_id(0)
    count = query.shape[0]
    scale = 0.125 * log2_e
    lane = lax.broadcasted_iota(jnp.int32, (1, LANES), 1)

    @pl.when(pair == 0)
    def _():
        logs[...] = jnp.zeros_like(logs)

    def rows_of(first, size, keys, offset):
        rows = pl.ds(first, size)
        ones = jnp.ones((keys.size, LANES), bf16)
        extended = jnp.concatenate([value[keys, :], ones], axis=1)
        picked = []
        kept_logs = logs[rows, :]
        for head in range(2):
            mine = (lane >= HD) if head else (lane < HD)
            masked = jnp.where(mine, query[rows, :], jnp.zeros((), bf16))
            scores = matmul(masked, key[keys, :], 1, 1) * scale
            if offset is not None:
                scores = scores + offset
            top = jnp.max(scores, axis=1, keepdims=True)
            terms = jnp.exp2(scores - top).astype(bf16)
            product = matmul(terms, extended)
            total = product[:, LANES:]
            picked.append(product[:, :LANES] / total)
            kept_logs = jnp.where(lane == 2 * pair + head, top + jnp.log2(total), kept_logs)
        attended[rows, :] = jnp.where(lane < HD, picked[0], picked[1]).astype(bf16)
        logs[rows, :] = kept_logs

    for first in range(0, LONG, 256):
        rows_of(first, 256, pl.ds(0, LONG), None)
    rest = count - LONG
    rows_of(LONG, rest, pl.ds(LONG, rest), bias[...])


def attend(info, joined, bias):
    count, columns = joined.shape
    width = columns // 3
    pairs = width // LANES
    specs = [pl.BlockSpec((count, LANES), lambda i, *_, n=n: (0, n * pairs + i)) for n in range(3)]
    return call(
        attend_body,
        (close((count, width), bf16), shaped((count, LANES), f32)),
        grid=(pairs,),
        in_specs=specs + [whole(bias.shape)],
        out_specs=(pl.BlockSpec((count, LANES), lambda i, *_: (0, i)), whole((count, LANES))),
        vmem=16,
        name="attend",
    )(info, *pinned(joined, joined, joined), bias)


def norm_parts(value):
    centered = value - jnp.mean(value, axis=1, keepdims=True)
    root = lax.rsqrt(jnp.mean(centered * centered, axis=1, keepdims=True) + eps_norm)
    return centered * root, root


def branch_body(layout, info, attended, rolled, *rest):
    parts = list(zip(layout, rest))
    normed, root, turned, kept, full, scratch, sem, keep_sem = rest[len(layout) :]
    step = pl.program_id(0)

    @pl.when(step == 0)
    def _():
        start_weight(info, parts, full, sem, pl.ds(0, full.shape[1]))
        wait_weight(full, sem, pl.ds(0, full.shape[1]))
        pltpu.make_async_copy(full, kept, keep_sem).start()

    first = rolled[...].astype(f32) + matmul(attended[...], full[...])
    value, inverse = norm_parts(first)
    normed[...] = value
    root[...] = jnp.broadcast_to(inverse, root.shape)
    scratch[...] = attended[...].T
    turn_rows(info, scratch, turned)

    @pl.when(step == pl.num_programs(0) - 1)
    def _():
        pltpu.make_async_copy(full, kept, keep_sem).wait()


def add_branch(info, attended, rolled, weight):
    layout, parts = weight
    count, width = attended.shape
    tile = 256
    rows = pl.BlockSpec((tile, width), lambda i, *_: (i, 0))
    return call(
        functools.partial(branch_body, layout),
        (
            shaped((count, width), f32),
            shaped((count, LANES), f32),
            shaped((4, width // 4, count), bf16),
            shaped((width, width), bf16),
        ),
        grid=(count // tile,),
        in_specs=[rows, rows] + [HBM] * len(parts),
        out_specs=(
            rows,
            pl.BlockSpec((tile, LANES), lambda i, *_: (i, 0)),
            pl.BlockSpec((4, width // 4, tile), lambda i, *_: (0, 0, i)),
            HBM,
        ),
        scratch=[
            pltpu.VMEM((width, width), bf16),
            pltpu.VMEM((width, tile), bf16),
            pltpu.SemaphoreType.DMA,
            pltpu.SemaphoreType.DMA,
        ],
        vmem=14,
        name="add_branch",
    )(info, *pinned(attended, rolled, *parts))


def gate_body(layout, info, normed, gain, shift, *rest):
    parts = list(zip(layout, rest))
    gate, hidden, turned, kept, full, low, scratch, sems, keep_sems = rest[len(layout) :]
    step = pl.program_id(0)
    tile = gate.shape[1]
    tiles = full.shape[1] // tile
    chunk = 512

    @pl.when(step == 0)
    def _():
        for j in range(tiles):
            start_weight(info, parts, full, sems.at[j], pl.ds(j * tile, tile))
        for first in range(0, low.shape[0], chunk):
            rows = pl.ds(first, chunk)
            value = (normed[rows, :] * gain[...] + shift[...]).astype(bf16)
            low[rows, :] = value
            scratch[:, rows] = value.T
        hidden[...] = low[...]
        turn_rows(info, scratch, turned)

    columns = pl.ds(pl.multiple_of(step * tile, tile), tile)
    wait_weight(full, sems.at[step], columns)
    pltpu.make_async_copy(full.at[:, columns], kept.at[:, columns], keep_sems.at[step]).start()
    for first in range(0, low.shape[0], chunk):
        rows = pl.ds(first, chunk)
        gate[rows, :] = matmul(low[rows, :], full[:, columns]).astype(bf16)

    @pl.when(step == tiles - 1)
    def _():
        for j in range(tiles):
            piece = pl.ds(j * tile, tile)
            pltpu.make_async_copy(full.at[:, piece], kept.at[:, piece], keep_sems.at[j]).wait()


def project_gate(info, normed, gain, shift, weight):
    layout, parts = weight
    count, width = normed.shape
    hidden = parts[0].shape[1]
    tile = 768
    columns = pl.BlockSpec((count, tile), lambda i, *_: (0, i))
    return call(
        functools.partial(gate_body, layout),
        (
            shaped((count, hidden), bf16),
            close((count, width), bf16),
            shaped((4, width // 4, count), bf16),
            shaped((width, hidden), bf16),
        ),
        grid=(hidden // tile,),
        in_specs=[whole(normed.shape), whole(gain.shape), whole(shift.shape)]
        + [HBM] * len(layout),
        out_specs=(columns, whole((count, width)), whole((4, width // 4, count)), HBM),
        scratch=[
            pltpu.VMEM((width, hidden), bf16),
            pltpu.VMEM((count, width), bf16),
            pltpu.VMEM((width, count), bf16),
            pltpu.SemaphoreType.DMA((hidden // tile,)),
            pltpu.SemaphoreType.DMA((hidden // tile,)),
        ],
        vmem=32,
        name="project_gate",
    )(info, *pinned(normed), gain, shift, *pinned(*parts))


def up_body(layout, info, low, gate, *rest):
    parts = list(zip(layout, rest))
    inner, up_out, kept, full, sems, keep_sems = rest[len(layout) :]
    step = pl.program_id(0)
    tile = inner.shape[1]
    tiles = full.shape[1] // tile
    chunk = 512

    @pl.when(step == 0)
    def _():
        for j in range(tiles):
            start_weight(info, parts, full, sems.at[j], pl.ds(j * tile, tile))

    columns = pl.ds(pl.multiple_of(step * tile, tile), tile)
    wait_weight(full, sems.at[step], columns)
    pltpu.make_async_copy(full.at[:, columns], kept.at[:, columns], keep_sems.at[step]).start()
    for first in range(0, low.shape[0], chunk):
        rows = pl.ds(first, chunk)
        up = matmul(low[rows, :], full[:, columns])
        up_out[rows, :] = up.astype(bf16)
        value = gate[rows, :].astype(f32)
        inner[rows, :] = (value * up * sigmoid(value)).astype(bf16)

    @pl.when(step == tiles - 1)
    def _():
        for j in range(tiles):
            piece = pl.ds(j * tile, tile)
            pltpu.make_async_copy(full.at[:, piece], kept.at[:, piece], keep_sems.at[j]).wait()


def project_up(info, low, gate, weight):
    layout, parts = weight
    count, width = low.shape
    hidden = parts[0].shape[1]
    tile = 768
    columns = pl.BlockSpec((count, tile), lambda i, *_: (0, i))
    return call(
        functools.partial(up_body, layout),
        (
            shaped((count, hidden), bf16),
            shaped((count, hidden), bf16),
            shaped((width, hidden), bf16),
        ),
        grid=(hidden // tile,),
        in_specs=[whole(low.shape), columns] + [HBM] * len(layout),
        out_specs=(columns, columns, HBM),
        scratch=[
            pltpu.VMEM((width, hidden), bf16),
            pltpu.SemaphoreType.DMA((hidden // tile,)),
            pltpu.SemaphoreType.DMA((hidden // tile,)),
        ],
        vmem=32,
        name="project_up",
    )(info, low, *pinned(gate, *parts))


def down_body(layout, info, inner, normed, gain_one, shift_one, gain, shift, member, sizes, *rest):
    parts = list(zip(layout, rest))
    output, normed_two, root, pooled, embedding, kept, full, feed, sems, keep_sem = rest[len(layout) :]
    step = pl.program_id(0)
    steps = pl.num_programs(0)
    tile = output.shape[0]
    quarter = full.shape[0] // 4

    @pl.when(step == 0)
    def _():
        start_weight(info, parts, full, sems, pl.ds(0, full.shape[1]), each=True)
        pooled[...] = jnp.zeros_like(pooled)
        for other in range(4):
            rows = pl.ds(pl.multiple_of((info[0] ^ other) * quarter, quarter), quarter)
            pltpu.make_async_copy(full.at[rows, :], full.at[rows, :], sems.at[other]).wait()
            product = matmul(inner[:, rows], full[rows, :])
            feed[...] = product if other == 0 else feed[...] + product
        pltpu.make_async_copy(full, kept, keep_sem).start()

    @pl.when(step > 0)
    def _():
        feed[...] = matmul(inner[...], full[...])

    hidden = normed[...] * gain_one[...] + shift_one[...]
    value, inverse = norm_parts(hidden + feed[...])
    normed_two[...] = value
    root[...] = jnp.broadcast_to(inverse, root.shape)
    result = value * gain[...] + shift[...]
    output[...] = result.astype(bf16)

    @pl.when(step < LONG // tile)
    def _():
        pooled[0:1, :] += jnp.sum(result, axis=0, keepdims=True)

    @pl.when(step == steps - 1)
    def _():
        longest = jnp.where(sizes[...] == LONG, pooled[0:1, :], 0.0)
        total = (longest + matmul(member[...], result, 0, 0, exact_arithmetic)) / sizes[...]
        pooled[...] = total
        square = jnp.sum(total * total, axis=1, keepdims=True)
        embedding[...] = total * lax.rsqrt(square + eps_embed)
        pltpu.make_async_copy(full, kept, keep_sem).wait()


def down_and_pool(info, inner, normed, gain_one, shift_one, gain, shift, member, sizes, weight):
    layout, parts = weight
    count, width = normed.shape
    hidden = inner.shape[1]
    seqs = member.shape[1]
    tile = 256
    rows = pl.BlockSpec((tile, width), lambda i, *_: (i, 0))
    vector = whole((1, width))
    return call(
        functools.partial(down_body, layout),
        (
            shaped((count, width), bf16),
            shaped((count, width), f32),
            shaped((count, LANES), f32),
            close((seqs, width), f32),
            close((seqs, width), f32),
            shaped((hidden, width), bf16),
        ),
        grid=(count // tile,),
        in_specs=[
            pl.BlockSpec((tile, hidden), lambda i, *_: (i, 0)),
            rows,
            vector,
            vector,
            vector,
            vector,
            pl.BlockSpec((tile, seqs), lambda i, *_: (LONG // tile, 0)),
            whole(sizes.shape),
        ]
        + [HBM] * len(parts),
        out_specs=(
            rows,
            rows,
            pl.BlockSpec((tile, LANES), lambda i, *_: (i, 0)),
            whole((seqs, width)),
            whole((seqs, width)),
            HBM,
        ),
        scratch=[
            pltpu.VMEM((hidden, width), bf16),
            pltpu.VMEM((tile, width), f32),
            pltpu.SemaphoreType.DMA((4,)),
            pltpu.SemaphoreType.DMA,
        ],
        vmem=24,
        name="down_and_pool",
    )(info, *pinned(inner, normed), gain_one, shift_one, gain, shift, member, sizes, *pinned(*parts))


def loss_body(info, everyone, pooled, embedding, sizes, member, normed, root, gain, *rest):
    loss, grad_second, grad_feed, vectors, pulled, upstreams = rest
    step = pl.program_id(0)
    seqs, width = embedding.shape
    pairs = seqs // 2

    @pl.when(step == 0)
    def _():
        devices = everyone.shape[0] // seqs
        count = devices * pairs
        blocks = everyone[...].reshape(devices, seqs, width)
        requests = blocks[:, :pairs].reshape(count, width)
        passages = blocks[:, pairs:].reshape(count, width)
        sims = matmul(requests, passages, 1, 1, exact_arithmetic) * (1.0 / logit_divisor)
        top = jnp.max(sims, axis=1, keepdims=True)
        terms = jnp.exp(sims - top)
        total = jnp.sum(terms, axis=1, keepdims=True)
        row = lax.broadcasted_iota(jnp.int32, sims.shape, 0)
        column = lax.broadcasted_iota(jnp.int32, sims.shape, 1)
        diagonal = jnp.sum(jnp.where(row == column, sims, 0.0), axis=1, keepdims=True)
        mean = jnp.sum(top + jnp.log(total) - diagonal, axis=0, keepdims=True) / count
        loss[...] = jnp.broadcast_to(mean, loss.shape)
        pulls = terms / total
        first = info[3] * pairs
        near = lax.broadcasted_iota(jnp.int32, (seqs, count), 0)
        place = lax.broadcasted_iota(jnp.int32, (seqs, count), 1)
        picked = jnp.where(place == first + near, 1.0, 0.0)
        my_rows = matmul(picked, pulls, 1, 0, exact_arithmetic)
        my_columns = matmul(picked, pulls, 1, 1, exact_arithmetic)
        to_requests = matmul(my_rows, passages, 1, 0, exact_arithmetic)
        to_passages = matmul(my_columns, requests, 1, 0, exact_arithmetic)
        own = embedding[...]
        swapped = jnp.concatenate([own[pairs:], own[:pairs]], axis=0)
        gathered = jnp.concatenate([to_requests[:pairs], to_passages[:pairs]], axis=0)
        grad_embed = (gathered - swapped) * (1.0 / (logit_divisor * count))
        means = pooled[...]
        inverse = lax.rsqrt(jnp.sum(means * means, axis=1, keepdims=True) + eps_embed)
        along = jnp.sum(means * grad_embed, axis=1, keepdims=True)
        pulled[...] = (inverse * grad_embed - inverse * inverse * inverse * means * along) / sizes[
            ...
        ]
        vectors[...] = jnp.zeros_like(vectors)

    @pl.when(step < LONG // normed.shape[0])
    def _():
        longest = jnp.sum(jnp.where(sizes[...] == LONG, pulled[...], 0.0), axis=0, keepdims=True)
        upstreams[...] = jnp.broadcast_to(longest, upstreams.shape)

    @pl.when(step >= LONG // normed.shape[0])
    def _():
        upstreams[...] = matmul(member[...], pulled[...], 1, 0, exact_arithmetic)

    upstream = upstreams[...]
    value = normed[...]
    vectors[0:1, :] += jnp.sum(upstream * value, axis=0, keepdims=True)
    vectors[1:2, :] += jnp.sum(upstream, axis=0, keepdims=True)
    result = norm_back(upstream, value, root[:, :1], gain[...])
    grad_second[...] = result
    grad_feed[...] = result.astype(bf16)


def norm_back(upstream, normed, root, gain):
    scaled = upstream * gain
    return root * (
        scaled
        - jnp.mean(scaled, axis=1, keepdims=True)
        - normed * jnp.mean(scaled * normed, axis=1, keepdims=True)
    )


def loss_and_norm(info, everyone, pooled, embedding, sizes, member, normed, root, gain):
    count, width = normed.shape
    seqs = member.shape[1]
    tile = 256
    rows = pl.BlockSpec((tile, width), lambda i, *_: (i, 0))
    return call(
        loss_body,
        (
            close((8, LANES), f32),
            shaped((count, width), f32),
            close((count, width), bf16),
            close((8, width), f32),
        ),
        grid=(count // tile,),
        in_specs=[
            whole(everyone.shape),
            whole(pooled.shape),
            whole(embedding.shape),
            whole(sizes.shape),
            pl.BlockSpec((tile, seqs), lambda i, *_: (i, 0)),
            rows,
            pl.BlockSpec((tile, LANES), lambda i, *_: (i, 0)),
            whole(gain.shape),
        ],
        out_specs=(whole((8, LANES)), rows, rows, whole((8, width))),
        scratch=[pltpu.VMEM((seqs, width), f32), pltpu.VMEM((tile, width), f32)],
        vmem=16 + everyone.shape[0] * width * 24 // 2**20,
        name="loss_and_norm",
    )(info, everyone, pooled, embedding, sizes, member, *pinned(normed, root), gain)


def outer_body(theirs, info, left, right, *outs):
    step = pl.program_id(0)
    product = matmul(left[...], right[...], 0, 0).astype(bf16)
    rows = product.shape[0] // 8
    for block in range(8):
        source = slice(block * rows, (block + 1) * rows)
        target = pl.ds(pl.multiple_of(relative_block(info, block) * rows, 16), rows)
        if theirs:
            outs[0][0, target, :] = product[source]
            continue
        for index, out in enumerate(outs):

            @pl.when(step == index)
            def _():
                out[target, :] = product[source]


def down_gradient(info, inner, grad_feed, theirs):
    count, hidden = inner.shape
    width = grad_feed.shape[1]
    rows = hidden // 4
    first, last = (3, 1) if theirs else (2, 0)

    def column(i, info):
        return (0, info[0] ^ jnp.where(i == 0, first, last))

    if theirs:
        outs = (shaped((2, rows, width), bf16),)
        specs = (pl.BlockSpec((1, rows, width), lambda i, *_: (i, 0, 0)),)
    else:
        outs = (shaped((rows, width), bf16),) * 2
        specs = (whole((rows, width)),) * 2
    return call(
        functools.partial(outer_body, theirs),
        outs,
        grid=(2,),
        in_specs=[pl.BlockSpec((count, rows), column), whole(grad_feed.shape)],
        out_specs=specs,
        vmem=20,
        name="down_theirs" if theirs else "down_own",
    )(info, *pinned(inner), grad_feed)


def piece_shapes(rows, columns):
    own = shaped((rows, columns), bf16)
    return shaped((2, rows, columns), bf16), own, own


def piece_specs(rows, tile):
    own = pl.BlockSpec((rows, tile), lambda i, *_: (0, i))
    return pl.BlockSpec((2, rows, tile), lambda i, *_: (0, 0, i)), own, own


def relative_block(info, block):
    place = block ^ info[5]
    return ((place & 1) << 2) | (place & 2) | (place >> 2)


def multiply_into(held, turned, grads, first):
    _, quarter, count = turned.shape
    grad = grads[0] if len(grads) == 1 else jnp.concatenate(grads, axis=1)
    products = matmul(turned[...].reshape(4 * quarter, count), grad).astype(bf16)
    width = held.shape[2]
    for index in range(len(grads)):
        rows = pl.ds((first + index) * quarter, quarter)
        for place in range(4):
            part = slice(place * quarter, (place + 1) * quarter)
            held[place, rows, :] = products[part, index * width : (index + 1) * width]


def write_pieces(info, held, theirs, far, near):
    rows = held.shape[1] // 8
    for block in range(8):
        source = slice(block * rows, (block + 1) * rows)
        target = pl.ds(pl.multiple_of(relative_block(info, block) * rows, 16), rows)
        near[target, :] = held[0, source, :]
        theirs[1, target, :] = held[1, source, :]
        far[target, :] = held[2, source, :]
        theirs[0, target, :] = held[3, source, :]


def feed_body(info, grad_feed, turned, gate_in, up_in, down, gate_full, up_full, held, *outs):
    *pieces, grad_hidden, products, turned_here, held_here, total, turned_sem, held_sem, out_sems = outs
    step = pl.program_id(0)
    last = step == pl.num_programs(0) - 1
    count = grad_feed.shape[0]
    chunk = 512
    gates, ups = [], []
    turned_copy = pltpu.make_async_copy(turned, turned_here, turned_sem)
    held_copy = pltpu.make_async_copy(held, held_here, held_sem)

    def out_copy(index):
        rows = pl.ds(index * chunk, chunk)
        return pltpu.make_async_copy(total.at[rows, :], grad_hidden.at[rows, :], out_sems.at[index])

    @pl.when(step == 0)
    def _():
        turned_copy.start()
        held_copy.start()
        total[...] = jnp.zeros_like(total)

    @pl.when(last)
    def _():
        held_copy.wait()
        total[...] += held_here[...]

    for index in range(count // chunk):
        rows = pl.ds(index * chunk, chunk)
        grad_inner = matmul(grad_feed[rows, :], down[...], 1, 1)
        gate = gate_in[rows, :].astype(f32)
        up = up_in[rows, :].astype(f32)
        share = sigmoid(gate)
        scaled = grad_inner * share
        grad_gate = (scaled * up * (1.0 + gate * (1.0 - share))).astype(bf16)
        grad_up = (scaled * gate).astype(bf16)
        gates.append(grad_gate)
        ups.append(grad_up)
        total[rows, :] += matmul(grad_gate, gate_full[...], 1, 1) + matmul(grad_up, up_full[...], 1, 1)

        @pl.when(last)
        def _():
            out_copy(index).start()

    @pl.when(step == 0)
    def _():
        turned_copy.wait()

    for which, grads in ((0, gates), (1, ups)):
        multiply_into(products, turned_here, [jnp.concatenate(grads, axis=0)], which)
    write_pieces(info, products, *pieces)

    @pl.when(last)
    def _():
        for index in range(count // chunk):
            out_copy(index).wait()


def feed_back(info, grad_feed, turned, gate, up, down, gate_full, up_full, base, steps, held):
    count = gate.shape[0]
    width = grad_feed.shape[1]
    quarter = width // 4
    tile = FEED_TILE
    columns = pl.BlockSpec((count, tile), lambda i, *_: (0, base + i))
    weights = pl.BlockSpec((width, tile), lambda i, *_: (0, base + i))
    return call(
        feed_body,
        piece_shapes(2 * quarter, steps * tile) + (shaped((count, width), f32),),
        grid=(steps,),
        in_specs=[
            whole(grad_feed.shape),
            HBM,
            columns,
            columns,
            pl.BlockSpec((tile, width), lambda i, *_: (base + i, 0)),
            weights,
            weights,
            HBM,
        ],
        out_specs=piece_specs(2 * quarter, tile) + (HBM,),
        scratch=[
            pltpu.VMEM((4, 2 * quarter, tile), bf16),
            pltpu.VMEM(turned.shape, bf16),
            pltpu.VMEM((count, width), f32),
            pltpu.VMEM((count, width), f32),
            pltpu.SemaphoreType.DMA,
            pltpu.SemaphoreType.DMA,
            pltpu.SemaphoreType.DMA((2,)),
        ],
        vmem=40,
        name=f"feed_back_{base}",
    )(info, grad_feed, *pinned(turned, gate, up, down, gate_full, up_full, held))


def first_body(info, grad_hidden, normed, root, gain, weight, *outs):
    grad_first, branch, grad_attended, vectors = outs

    @pl.when(pl.program_id(0) == 0)
    def _():
        vectors[...] = jnp.zeros_like(vectors)

    upstream = grad_hidden[...]
    value = normed[...]
    vectors[0:1, :] += jnp.sum(upstream * value, axis=0, keepdims=True)
    vectors[1:2, :] += jnp.sum(upstream, axis=0, keepdims=True)
    result = norm_back(upstream, value, root[:, :1], gain[...])
    grad_first[...] = result
    low = result.astype(bf16)
    branch[...] = low
    grad_attended[...] = matmul(low, weight[...], 1, 1).astype(bf16)


def first_back(info, grad_hidden, normed, root, gain, weight):
    count, width = normed.shape
    tile = 256
    rows = pl.BlockSpec((tile, width), lambda i, *_: (i, 0))
    return call(
        first_body,
        (
            shaped((count, width), f32),
            shaped((count, width), bf16),
            shaped((count, width), bf16),
            close((8, width), f32),
        ),
        grid=(count // tile,),
        in_specs=[
            rows,
            rows,
            pl.BlockSpec((tile, LANES), lambda i, *_: (i, 0)),
            whole(gain.shape),
            whole(weight.shape),
        ],
        out_specs=(rows, rows, rows, whole((8, width))),
        vmem=20,
        name="first_back",
    )(info, *pinned(grad_hidden, normed, root), gain, weight)


def attend_back_body(base, info, query, key, value, attended, upstream, logs, bias, cosine, sine, *rest):
    (grad_query, grad_key, grad_value, logs_row, sums) = rest
    pair = base + pl.program_id(0)
    count = query.shape[0]
    scale = 0.125 * log2_e
    lane = lax.broadcasted_iota(jnp.int32, (1, LANES), 1)

    @pl.when(pl.program_id(0) == 0)
    def _():
        logs_row[...] = logs[...].T

    both = upstream[...].astype(f32) * attended[...].astype(f32)
    row = lax.broadcasted_iota(jnp.int32, (8, LANES), 0)
    column = lax.broadcasted_iota(jnp.int32, (8, LANES), 1)
    chooser = jnp.where((column // HD) == row, 1.0, 0.0)
    sums[...] = matmul(chooser, both, 1, 1, exact_arithmetic)

    zero = jnp.zeros((), bf16)
    for first, size, offset in ((0, LONG, None), (LONG, count - LONG, bias)):
        rows = pl.ds(first, size)
        key_rows, query_rows, up_rows = key[rows, :], query[rows, :], upstream[rows, :]
        key_grad = value_grad = query_grad = None
        for head in range(2):
            mine = (lane >= HD) if head else (lane < HD)
            masked_query = jnp.where(mine, query_rows, zero)
            masked_up = jnp.where(mine, up_rows, zero)
            masked_key = jnp.where(mine, key_rows, zero)
            log_row = logs_row[pl.ds(2 * pair + head, 1), rows]
            sum_row = sums[head : head + 1, rows]
            key_pieces, value_pieces = [], []
            query_total = None
            for start in range(first, first + size, 256):
                keys = pl.ds(start, 256)
                scores = matmul(key[keys, :], masked_query, 1, 1) * scale
                if offset is not None:
                    scores = scores + offset[...]
                probs = jnp.exp2(scores - log_row)
                grad_probs = matmul(value[keys, :], masked_up, 1, 1)
                grad_scores = (probs * (grad_probs - sum_row)).astype(bf16)
                value_pieces.append(matmul(probs.astype(bf16), masked_up))
                key_pieces.append(matmul(grad_scores, masked_query))
                kept_key = masked_key[start - first : start - first + 256]
                piece = matmul(grad_scores, kept_key, 0, 0)
                query_total = piece if query_total is None else query_total + piece
            key_head = jnp.concatenate(key_pieces, axis=0)
            value_head = jnp.concatenate(value_pieces, axis=0)
            key_grad = key_head if key_grad is None else key_grad + key_head
            value_grad = value_head if value_grad is None else value_grad + value_head
            query_grad = query_total if query_grad is None else query_grad + query_total
        turn_cos, turn_sin = cosine[rows, :], sine[rows, :]
        for grad, target in ((query_grad, grad_query), (key_grad, grad_key)):
            low = (grad * 0.125).astype(bf16).astype(f32)
            target[rows, :] = rope_lanes(low, turn_cos, -turn_sin).astype(bf16)
        grad_value[rows, :] = value_grad.astype(bf16)


def attend_back(info, joined, attended, upstream, logs, bias, cosine, sine, base, pairs):
    count, columns = joined.shape
    every = columns // 3 // LANES
    specs = [
        pl.BlockSpec((count, LANES), lambda i, *_, n=n: (0, n * every + base + i)) for n in range(3)
    ]
    block = pl.BlockSpec((count, LANES), lambda i, *_: (0, base + i))
    return call(
        functools.partial(attend_back_body, base),
        (close((count, pairs * LANES), bf16),) * 3,
        grid=(pairs,),
        in_specs=specs
        + [block, block, whole(logs.shape), whole(bias.shape)]
        + [whole(cosine.shape)] * 2,
        out_specs=(pl.BlockSpec((count, LANES), lambda i, *_: (0, i)),) * 3,
        scratch=[pltpu.VMEM((LANES, count), f32), pltpu.VMEM((8, count), f32)],
        vmem=32,
        name=f"attend_back_{base}",
    )(info, *pinned(joined, joined, joined, attended, upstream), logs, bias, cosine, sine)


def turned_body(info, turned_a, turned_b, *rest):
    grads, pieces, held = rest[:-4], rest[-4:-1], rest[-1]
    used = len(grads) * turned_a.shape[1]
    spare = held.shape[1] - used
    if len(grads) > 3:
        extra = grads[-1]
        grads = grads[:-1]
        used = len(grads) * turned_a.shape[1]
        held[:, used:, :] = extra[...]
    else:
        held[:, used:, :] = jnp.zeros((4, spare, held.shape[2]), bf16)
    for turned, first, several in ((turned_a, 0, grads[:3]), (turned_b, 3, grads[3:])):
        if several:
            multiply_into(held, turned, [grad[...] for grad in several], first)
    write_pieces(info, held, *pieces)


def weight_gradients(info, turned_a, turned_b, grads, name, branch=None, extra=None):
    _, quarter, count = turned_a.shape
    width = grads[0].shape[1]
    tile = LANES
    specs = [pl.BlockSpec((count, tile), lambda i, *_: (0, i))] * len(grads)
    rows = len(grads) * quarter + SPARE_ROWS
    args = list(grads)
    if branch is not None:
        specs += [
            pl.BlockSpec((count, tile), lambda i, *_, n=n: (0, n * width // tile + i)) for n in range(2)
        ]
        specs.append(pl.BlockSpec((4, SPARE_ROWS, tile), lambda i, *_: (0, 0, i)))
        args += [branch, branch, extra]
        rows += 2 * quarter
    return call(
        turned_body,
        piece_shapes(rows, width),
        grid=(width // tile,),
        in_specs=[whole(turned_a.shape), whole(turned_b.shape)] + specs,
        out_specs=piece_specs(rows, tile),
        scratch=[pltpu.VMEM((4, rows, tile), bf16)],
        vmem=22,
        name=name,
    )(info, *pinned(turned_a, turned_b, *args))


def tokens_body(info, grad_first, weight, *rest):
    grads, out = rest[:-1], rest[-1]
    total = grad_first[...]
    width = grads[0].shape[1]
    for part in range(2):
        for index in range(3):
            first = (2 * index + part) * width
            grad = grads[3 * part + index]
            total = total + matmul(grad[...], weight[:, first : first + width], 1, 1)
    out[...] = pltpu.roll(total, info[2], 0)


def tokens_gradient(info, grad_first, grads, weight):
    count, width = grad_first.shape
    tile = 256
    block = pl.BlockSpec((count, tile), lambda i, *_: (0, i))
    return call(
        tokens_body,
        shaped((count, width), f32),
        grid=(width // tile,),
        in_specs=[block, pl.BlockSpec((tile, weight.shape[1]), lambda i, *_: (i, 0))]
        + [whole(grad.shape) for grad in grads],
        out_specs=block,
        vmem=26,
        name="tokens_gradient",
    )(info, grad_first, weight, *grads)


def settle(info, mine, other, held, target):
    half = mine.shape[0]
    held[:half, :] = mine[...].astype(f32)
    held[half:, :] = other[...].astype(f32)
    rows = half // 4
    for block in range(8):
        source = pl.ds(pl.multiple_of(relative_block(info, block) * rows, 8), rows)
        target[block * rows : (block + 1) * rows, :] = held[source, :]


def finish_body(info, front_a, front_b, back_a, back_b, grad_qkv, grad_out, vectors, *scratch):
    quarter, width = grad_out.shape
    half = width // 2
    front_held, front, back_held, back = scratch
    settle(info, front_a, front_b, front_held, front)
    settle(info, back_a, back_b, back_held, back)
    for index in range(3):
        rows = slice(index * quarter, (index + 1) * quarter)
        grad_qkv[:, index * width : index * width + half] = front[rows, :]
        grad_qkv[:, index * width + half : (index + 1) * width] = back[rows, :]
    grad_out[:, :half] = front[3 * quarter : 4 * quarter, :]
    grad_out[:, half:] = front[4 * quarter : 5 * quarter, :]
    vectors[...] = front[5 * quarter : 5 * quarter + 8, :]


def finish(info, front, back):
    half = front[0].shape[1]
    rows, back_rows = 2 * front[0].shape[0], 2 * back[0].shape[0]
    quarter = (rows - SPARE_ROWS) // 5
    shapes = ((quarter, 6 * half), (quarter, 2 * half), (8, half))
    return call(
        finish_body,
        tuple(close(shape, f32) for shape in shapes),
        grid=(1,),
        in_specs=[whole(value.shape) for value in (*front, *back)],
        out_specs=tuple(whole(shape) for shape in shapes),
        scratch=[pltpu.VMEM((count, half), f32) for count in (rows, rows, back_rows, back_rows)],
        vmem=20,
        name="finish",
    )(info, *front, *back)


def gates_body(info, first_a, first_b, later_a, later_b, grad_gate, grad_up, held, target):
    quarter = grad_gate.shape[0]
    start = 0
    for mine, other in ((first_a, first_b), (later_a, later_b)):
        settle(info, mine, other, held, target)
        columns = slice(start, start + mine.shape[1])
        grad_gate[:, columns] = target[:quarter, :]
        grad_up[:, columns] = target[quarter:, :]
        start += mine.shape[1]


def finish_gates(info, first, later):
    half, columns = first[0].shape
    shape = (half, 2 * columns)
    return call(
        gates_body,
        (shaped(shape, f32),) * 2,
        grid=(1,),
        in_specs=[whole(first[0].shape)] * 4,
        out_specs=(whole(shape),) * 2,
        scratch=[pltpu.VMEM((2 * half, columns), f32)] * 2,
        vmem=28,
        name="finish_gates",
    )(info, *pinned(*first, *later))


def settle_down_body(info, mine, other, grad_down, held):
    settle(info, mine, other, held, grad_down)


def finish_down(info, down):
    half, columns = down[0].shape
    shape = (2 * half, columns)
    return call(
        settle_down_body,
        shaped(shape, f32),
        grid=(1,),
        in_specs=[whole(down[0].shape)] * 2,
        out_specs=whole(shape),
        scratch=[pltpu.VMEM(shape, f32)],
        vmem=16,
        name="finish_down",
    )(info, *pinned(*down))


def swap(value, axis, bit):
    size = lax.axis_size(axis)
    return lax.ppermute(value, axis, [(i, i ^ bit) for i in range(size)])


def choose(value, index):
    return lax.dynamic_index_in_dim(value, index, 0, keepdims=False)


def low_sum(*terms):
    total = terms[0].astype(f32)
    for term in terms[1:]:
        total = total + term.astype(f32)
    return total.astype(bf16)


class Order:
    def __init__(self):
        self.last = ()

    def after(self, *values):
        if self.last:
            values = lax.optimization_barrier((*values, *self.last))[: len(values)]
        return values[0] if len(values) == 1 else values

    def done(self, *values):
        self.last = values


def cut_rows(shard, blocks):
    rows, columns = shard.shape
    return shard.reshape(blocks, rows // blocks, columns)


def lowest(info):
    return info[4]


def not_lowest(info):
    return 1 - info[4]


def second(info):
    return info[1]


def not_second(info):
    return 1 - info[1]


def whole_pieces(base):
    return ((0, 1, None, 0), (1, 1, None, base), (2, 1, None, 0), (3, 1, None, 0))


def half_pieces(base, here, there):
    far = tuple((place, 2, block, 0) for place in (2, 3) for block in (here, there))
    return ((0, 1, None, 0), (1, 1, None, base)) + far


def join_vectors(pieces, me):
    pieces = jnp.stack(pieces)
    full = jnp.concatenate([choose(pieces, me ^ q) for q in range(4)], axis=1)
    return [full[i : i + 1].astype(f32) for i in range(full.shape[0])]


def gather_blocks(block):
    dp_size, fsdp_size = lax.axis_size("dp"), lax.axis_size("fsdp")
    bits = dp_size.bit_length() - 1
    held = block[None]
    for bit in reversed(range(bits)):
        other = swap(held, "dp", 1 << bit)
        low = ((lax.axis_index("dp") >> bit) & 1) == 0
        held = jnp.where(low, jnp.stack([held, other]), jnp.stack([other, held]))
        held = held.reshape((-1,) + block.shape)
    held = held.reshape((2,) * bits + block.shape)
    held = held.transpose(tuple(range(bits))[::-1] + tuple(range(bits, bits + block.ndim)))
    held = held.reshape((dp_size,) + block.shape)
    held = lax.all_gather(held, "fsdp", axis=1)
    return held.reshape((dp_size * fsdp_size,) + block.shape)


def reduce_steps(order, pieces):
    bits = lax.axis_size("dp").bit_length() - 1
    from_core = swap(order.after(pieces[0]), "fsdp", 1)
    yield None
    far, near = pieces[1:]
    far, from_core = order.after(far, from_core)
    total = low_sum(far, from_core[0])
    order.done(total)
    from_far = swap(total, "fsdp", 2)
    yield None
    terms = order.after(near, from_core, from_far)
    terms = [terms[0], terms[1][1], terms[2]]
    rows = near.shape[0]
    for step in range(3):
        rows //= 2
        send = low_sum(*[term[rows : 2 * rows] for term in terms])
        order.done(send)
        other = swap(send, "dp", 1 << step)
        yield None
        terms = list(order.after(near, from_core, from_far, *terms[3:], other))
        terms[1] = terms[1][1]
    held = low_sum(*[term[:rows] for term in terms])
    for step in range(3, bits):
        order.done(held)
        other = swap(held, "dp", 1 << step)
        yield None
        held = low_sum(*order.after(held, other))
    for step in (2, 1, 0):
        order.done(held)
        other = swap(held, "dp", 1 << step)
        yield None
        held, other = order.after(held, other)
        if step:
            held = jnp.concatenate([held, other])
    order.done(held, other)
    yield held, other


class Unit:
    def __init__(self, order):
        self.pieces = []
        self.steps = reduce_steps(order, self.pieces)
        self.result = None

    def step(self):
        if self.result is None:
            self.result = next(self.steps)

    def drained(self):
        while self.result is None:
            self.step()
        return self.result


def pack_layout(lengths_row, count):
    ends = jnp.cumsum(lengths_row)
    starts = ends - lengths_row
    shift = jnp.sum(jnp.where(lengths_row == LONG, starts, 0))
    places = lax.rem(lax.iota(jnp.int32, count) + shift, count)
    segment = jnp.sum((places[:, None] >= ends[None, :]).astype(jnp.int32), axis=1)
    member = segment[:, None] == lax.iota(jnp.int32, lengths_row.shape[0])[None, :]
    offset = jnp.sum(jnp.where(member, starts[None, :], 0), axis=1)
    return shift, segment, places - offset, member.astype(f32)


def rotary_tables(position):
    lane = lax.iota(jnp.int32, LANES)
    frequency = rope_base ** (-2.0 * (lane % (HD // 2)).astype(f32) / HD)
    angles = position.astype(f32)[:, None] * frequency[None, :]
    sine = jnp.sin(angles)
    return jnp.cos(angles), jnp.where((lane & (HD // 2)) == 0, -sine, sine)


def per_device(
    tokens, lengths, w_qkv, w_out, w_gate, w_up, w_down, gain_one, shift_one, gain_two, shift_two
):
    count, width = tokens.shape
    me = lax.axis_index("fsdp")
    dp = lax.axis_index("dp")
    side = dp & 1
    order = Order()

    shift, segment, position, member = pack_layout(lengths[0], count)
    sizes = lengths[0].astype(f32)[:, None]
    cosine, sine = rotary_tables(position)
    tail = segment[LONG:]
    bias = jnp.where(tail[:, None] == tail[None, :], 0.0, -1e30).astype(f32)
    device = dp * lax.axis_size("fsdp") + me
    info = jnp.stack([me, (dp >> 1) & 1, shift, device, side, dp & 7]).astype(jnp.int32)

    far_qkv = swap(w_qkv, "fsdp", 2)
    core_qkv = swap(w_qkv, "fsdp", 1)
    vectors = jnp.stack([gain_one, shift_one, gain_two, shift_two])
    core_vectors = swap(vectors, "fsdp", 1)
    far_vectors = swap(vectors, "fsdp", 2)
    half_gate = choose(cut_rows(w_gate, 2), side)
    half_up = choose(cut_rows(w_up, 2), info[1])
    half_down = choose(cut_rows(w_down, 2), side)
    several = jnp.concatenate([w_out, w_gate, w_up], axis=1)
    gate_base, up_base = w_out.shape[1], w_out.shape[1] + w_gate.shape[1]
    rolled, tokens_turned = roll_tokens(info, tokens)
    order.done(rolled, cosine, sine, bias, member, half_gate, half_up, half_down, several)

    far_qkv, core_qkv = order.after(far_qkv, core_qkv)
    order.done(far_qkv)
    far_gate = swap(order.after(half_gate), "fsdp", 2)
    core_several = swap(order.after(several), "fsdp", 1)
    core_down = swap(order.after(w_down), "fsdp", 1)
    cross_qkv = order.after(swap(far_qkv, "fsdp", 1))
    order.done(cross_qkv)
    far_vectors, core_vectors = order.after(far_vectors, core_vectors)
    order.done(far_vectors)
    joined, full_qkv = project_qkv(
        info, order.after(rolled), cosine, sine, (whole_pieces(0), (w_qkv, core_qkv, far_qkv, cross_qkv))
    )
    order.done(joined)
    far_gate, core_several, core_down = order.after(far_gate, core_several, core_down)
    order.done(far_gate)
    far_out = swap(order.after(w_out), "fsdp", 2)
    far_up = swap(order.after(half_up), "fsdp", 2)
    more_gate = swap(far_gate, "dp", 1)
    cross_gate = order.after(swap(far_gate, "fsdp", 1))
    order.done(cross_gate)
    attended, logs = attend(info, order.after(joined), bias)
    order.done(attended)
    far_out = order.after(far_out)
    order.done(far_out)
    cross_out = swap(far_out, "fsdp", 1)
    cross_vectors = swap(order.after(far_vectors), "fsdp", 1)
    more_gate = order.after(more_gate)
    order.done(more_gate)
    more_cross_gate = swap(more_gate, "fsdp", 1)
    far_up, cross_out = order.after(far_up, cross_out)
    order.done(far_up)
    more_up = swap(far_up, "dp", 2)
    cross_up = swap(far_up, "fsdp", 1)
    normed_one, root_one, attended_turned, full_out = add_branch(
        info, order.after(attended), rolled, (whole_pieces(0), (w_out, core_several, far_out, cross_out))
    )
    order.done(normed_one)
    cross_vectors, more_cross_gate, cross_up = order.after(cross_vectors, more_cross_gate, cross_up)
    gain_a, shift_a, gain_b, shift_b = join_vectors([vectors, core_vectors, far_vectors, cross_vectors], me)
    far_down = swap(order.after(half_down), "fsdp", 2)
    gate_pieces = (w_gate, core_several, far_gate, more_gate, cross_gate, more_cross_gate)
    gate, hidden_low, hidden_turned, full_gate = project_gate(
        info, order.after(normed_one), gain_a, shift_a, (half_pieces(gate_base, lowest, not_lowest), gate_pieces)
    )
    order.done(gate)
    more_up = order.after(more_up)
    order.done(more_up)
    more_cross_up = swap(more_up, "fsdp", 1)
    far_down = order.after(far_down)
    order.done(far_down)
    more_down = swap(far_down, "dp", 1)
    cross_down = swap(far_down, "fsdp", 1)
    more_cross_up = order.after(more_cross_up)
    order.done(more_cross_up)
    up_pieces = (w_up, core_several, far_up, more_up, cross_up, more_cross_up)
    inner, up, full_up = project_up(
        info, order.after(hidden_low), gate, (half_pieces(up_base, second, not_second), up_pieces)
    )
    order.done(inner)
    more_down, cross_down = order.after(more_down, cross_down)
    order.done(more_down)
    down_pieces = (w_down, core_down, far_down, more_down, cross_down, swap(more_down, "fsdp", 1))
    output, normed_two, root_two, pooled, embedding, full_down = down_and_pool(
        info, order.after(inner), normed_one, gain_a, shift_a, gain_b, shift_b, member, sizes,
        (half_pieces(0, lowest, not_lowest), down_pieces),
    )
    order.done(embedding)
    everyone = gather_blocks(embedding).reshape(-1, width)

    quarter = width // 4
    tiles = gate.shape[1] // FEED_TILE
    pairs = width // LANES // 2
    had = types.SimpleNamespace()
    down, first, later, front, back = [Unit(order) for _ in range(5)]

    def run_loss():
        had.loss, had.grad_second, had.grad_feed, had.vectors_two = loss_and_norm(
            info, everyone, pooled, embedding, sizes, member, normed_two, root_two, gain_b
        )
        order.done(had.grad_feed)

    def run_down_theirs():
        down.pieces.extend(down_gradient(info, inner, order.after(had.grad_feed), True))
        order.done(*down.pieces)

    def run_down_own():
        down.pieces.extend(down_gradient(info, order.after(inner), had.grad_feed, False))
        order.done(*down.pieces[1:])

    def run_feed(unit, held, base, steps):
        *made, had.grad_hidden = feed_back(
            info, order.after(had.grad_feed), hidden_turned, gate, up, full_down, full_gate, full_up,
            base, steps, held,
        )
        unit.pieces.extend(made)
        order.done(had.grad_hidden)

    def run_norm():
        had.grad_first, had.branch, had.grad_attended, vectors_one = first_back(
            info, order.after(had.grad_hidden), normed_one, root_one, gain_a, full_out
        )
        order.done(had.grad_attended)
        vectors = jnp.concatenate([vectors_one[:2], had.vectors_two[:2]]).astype(bf16)
        vectors = vectors.reshape(4, 4, quarter).transpose(1, 0, 2)
        vectors = jnp.stack([choose(vectors, me ^ k) for k in range(4)])
        vectors = vectors.reshape(4, 2, width // 2)
        had.vectors = jnp.pad(vectors, ((0, 0), (0, SPARE_ROWS - 2), (0, 0)))

    def run_attend(base):
        grads = attend_back(
            info, order.after(joined), attended, had.grad_attended, logs, bias, cosine, sine, base, pairs
        )
        order.done(*grads)
        return grads

    def run_front():
        front.pieces.extend(
            weight_gradients(
                info, tokens_turned, attended_turned, order.after(*had.grads_front), "front",
                had.branch, had.vectors,
            )
        )
        order.done(*front.pieces)

    def run_back():
        back.pieces.extend(
            weight_gradients(info, tokens_turned, attended_turned, order.after(*had.grads_back), "back")
        )
        order.done(*back.pieces)

    def run_tokens():
        grads = had.grads_front + had.grads_back
        had.grad_tokens = tokens_gradient(info, order.after(had.grad_first), grads, full_qkv)
        order.done(had.grad_tokens)

    def run_unroll():
        had.output = unroll(info, order.after(output))
        order.done(had.output)

    def run_down():
        had.grad_down = finish_down(info, order.after(*down.drained()))
        order.done(had.grad_down)

    def run_gates():
        values = order.after(*first.drained(), *later.drained())
        had.gates = finish_gates(info, values[:2], values[2:])
        order.done(*had.gates)

    def run_feed_first():
        run_feed(first, had.grad_second, 0, tiles // 2)

    def run_feed_later():
        run_feed(later, had.grad_hidden, tiles // 2, tiles - tiles // 2)

    def run_attend_front():
        had.grads_front = run_attend(0)

    def run_attend_back():
        had.grads_back = run_attend(pairs)

    for run in (
        run_loss, run_down_theirs, down.step, run_down_own, down.step, run_feed_first, first.step,
        run_unroll, first.step, down.step, run_feed_later, later.step, down.step, run_norm,
        later.step, first.step, down.step, run_attend_front, down.step, first.step, run_front,
        down.step, first.step, front.step, later.step, front.step, run_attend_back, front.step,
        first.step, later.step, run_back, front.step, back.step, down.step, first.step, later.step,
        back.step, run_tokens, front.step, later.step, back.step, first.step, back.step, down.step,
        front.step, later.step, back.step, front.step, later.step, back.step, front.step, run_down,
        first.step, back.step, back.step, later.step, run_gates, front.step, back.step,
    ):
        run()

    grad_qkv, grad_out, sums = finish(info, front.drained(), back.drained())
    sums = sums[:2].reshape(4, quarter)
    return (
        had.loss[0, 0],
        had.output,
        had.grad_tokens,
        grad_qkv,
        grad_out,
        had.gates[0],
        had.gates[1],
        had.grad_down,
        sums[0],
        sums[1],
        sums[2],
        sums[3],
    )


def solution(mesh):
    placed = (
        P(("dp", "fsdp"), None),
        P(("dp", "fsdp"), None),
        P("fsdp", None),
        P("fsdp", None),
        P("fsdp", None),
        P("fsdp", None),
        P("fsdp", None),
        P("fsdp"),
        P("fsdp"),
        P("fsdp"),
        P("fsdp"),
    )
    return jax.shard_map(
        per_device,
        mesh=mesh,
        in_specs=placed,
        out_specs=(
            P(),
            P(("dp", "fsdp"), None),
            P(("dp", "fsdp"), None),
            P("fsdp", None),
            P("fsdp", None),
            P("fsdp", None),
            P("fsdp", None),
            P("fsdp", None),
            P("fsdp"),
            P("fsdp"),
            P("fsdp"),
            P("fsdp"),
        ),
        check_vma=False,
    )
```
